32 devices in a mesh: dp: 1, tm: 32 (over z, y, x, core).
Axes of the slice: x: 2, y: 2, z: 4, core: 2. Of those that a mesh axis runs over, the one named last changes fastest.
Arguments:
- features: bfloat16 [1, 4096, 1536], P('dp', 'tm'), may hold values from -8 to 8
- start_noise: bfloat16 [1, 4096, 1536], P('dp', 'tm'), may hold values from -1 to 1
- cotangent: bfloat16 [1, 4096, 1536], P('dp', 'tm'), may hold values from -0.09375 to 0.09375
- in_weight: bfloat16 [3072, 1536], P('tm'), may hold values from -0.15625 to 0.15625
- kernel: float32 [31, 1536], replicated, may hold values from -1 to 1
- bn_gain: float32 [1536], replicated, may hold values from 0.25 to 1.75
- bn_shift: float32 [1536], replicated, may hold values from -1 to 1
- ends: int32 [1], replicated, may hold values from 2048 to 4096
Outputs:
- perturbation: float32 [1, 4096, 1536], P('dp', 'tm')
- grad_kernel: float32 [31, 1536], P(None, 'tm')
- grad_norm: float32 [2, 1536], P(None, 'tm')
The draws below stay inside these ranges and needn't reach their ends.
Inputs may be any that keep to these rules, and one draw needn't show every extreme that they name: `ends`: frames at or after an utterance's end are padding.
All inputs are finite; a program needn't handle non-finite values.
Results may differ from the reference program's by a relative error of at most 0.0059.
Values may be sent and summed in bfloat16 or wider, within the bound.
No kernel may reach another device: no remote copies, remote signals or barrier semaphores. Data moves between devices by JAX's collectives and lax.ppermute only.
A program may use at most 128 MiB of HBM per device.

```python
import jax
import jax.numpy as jnp
from jax import lax

D = 1536
KSIZE = 31
ASCENT = 2
SEQS = 1
FRAMES = 4096


def draw_features(key, part):
    noise_key = jax.random.fold_in(key, 11)
    shared_key = jax.random.fold_in(key, 12)
    noise = jax.random.normal(noise_key, (SEQS, FRAMES, D), jnp.float32)
    shared = jax.random.normal(shared_key, (SEQS, 1, D), jnp.float32)
    ramp = jnp.arange(SEQS, dtype=jnp.float32) / max(SEQS - 1, 1)
    strength = 0.6 * (1.0 + 2.0 * ramp)
    return jnp.clip(noise + strength[:, None, None] * shared, -8.0, 8.0).astype(jnp.bfloat16)


def shard_levels(own_key, shape, split, low, top_value):
    factor_of, own = 1.0, jax.random.fold_in(own_key, 6)
    for axis_at, parts in split:
        steps = jnp.exp(jax.random.uniform(jax.random.fold_in(own, axis_at), (parts,), jnp.float32, low / len(split), top_value / len(split)))
        factor_of = factor_of * jnp.repeat(steps, shape[axis_at] // parts).reshape([-1 if axis == axis_at else 1 for axis in range(len(shape))])
    return factor_of


def normal_values(key, dims, width, most, cuts=(), kind=jnp.bfloat16):
    factor_of = shard_levels(key, dims, cuts, -0.22, 0.18) if cuts else 1.0
    drawn = jax.random.normal(key, dims, jnp.float32) * width * factor_of
    return jnp.minimum(jnp.maximum(drawn, -most), most).astype(kind)


def setup_inputs(seed: int = 0) -> dict:
    splits = jax.random.split(jax.random.key(seed), 9)
    features = draw_features(jax.random.fold_in(splits[8], 71), 0)
    start_noise = jnp.clip(jax.random.uniform(splits[1], (SEQS, FRAMES, D), jnp.float32, -1.0, 1.0) * shard_levels(splits[1], (SEQS, FRAMES, D), ((1, 32),), -0.4, 0.0), -1.0, 1.0).astype(jnp.bfloat16)
    cotangent = normal_values(splits[2], (SEQS, FRAMES, D), (1.0 / (SEQS * FRAMES) ** 0.5), 0.09375, ((1, 32),))
    in_weight = normal_values(splits[3], (2 * D, D), D ** -0.5, 0.15625, ((0, 32),))
    kernel = normal_values(splits[4], (KSIZE, D), KSIZE ** -0.5, 1.0, (), jnp.float32)
    bn_gain = jnp.clip(1.0 + 0.15 * jax.random.normal(splits[5], (D,), jnp.float32), 0.25, 1.75)
    bn_shift = jnp.clip(jax.random.uniform(splits[6], (D,), jnp.float32, -1.0, 1.0), -1.0, 1.0)
    ends = jax.random.randint(splits[7], (SEQS,), FRAMES // 2, FRAMES + 1).astype(jnp.int32)
    return {"features": features, "start_noise": start_noise, "cotangent": cotangent, "in_weight": in_weight, "kernel": kernel, "bn_gain": bn_gain, "bn_shift": bn_shift, "ends": ends}


noise_scale = 0.5
ascent_rate = 0.5
layer_epsilon = 1e-05
batch_epsilon = 1e-05
ascent_epsilon = 1e-06

def normalize(summed):
    centre = summed - lax.optimization_barrier(jnp.mean(summed, axis=-1, keepdims=True))
    inverse = lax.rsqrt(lax.optimization_barrier(jnp.mean(centre * centre, axis=-1, keepdims=True)) + layer_epsilon)
    return (centre * inverse, inverse)

def conv_forward(padded, kernel, out_length):
    result = jnp.zeros((out_length, padded.shape[1]), jnp.float32)
    for offset in range(kernel.shape[0]):
        result = result + kernel[offset] * padded[offset:offset + out_length].astype(jnp.float32)
    return result

def conv_input_grad(padded, kernel, out_length):
    tap_span = kernel.shape[0] - 1
    result = jnp.zeros((out_length, padded.shape[1]), jnp.float32)
    for offset in range(kernel.shape[0]):
        start_row = tap_span - offset
        result = result + kernel[offset] * padded[start_row:start_row + out_length].astype(jnp.float32)
    return result

def conv_kernel_grad(grad_bf, padded, out_length):
    grad_float = grad_bf.astype(jnp.float32)
    rows_list = []
    for offset in range(padded.shape[0] - out_length + 1):
        rows_list.append(lax.optimization_barrier(jnp.sum(grad_float * padded[offset:offset + out_length].astype(jnp.float32), axis=0)))
    return jnp.stack(rows_list)

def reference(features, start_noise, cotangent, in_weight, kernel, bn_gain, bn_shift, ends):
    half_span = (KSIZE - 1) // 2
    model_width = in_weight.shape[1]
    frame_ids = jnp.arange(FRAMES, dtype=jnp.int32)
    live_frames = (frame_ids[None, :] < ends[:, None]).astype(jnp.float32)
    live_count = jnp.sum(ends).astype(jnp.float32)
    lengths = ends.astype(jnp.float32)
    inputs = features.astype(jnp.float32)
    perturbation = noise_scale * start_noise.astype(jnp.float32) * live_frames[:, :, None]
    grad_kernel = jnp.zeros((KSIZE, model_width), jnp.float32)
    grad_gain = jnp.zeros((model_width,), jnp.float32)
    grad_shift = jnp.zeros((model_width,), jnp.float32)

    def project(summed):
        normed, inverse = normalize(summed)
        hidden = jnp.dot(normed.astype(jnp.bfloat16), in_weight.T, preferred_element_type=jnp.float32)
        return (normed, inverse, hidden)

    def forward_one(packed):
        summed, live_mask = packed
        normed, inverse, hidden = project(summed)
        glu = (hidden[:, :model_width] * jax.nn.sigmoid(hidden[:, model_width:]) * live_mask[:, None]).astype(jnp.bfloat16)
        padded = jnp.pad(glu, ((half_span, half_span), (0, 0)))
        return (glu, conv_forward(padded, kernel, FRAMES))

    def kernel_one(packed):
        grad_seq, glu = packed
        padded = jnp.pad(glu, ((half_span, half_span), (0, 0)))
        return conv_kernel_grad(grad_seq, padded, FRAMES)

    def backward_one(packed):
        summed, live_mask, grad_seq, utter_length = packed
        normed, inverse, hidden = project(summed)
        padded = jnp.pad(grad_seq, ((half_span, half_span), (0, 0)))
        grad_glu = (conv_input_grad(padded, kernel, FRAMES) * live_mask[:, None]).astype(jnp.bfloat16)
        grad_glu = lax.optimization_barrier(grad_glu).astype(jnp.float32)
        value_half = hidden[:, :model_width]
        gate_half = jax.nn.sigmoid(hidden[:, model_width:])
        grad_hidden = jnp.concatenate([grad_glu * gate_half, grad_glu * value_half * gate_half * (1.0 - gate_half)], axis=1).astype(jnp.bfloat16)
        grad_normed = jnp.dot(grad_hidden, in_weight, preferred_element_type=jnp.float32)
        grad_sum = inverse * (grad_normed - lax.optimization_barrier(jnp.mean(grad_normed, axis=-1, keepdims=True)) - normed * lax.optimization_barrier(jnp.mean(grad_normed * normed, axis=-1, keepdims=True)))
        direction = live_mask[:, None] * grad_sum
        square_total = jnp.sum(direction * direction)
        return direction * (ascent_rate * jnp.sqrt(utter_length * model_width) / (jnp.sqrt(square_total) + ascent_epsilon))
    for ascent_step in range(ASCENT):
        summed_all = inputs + perturbation
        glu_all, conv_all = lax.map(forward_one, (summed_all, live_frames))
        weights_live = live_frames[:, :, None]
        batch_mean = lax.optimization_barrier(jnp.sum(weights_live * conv_all, axis=(0, 1))) / live_count
        centred = conv_all - batch_mean
        variance = lax.optimization_barrier(jnp.sum(weights_live * centred * centred, axis=(0, 1))) / live_count
        inv_std = lax.rsqrt(variance + batch_epsilon)
        scaled = centred * inv_std
        pre_act = bn_gain * scaled + bn_shift
        pre_sigmoid = jax.nn.sigmoid(pre_act)
        upstream = weights_live * cotangent.astype(jnp.float32) / ASCENT
        grad_pre = upstream * pre_sigmoid * (1.0 + pre_act * (1.0 - pre_sigmoid))
        shift_sum = lax.optimization_barrier(jnp.sum(grad_pre, axis=(0, 1)))
        gain_sum = lax.optimization_barrier(jnp.sum(grad_pre * scaled, axis=(0, 1)))
        grad_shift = grad_shift + shift_sum
        grad_gain = grad_gain + gain_sum
        grad_conv = (weights_live * inv_std * bn_gain * (grad_pre - (shift_sum + scaled * gain_sum) / live_count)).astype(jnp.bfloat16)
        grad_kernel = grad_kernel + lax.optimization_barrier(jnp.sum(lax.map(kernel_one, (grad_conv, glu_all)), axis=0))
        if ascent_step + 1 < ASCENT:
            perturbation = perturbation + lax.map(backward_one, (summed_all, live_frames, grad_conv, lengths))
    return (perturbation, grad_kernel, jnp.stack([grad_gain, grad_shift]))
```

```python
import functools

import jax
import jax.numpy as jnp
from jax import lax
from jax.experimental import pallas as pl
from jax.experimental.pallas import tpu as pltpu
from jax.sharding import PartitionSpec as P

ASCENT = 2

noise_scale = 0.5
ascent_rate = 0.5
layer_epsilon = 1e-05
batch_epsilon = 1e-05
ascent_epsilon = 1e-06

HALO = 32
EDGE = 16
PAY = 128
F32 = jnp.float32
BF16 = jnp.bfloat16


def params(limit=56 * 1024 * 1024):
    return pltpu.CompilerParams(vmem_limit_bytes=limit)


def cost(flops, nbytes):
    return pl.CostEstimate(flops=int(flops), bytes_accessed=int(nbytes), transcendentals=0)


def normalize(summed):
    centre = summed - jnp.mean(summed, axis=-1, keepdims=True)
    inverse = lax.rsqrt(jnp.mean(centre * centre, axis=-1, keepdims=True) + layer_epsilon)
    return (centre * inverse, inverse)


def live_rows(first, rows, end):
    ids = first + lax.broadcasted_iota(jnp.int32, (rows, 1), 0)
    return jnp.where((ids >= 0) & (ids < end), 1.0, 0.0).astype(F32)


def forward_kernel(taps_n, scal, nb, wv, wg, taps, value, gate, glu, conv, stats, wide):
    start, end = scal[0], scal[1]
    rows, span = value.shape[0], nb.shape[0]
    half = (taps_n - 1) // 2
    contract = (((1,), (1,)), ((), ()))
    v = lax.dot_general(nb[...], wv[...], contract, preferred_element_type=F32)
    s = jax.nn.sigmoid(lax.dot_general(nb[...], wg[...], contract, preferred_element_type=F32))
    value[...] = v[HALO : HALO + rows]
    gate[...] = s[HALO : HALO + rows]
    gated = (v * s * live_rows(start - HALO, span, end)).astype(BF16)
    glu[...] = gated
    wide[...] = gated.astype(F32)
    count = conv.shape[0]
    shift = HALO - EDGE - half
    block = 32
    for lane in range(0, conv.shape[1], 128):
        lanes = slice(lane, lane + 128)
        for row in range(0, count, block):
            total = jnp.zeros((block, 128), F32)
            for tap in range(taps_n):
                at = row + shift + tap
                total = total + taps[tap : tap + 1, lanes] * wide[at : at + block, lanes]
            conv[row : row + block, lanes] = total
    live = live_rows(start, rows, end)
    own = conv[EDGE : EDGE + rows, :]
    mass = jnp.sum(live * own, axis=0, keepdims=True)
    centre = live * (own - mass / jnp.maximum(jnp.sum(live), 1.0))
    both = jnp.concatenate([mass, jnp.sum(centre * centre, axis=0, keepdims=True)], axis=0)
    for peer in range(stats.shape[0]):
        stats[peer] = both


def forward(scal, nb, weight, taps, rows, peers):
    span, width = nb.shape
    half_width = weight.shape[0] // 2
    chunk = 256 if half_width % 256 == 0 else 128
    steps = half_width // chunk
    col = lambda n: pl.BlockSpec((n, chunk), lambda i: (0, i))
    return pl.pallas_call(
        functools.partial(forward_kernel, taps.shape[0]),
        grid=(steps,),
        in_specs=[
            pl.BlockSpec(memory_space=pltpu.SMEM),
            pl.BlockSpec((span, width), lambda i: (0, 0)),
            pl.BlockSpec((chunk, width), lambda i: (i, 0)),
            pl.BlockSpec((chunk, width), lambda i: (i + steps, 0)),
            col(taps.shape[0]),
        ],
        out_specs=[
            col(rows),
            col(rows),
            col(span),
            col(rows + 2 * EDGE),
            pl.BlockSpec((peers, 2, chunk), lambda i: (0, 0, i)),
        ],
        out_shape=[
            jax.ShapeDtypeStruct((rows, half_width), F32),
            jax.ShapeDtypeStruct((rows, half_width), F32),
            jax.ShapeDtypeStruct((span, half_width), BF16),
            jax.ShapeDtypeStruct((rows + 2 * EDGE, half_width), F32),
            jax.ShapeDtypeStruct((peers, 2, half_width), F32),
        ],
        scratch_shapes=[pltpu.VMEM((span, chunk), F32)],
        compiler_params=params(),
        cost_estimate=cost(2 * span * width * 2 * half_width, 4 * half_width * width + 10 * span * half_width),
        name="project_glu_conv",
    )(scal, nb, weight, weight, taps)


def moments(counts, stats, live_count):
    mass = stats[0, 0:1, :]
    square = stats[0, 1:2, :]
    for peer in range(1, stats.shape[0]):
        mass = mass + stats[peer, 0:1, :]
        square = square + stats[peer, 1:2, :]
    mean = mass / live_count
    for peer in range(stats.shape[0]):
        off = stats[peer, 0:1, :] - counts[0, peer] * mean
        square = square + off * off * counts[1, peer]
    return mean, lax.rsqrt(square / live_count + batch_epsilon)


def swish_grads(scal, counts, stats, conv, cot, gain, shift):
    start, end = scal[0], scal[1]
    live_count = scal[3].astype(F32)
    mean, inv = moments(counts, stats, live_count)
    scaled = (conv[...] - mean) * inv
    pre = gain[...] * scaled + shift[...]
    sig = jax.nn.sigmoid(pre)
    live = live_rows(start - EDGE, conv.shape[0], end)
    upstream = live * cot[...].astype(F32) / ASCENT
    return scaled, upstream * sig * (1.0 + pre * (1.0 - sig)), live, mean, inv


def batch_kernel(scal, counts, stats, conv, cot, gain, shift, scaled_out, grad_out, inv_out, sums):
    scaled, grad, live, mean, inv = swish_grads(scal, counts, stats, conv, cot, gain, shift)
    scaled_out[...] = scaled
    grad_out[...] = grad
    inv_out[...] = inv
    rows = conv.shape[0] - 2 * EDGE
    own = grad[EDGE : EDGE + rows]
    both = jnp.concatenate(
        [
            jnp.sum(own, axis=0, keepdims=True),
            jnp.sum(own * scaled[EDGE : EDGE + rows], axis=0, keepdims=True),
        ],
        axis=0,
    )
    for peer in range(sums.shape[0]):
        sums[peer] = both


def batch(scal, counts, stats, conv, cot, gain, shift, peers):
    span, half_width = conv.shape
    chunk = 256 if half_width % 256 == 0 else 128
    col = lambda n: pl.BlockSpec((n, chunk), lambda i: (0, i))
    smem = pl.BlockSpec(memory_space=pltpu.SMEM)
    return pl.pallas_call(
        batch_kernel,
        grid=(half_width // chunk,),
        in_specs=[
            smem,
            smem,
            pl.BlockSpec((stats.shape[0], 2, chunk), lambda i: (0, 0, i)),
            col(span),
            col(span),
            col(1),
            col(1),
        ],
        out_specs=[col(span), col(span), col(1), pl.BlockSpec((peers, 2, chunk), lambda i: (0, 0, i))],
        out_shape=[
            jax.ShapeDtypeStruct((span, half_width), F32),
            jax.ShapeDtypeStruct((span, half_width), F32),
            jax.ShapeDtypeStruct((1, half_width), F32),
            jax.ShapeDtypeStruct((peers, 2, half_width), F32),
        ],
        compiler_params=params(),
        cost_estimate=cost(40 * span * half_width, 16 * span * half_width),
        name="batch_norm_swish",
    )(scal, counts, stats, conv, cot, gain, shift)


def backward_kernel(taps_n, scal, sums, scaled, grad, inv, gain, taps, value, gate, wv, wg, part, grad_conv, wide):
    start, end = scal[0], scal[1]
    rows, half = value.shape[0], (taps_n - 1) // 2
    live_count = scal[3].astype(F32)
    both = sums[0]
    for peer in range(1, sums.shape[0]):
        both = both + sums[peer]
    shift_sum, gain_sum = both[0:1], both[1:2]
    live = live_rows(start - EDGE, scaled.shape[0], end)
    through = live * (inv[...] * gain[...]) * (
        grad[...] - (shift_sum + scaled[...] * gain_sum) / live_count
    )
    rounded = through.astype(BF16)
    grad_conv[...] = rounded[EDGE : EDGE + rows]
    wide[...] = rounded.astype(F32)
    block = 32
    columns = []
    for lane in range(0, value.shape[1], 128):
        lanes = slice(lane, lane + 128)
        tiles = []
        for row in range(0, rows, block):
            total = jnp.zeros((block, 128), F32)
            for tap in range(taps_n):
                at = row + EDGE + half - tap
                total = total + taps[tap : tap + 1, lanes] * wide[at : at + block, lanes]
            tiles.append(total)
        columns.append(jnp.concatenate(tiles, axis=0))
    grad_glu = jnp.concatenate(columns, axis=1) * live_rows(start, rows, end)
    grad_glu = grad_glu.astype(BF16).astype(F32)
    sig = gate[...]
    to_value = (grad_glu * sig).astype(BF16)
    to_gate = (grad_glu * value[...] * sig * (1.0 - sig)).astype(BF16)
    product = jnp.dot(to_value, wv[...], preferred_element_type=F32) + jnp.dot(
        to_gate, wg[...], preferred_element_type=F32
    )

    @pl.when(pl.program_id(0) == 0)
    def _():
        part[...] = product

    @pl.when(pl.program_id(0) > 0)
    def _():
        part[...] += product


def backward(scal, sums, scaled, grad, inv, gain, taps, value, gate, weight):
    span, half_width = scaled.shape
    rows, width = value.shape[0], weight.shape[1]
    chunk = 256 if half_width % 256 == 0 else 128
    steps = half_width // chunk
    col = lambda n: pl.BlockSpec((n, chunk), lambda i: (0, i))
    return pl.pallas_call(
        functools.partial(backward_kernel, taps.shape[0]),
        grid=(steps,),
        in_specs=[
            pl.BlockSpec(memory_space=pltpu.SMEM),
            pl.BlockSpec((sums.shape[0], 2, chunk), lambda i: (0, 0, i)),
            col(span),
            col(span),
            col(1),
            col(1),
            col(taps.shape[0]),
            col(rows),
            col(rows),
            pl.BlockSpec((chunk, width), lambda i: (i, 0)),
            pl.BlockSpec((chunk, width), lambda i: (i + steps, 0)),
        ],
        out_specs=[pl.BlockSpec((rows, width), lambda i: (0, 0)), col(rows)],
        out_shape=[
            jax.ShapeDtypeStruct((rows, width), F32),
            jax.ShapeDtypeStruct((rows, half_width), BF16),
        ],
        scratch_shapes=[pltpu.VMEM((span, chunk), F32)],
        compiler_params=params(),
        cost_estimate=cost(2 * rows * width * 2 * half_width, 4 * half_width * width + 20 * span * half_width),
        name="grad_conv_project_back",
    )(scal, sums, scaled, grad, inv, gain, taps, value, gate, weight, weight)


def correlate(taps_n, left, wide, first):
    rows = left.shape[0]
    return jnp.concatenate(
        [
            jnp.sum(left * wide[first + tap : first + tap + rows], axis=0, keepdims=True)
            for tap in range(taps_n)
        ],
        axis=0,
    )


def tap_grad_kernel(taps_n, grad_conv, glu, out, wide):
    wide[...] = glu[...].astype(F32)
    first = HALO - (taps_n - 1) // 2
    out[...] = correlate(taps_n, grad_conv[...].astype(F32), wide, first)


def tap_grad(taps_n, grad_conv, glu):
    rows, half_width = grad_conv.shape
    span = glu.shape[0]
    col = lambda n: pl.BlockSpec((n, 128), lambda i: (0, i))
    return pl.pallas_call(
        functools.partial(tap_grad_kernel, taps_n),
        grid=(half_width // 128,),
        in_specs=[col(rows), col(span)],
        out_specs=col(taps_n),
        out_shape=jax.ShapeDtypeStruct((taps_n, half_width), F32),
        scratch_shapes=[pltpu.VMEM((span, 128), F32)],
        compiler_params=params(),
        cost_estimate=cost(2 * taps_n * rows * half_width, 4 * span * half_width),
        name="tap_grad",
    )(grad_conv, glu)


def raw_taps_kernel(taps_n, scal, conv, glu, stats, plain, crossed, wide):
    start, end = scal[0], scal[1]
    rows, span = conv.shape[0] - 2 * EDGE, glu.shape[0]
    wide[...] = glu[...].astype(F32)
    first = HALO - (taps_n - 1) // 2
    live = live_rows(start, rows, end)
    local = stats[0, 0:1, :] / jnp.maximum(jnp.sum(live), 1.0)
    crossed[...] = correlate(taps_n, live * (conv[EDGE : EDGE + rows, :] - local), wide, first)
    tap = lax.broadcasted_iota(jnp.int32, (taps_n, span), 0)
    at = lax.broadcasted_iota(jnp.int32, (taps_n, span), 1) - first - tap
    inside = (at >= 0) & (at < jnp.clip(end - start, 0, rows))
    plain[...] = jnp.dot(
        jnp.where(inside, 1.0, 0.0).astype(BF16), glu[...], preferred_element_type=F32
    )


def raw_taps(taps_n, scal, conv, glu, stats):
    rows, half_width = conv.shape
    span = glu.shape[0]
    col = lambda n: pl.BlockSpec((n, 128), lambda i: (0, i))
    return pl.pallas_call(
        functools.partial(raw_taps_kernel, taps_n),
        grid=(half_width // 128,),
        in_specs=[
            pl.BlockSpec(memory_space=pltpu.SMEM),
            col(rows),
            col(span),
            pl.BlockSpec((1, 2, 128), lambda i: (0, 0, i)),
        ],
        out_specs=[col(taps_n), col(taps_n)],
        out_shape=[jax.ShapeDtypeStruct((taps_n, half_width), F32)] * 2,
        scratch_shapes=[pltpu.VMEM((span, 128), F32)],
        compiler_params=params(),
        cost_estimate=cost(2 * taps_n * rows * half_width, 8 * span * half_width),
        name="raw_taps",
    )(scal, conv, glu, stats)


def last_kernel(taps_n, block, scal, counts, stats, conv, cot, gain, shift, glu, plain, crossed, local_stats, taps_before, sums_before, out, wide, pay):
    step = pl.program_id(0)
    scaled, grad, live, mean, inv = swish_grads(scal, counts, stats, conv, cot, gain, shift)
    rows = conv.shape[0] - 2 * EDGE
    wide[...] = glu[...].astype(F32)
    first = HALO - (taps_n - 1) // 2
    factor = inv * gain[...]
    own = grad[EDGE : EDGE + rows]
    direct = correlate(taps_n, own, wide, first)
    own_live = live[EDGE : EDGE + rows]
    local = local_stats[0, 0:1, :] / jnp.maximum(jnp.sum(own_live), 1.0)
    with_scaled = inv * (crossed[...] + (local - mean) * plain[...])
    both = sums_before[0]
    lanes = 128
    filler = jnp.zeros((PAY - 3 * taps_n - 5, lanes), F32)
    pay[step] = jnp.concatenate(
        [
            taps_before[...] + factor * direct,
            with_scaled,
            plain[...],
            jnp.sum(own, axis=0, keepdims=True),
            jnp.sum(own * scaled[EDGE : EDGE + rows], axis=0, keepdims=True),
            both,
            factor,
            filler,
        ],
        axis=0,
    )

    @pl.when(step == pl.num_programs(0) - 1)
    def _():
        core = scal[2]
        turned = jnp.concatenate([jnp.transpose(pay[s]) for s in range(pay.shape[0])], axis=0)
        for index in range(out.shape[0]):
            out[index, core] = turned[index * block : (index + 1) * block]
            out[index, 1 - core] = jnp.zeros((block, PAY), F32)


def last(taps_n, block, scal, counts, stats, conv, cot, gain, shift, glu, plain, crossed, local_stats, taps_before, sums_before):
    span, half_width = conv.shape
    chunk = 128
    steps = half_width // chunk
    col = lambda n: pl.BlockSpec((n, chunk), lambda i: (0, i))
    one = pl.BlockSpec((1, 2, chunk), lambda i: (0, 0, i))
    smem = pl.BlockSpec(memory_space=pltpu.SMEM)
    blocks = half_width // block
    return pl.pallas_call(
        functools.partial(last_kernel, taps_n, block),
        grid=(steps,),
        in_specs=[
            smem,
            smem,
            pl.BlockSpec((stats.shape[0], 2, chunk), lambda i: (0, 0, i)),
            col(span),
            col(span),
            col(1),
            col(1),
            col(glu.shape[0]),
            col(taps_n),
            col(taps_n),
            one,
            col(taps_n),
            one,
        ],
        out_specs=pl.BlockSpec((blocks, 2, block, PAY), lambda i: (0, 0, 0, 0)),
        out_shape=jax.ShapeDtypeStruct((blocks, 2, block, PAY), F32),
        scratch_shapes=[pltpu.VMEM((glu.shape[0], chunk), F32), pltpu.VMEM((steps, PAY, chunk), F32)],
        compiler_params=params(),
        cost_estimate=cost(100 * span * half_width, 10 * span * half_width),
        name="batch_norm_swish_taps",
    )(scal, counts, stats, conv, cot, gain, shift, glu, plain, crossed, local_stats, taps_before, sums_before)


def finish_kernel(taps_n, sources, scal, received, taps_out, norm_out):
    total = received[0]
    for index in range(1, received.shape[0]):
        total = total + received[index]
    total = jnp.transpose(total)
    at = 3 * taps_n
    shift_sum, gain_sum = total[at : at + 1], total[at + 1 : at + 2]
    factor = total[at + 4 : at + 5] / sources / scal[3].astype(F32)
    taps_out[...] = total[:taps_n] - factor * (
        gain_sum * total[taps_n : 2 * taps_n] + shift_sum * total[2 * taps_n : at]
    )
    norm_out[...] = jnp.concatenate(
        [gain_sum + total[at + 3 : at + 4], shift_sum + total[at + 2 : at + 3]], axis=0
    )


def finish(taps_n, sources, scal, received):
    width = received.shape[1]
    return pl.pallas_call(
        functools.partial(finish_kernel, taps_n, float(sources)),
        in_specs=[pl.BlockSpec(memory_space=pltpu.SMEM), pl.BlockSpec(memory_space=pltpu.VMEM)],
        out_shape=[
            jax.ShapeDtypeStruct((taps_n, width), F32),
            jax.ShapeDtypeStruct((2, width), F32),
        ],
        compiler_params=params(),
        name="finish",
    )(scal, received)


def direction_kernel(scal, mine, other, features, noise, out, squares):
    rows = mine.shape[0]
    first = scal[0] + scal[2] * rows
    block = 32
    total = jnp.zeros((1, 128), F32)
    for row in range(0, rows, block):
        at = slice(row, row + block)
        live = live_rows(first + row, block, scal[1])
        summed = features[at].astype(F32) + noise_scale * noise[at].astype(F32) * live
        normed, inverse = normalize(summed)
        grad = mine[at] + other[at]
        moved = (
            live
            * inverse
            * (
                grad
                - jnp.mean(grad, axis=-1, keepdims=True)
                - normed * jnp.mean(grad * normed, axis=-1, keepdims=True)
            )
        )
        out[at] = moved
        total = total + jnp.sum(moved * moved)
    for peer in range(squares.shape[0]):
        squares[peer] = total


def direction(scal, mine, other, features, noise, peers):
    rows, width = mine.shape
    vmem = pl.BlockSpec(memory_space=pltpu.VMEM)
    return pl.pallas_call(
        direction_kernel,
        in_specs=[pl.BlockSpec(memory_space=pltpu.SMEM)] + [vmem] * 4,
        out_shape=[
            jax.ShapeDtypeStruct((rows, width), F32),
            jax.ShapeDtypeStruct((peers, 1, 128), F32),
        ],
        compiler_params=params(),
        cost_estimate=cost(30 * rows * width, 16 * rows * width),
        name="direction",
    )(scal, mine, other, features, noise)


def ascend_kernel(scal, squares, features, noise, mine, partner, near, far, own_noise, perturbation, normed_out):
    start, end, core = scal[0], scal[1], scal[2]
    rows, width = mine.shape
    total = squares[0]
    for index in range(1, squares.shape[0]):
        total = total + squares[index]
    total = total[0:1, 0:1]
    length = jnp.full((1, 1), 1.0, F32) * end.astype(F32)
    rate = ascent_rate * jnp.sqrt(length * width) / (jnp.sqrt(total) + ascent_epsilon)
    block = 32
    is_first = core == 0

    def place(row, moved):
        at = slice(row, row + block)
        live = live_rows(start - HALO + row, block, end)
        summed = features[at].astype(F32) + (noise_scale * noise[at].astype(F32) * live + moved * rate)
        normed_out[at] = normalize(summed)[0].astype(BF16)

    place(0, jnp.where(is_first, far[...], near[...]))
    for row in range(0, rows, block):
        at = slice(row, row + block)
        place(HALO + row, jnp.where(is_first, mine[at], partner[at]))
        place(HALO + rows + row, jnp.where(is_first, partner[at], mine[at]))
        live = live_rows(start + core * rows + row, block, end)
        perturbation[at] = noise_scale * own_noise[at].astype(F32) * live + mine[at] * rate
    place(HALO + 2 * rows, jnp.where(is_first, near[...], far[...]))


def ascend(scal, squares, features, noise, mine, partner, near, far, own_noise):
    vmem = pl.BlockSpec(memory_space=pltpu.VMEM)
    return pl.pallas_call(
        ascend_kernel,
        in_specs=[pl.BlockSpec(memory_space=pltpu.SMEM)] + [vmem] * 8,
        out_shape=[
            jax.ShapeDtypeStruct(mine.shape, F32),
            jax.ShapeDtypeStruct(features.shape, BF16),
        ],
        compiler_params=params(),
        cost_estimate=cost(30 * features.size, 8 * features.size),
        name="ascend",
    )(scal, squares, features, noise, mine, partner, near, far, own_noise)


def on_device(on_dp, features, start_noise, cotangent, in_weight, kernel, bn_gain, bn_shift, ends):
    rows, width = features.shape[1:]
    taps_n = kernel.shape[0]
    shards = lax.axis_size("tm")
    chips = shards // 2
    index = lax.axis_index("tm")
    group = lax.axis_index("dp")
    chip, core = index // 2, index % 2
    chip_rows = 2 * rows
    block = in_weight.shape[0]
    half_width = width // 2
    end = lax.dynamic_index_in_dim(ends, group, 0, keepdims=False)
    scal = jnp.stack([chip * chip_rows, end, core, jnp.sum(ends)]).astype(jnp.int32)
    held = jnp.clip(
        ends[:, None] - chip_rows * jnp.arange(chips, dtype=jnp.int32)[None, :], 0, chip_rows
    ).reshape(-1).astype(F32)
    counts = jnp.stack([held, jnp.where(held > 0, 1.0 / jnp.maximum(held, 1.0), 0.0)])

    cores = [[2 * c + k for c in range(chips)] for k in range(2)]
    swap = [(i, i ^ 1) for i in range(shards)]
    near_pairs = [(2 * c, 2 * c - 2) for c in range(1, chips)] + [
        (2 * c + 1, 2 * c + 3) for c in range(chips - 1)
    ]
    far_pairs = [(2 * c, 2 * c - 1) for c in range(1, chips)] + [
        (2 * c + 1, 2 * c + 2) for c in range(chips - 1)
    ]

    def edges(array):
        return jnp.where(core == 0, array[..., :HALO, :], array[..., -HALO:, :])

    def across(array):
        edge = edges(array)
        return (
            lax.ppermute(array, "tm", swap),
            lax.ppermute(edge, "tm", near_pairs),
            lax.ppermute(edge, "tm", far_pairs),
        )

    def peers_of(array):
        array = lax.all_to_all(array, "tm", 0, 0, axis_index_groups=cores, tiled=True)
        if on_dp:
            array = lax.all_gather(array, "dp", axis=0, tiled=True)
        return array

    weight = lax.all_gather(in_weight, "tm", axis=0, axis_index_groups=cores, tiled=True)

    packed = jnp.concatenate([features, start_noise, cotangent], axis=0)
    partner, near, far = across(packed)
    first = core == 0
    whole = jnp.concatenate(
        [
            jnp.where(first, far, near),
            jnp.where(first, packed, partner),
            jnp.where(first, partner, packed),
            jnp.where(first, near, far),
        ],
        axis=1,
    )
    wide_features, wide_noise, wide_cot = whole[0], whole[1], whole[2]

    out_channel = jnp.arange(half_width, dtype=jnp.int32)
    source = (2 * (out_channel // block) + core) * block + out_channel % block
    chosen = (jnp.arange(width, dtype=jnp.int32)[:, None] == source[None, :]).astype(BF16)
    cot = jnp.dot(wide_cot[HALO - EDGE : -(HALO - EDGE)], chosen, preferred_element_type=F32).astype(BF16)

    def mine_of(array):
        parts = array.reshape(array.shape[0], width // (2 * block), 2, block)
        return lax.dynamic_index_in_dim(parts, core, 2, keepdims=False).reshape(-1, half_width)

    taps = mine_of(kernel)
    gain, shift = mine_of(bn_gain[None]), mine_of(bn_shift[None])

    frame_ids = chip * chip_rows - HALO + jnp.arange(whole.shape[1], dtype=jnp.int32)
    live = ((frame_ids >= 0) & (frame_ids < end)).astype(F32)
    summed = wide_features.astype(F32) + noise_scale * wide_noise.astype(F32) * live[:, None]
    normed_b = normalize(summed)[0].astype(BF16)

    value, gate, glu, conv, stats = forward(scal, normed_b, weight, taps, chip_rows, chips)
    scaled, grad, inv, sums_before = batch(
        scal, counts, peers_of(stats), conv, cot, gain, shift, chips
    )
    part, grad_conv = backward(
        scal, peers_of(sums_before), scaled, grad, inv, gain, taps, value, gate, weight
    )
    mine = lax.dynamic_slice_in_dim(part, core * rows, rows, 0)
    other = lax.dynamic_slice_in_dim(part, (1 - core) * rows, rows, 0)
    other = lax.ppermute(other, "tm", swap)
    moved, squares = direction(scal, mine, other, features[0], start_noise[0], shards)
    squares = lax.all_to_all(squares, "tm", 0, 0, tiled=True)
    partner, near, far = across(moved)
    taps_before = tap_grad(taps_n, grad_conv, glu)
    perturbation, normed_b = ascend(
        scal, squares, wide_features, wide_noise, moved, partner, near, far, start_noise[0]
    )

    _, _, glu, conv, stats = forward(scal, normed_b, weight, taps, chip_rows, chips)
    plain, crossed = raw_taps(taps_n, scal, conv, glu, stats)
    outgoing = last(
        taps_n, block, scal, counts, peers_of(stats), conv, cot, gain, shift, glu, plain, crossed, stats, taps_before, sums_before
    )
    outgoing = outgoing.reshape(shards, block // 2, PAY)
    if on_dp:
        outgoing = lax.psum(outgoing, "dp")
    received = lax.all_to_all(outgoing, "tm", 0, 0, tiled=True)
    sources = chips * (lax.axis_size("dp") if on_dp else 1)
    kernel_total, norm_total = finish(taps_n, sources, scal, received)
    return (perturbation[None], kernel_total, norm_total)


def solution(mesh):
    return jax.shard_map(
        functools.partial(on_device, mesh.shape["dp"] > 1),
        mesh=mesh,
        in_specs=(
            P("dp", "tm", None),
            P("dp", "tm", None),
            P("dp", "tm", None),
            P("tm", None),
            P(),
            P(),
            P(),
            P(),
        ),
        out_specs=(P("dp", "tm", None), P(None, "tm"), P(None, "tm")),
        check_vma=False,
    )
```

```python
import functools

import jax
import jax.numpy as jnp
from jax import lax
from jax.experimental import pallas as pl
from jax.experimental.pallas import tpu as pltpu
from jax.sharding import PartitionSpec as P

ASCENT = 2

noise_scale = 0.5
ascent_rate = 0.5
layer_epsilon = 1e-05
batch_epsilon = 1e-05
ascent_epsilon = 1e-06

HALO = 32
EDGE = 16
F32 = jnp.float32
BF16 = jnp.bfloat16


def params(limit=56 * 1024 * 1024):
    return pltpu.CompilerParams(vmem_limit_bytes=limit)


def cost(flops, nbytes):
    return pl.CostEstimate(flops=int(flops), bytes_accessed=int(nbytes), transcendentals=0)


def normalize(summed):
    centre = summed - jnp.mean(summed, axis=-1, keepdims=True)
    inverse = lax.rsqrt(jnp.mean(centre * centre, axis=-1, keepdims=True) + layer_epsilon)
    return (centre * inverse, inverse)


def live_rows(first, rows, end):
    ids = first + lax.broadcasted_iota(jnp.int32, (rows, 1), 0)
    return jnp.where((ids >= 0) & (ids < end), 1.0, 0.0).astype(F32)


def spread(plain, shifted, array):
    plain[...] = array
    rows, tiles = shifted.shape[1] * 8, shifted.shape[1]
    for s in range(8):
        shifted[s] = plain[s : s + rows].reshape(tiles, 8, -1)


def tiles_at(shifted, row, tiles, lanes):
    first = (row - row % 8) // 8
    return shifted[row % 8, first : first + tiles, :, lanes]


def convolve(taps, shifted, offsets, rows, most):
    most = max(n for n in range(1, most + 1) if rows // 8 % n == 0)
    columns = []
    for lane in range(0, taps.shape[2], 128):
        lanes = slice(lane, lane + 128)
        parts = []
        for tile in range(0, rows // 8, most):
            total = jnp.zeros((most, 8, 128), F32)
            for tap, offset in enumerate(offsets):
                total = total + taps[tap, :, lanes][None] * tiles_at(
                    shifted, offset + 8 * tile, most, lanes
                )
            parts.append(total.reshape(most * 8, 128))
        columns.append(jnp.concatenate(parts, axis=0))
    return jnp.concatenate(columns, axis=1)


def correlate(taps_n, left, shifted, first):
    rows = left.shape[0]
    lanes = slice(0, 128)
    most = 16
    totals = [None] * taps_n
    for tile in range(0, rows // 8, most):
        part = left[8 * tile : 8 * (tile + most)].reshape(most, 8, 128)
        for tap in range(taps_n):
            product = jnp.sum(
                part * tiles_at(shifted, first + tap + 8 * tile, most, lanes), axis=0, keepdims=True
            )
            totals[tap] = product if totals[tap] is None else totals[tap] + product
    return jnp.sum(jnp.concatenate(totals, axis=0), axis=1)


def place_weights(scal, weights, low, high, steps_a, value_w, gate_w):
    own_v, own_g, x_v, x_g, y_v, y_g, d_v, d_g = weights
    step, spot = pl.program_id(0), scal[4]
    rows = own_v.shape[1]

    @pl.when(step < steps_a)
    def _():
        for other, (v, g) in enumerate(((own_v, own_g), (x_v, x_g), (y_v, y_g), (d_v, d_g))):
            at = pl.ds(pl.multiple_of((spot ^ other) * rows, rows), rows)
            value_w[at, :] = v[0]
            gate_w[at, :] = g[0]

    @pl.when(step >= steps_a)
    def _():
        value_w[...] = low[...]
        gate_w[...] = high[...]


def weight_specs(wide_parts, square):
    own, _, _, d_low, _ = wide_parts
    depth, rows, width = own.shape
    half = depth // 2
    chunk = 4 * rows
    steps_b = square.shape[0] // 2 // chunk
    low = lambda i: (jnp.minimum(i, half - 1), 0, 0)
    high = lambda i: (jnp.minimum(i, half - 1) + half, 0, 0)
    block = (1, rows, width)
    specs = []
    for _ in range(3):
        specs += [pl.BlockSpec(block, low), pl.BlockSpec(block, high)]
    specs += [pl.BlockSpec(block, low), pl.BlockSpec(block, low)]
    specs += [
        pl.BlockSpec((chunk, width), lambda i: (jnp.maximum(i - half, 0), 0)),
        pl.BlockSpec((chunk, width), lambda i: (jnp.maximum(i - half, 0) + steps_b, 0)),
    ]
    own, x, y, d_low, d_high = wide_parts
    operands = [own, own, x, x, y, y, d_low, d_high, square, square]
    scratch = [pltpu.VMEM((chunk, width), BF16)] * 2
    return chunk, half, half + steps_b, specs, operands, scratch


def forward_kernel(steps_a, keep, scal, nb, *refs):
    weights, (low, high, taps), refs = refs[:8], refs[8:11], refs[11:]
    kept, (glu, conv, stats, value_w, gate_w, plain, shifted) = refs[: 2 * keep], refs[2 * keep :]
    place_weights(scal, weights, low, high, steps_a, value_w, gate_w)
    start, end = scal[0], scal[1]
    span, taps_n = nb.shape[0], taps.shape[0]
    rows = conv.shape[0] - 2 * EDGE
    contract = (((1,), (1,)), ((), ()))
    v = lax.dot_general(nb[...], value_w[...], contract, preferred_element_type=F32)
    s = jax.nn.sigmoid(lax.dot_general(nb[...], gate_w[...], contract, preferred_element_type=F32))
    if keep:
        kept[0][...] = v[HALO : HALO + rows]
        kept[1][...] = s[HALO : HALO + rows]
    gated = (v * s * live_rows(start - HALO, span, end)).astype(BF16)
    glu[...] = gated
    spread(plain, shifted, gated.astype(F32))
    shift = HALO - EDGE - (taps_n - 1) // 2
    conv[...] = convolve(taps, shifted, [shift + tap for tap in range(taps_n)], conv.shape[0], 12)
    live = live_rows(start, rows, end)
    own = conv[EDGE : EDGE + rows, :]
    mass = jnp.sum(live * own, axis=0, keepdims=True)
    centre = live * (own - mass / jnp.maximum(jnp.sum(live), 1.0))
    both = jnp.concatenate([mass, jnp.sum(centre * centre, axis=0, keepdims=True)], axis=0)
    for peer in range(stats.shape[0]):
        stats[peer] = both


def forward(scal, nb, wide_parts, square, taps, rows, peers, keep):
    span, width = nb.shape
    taps_n, _, half_width = taps.shape
    chunk, steps_a, steps, specs, operands, scratch = weight_specs(wide_parts, square)
    col = lambda n: pl.BlockSpec((n, chunk), lambda i: (0, i))
    return pl.pallas_call(
        functools.partial(forward_kernel, steps_a, keep),
        grid=(steps,),
        in_specs=[
            pl.BlockSpec(memory_space=pltpu.SMEM),
            pl.BlockSpec((span, width), lambda i: (0, 0)),
            *specs,
            pl.BlockSpec((taps_n, 8, chunk), lambda i: (0, 0, i)),
        ],
        out_specs=[
            *([col(rows)] * (2 * keep)),
            col(span),
            col(rows + 2 * EDGE),
            pl.BlockSpec((peers, 2, chunk), lambda i: (0, 0, i)),
        ],
        out_shape=[
            *([jax.ShapeDtypeStruct((rows, half_width), F32)] * (2 * keep)),
            jax.ShapeDtypeStruct((span, half_width), BF16),
            jax.ShapeDtypeStruct((rows + 2 * EDGE, half_width), F32),
            jax.ShapeDtypeStruct((peers, 2, half_width), F32),
        ],
        scratch_shapes=[
            *scratch,
            pltpu.VMEM((span, chunk), F32),
            pltpu.VMEM((8, span // 8 - 1, 8, chunk), F32),
        ],
        compiler_params=params(),
        cost_estimate=cost(2 * span * width * 2 * half_width, 4 * half_width * width + 10 * span * half_width),
        name="project_glu_conv",
    )(scal, nb, *operands, taps)


def moments(counts, stats, live_count):
    mass = stats[0, 0:1, :]
    square = stats[0, 1:2, :]
    for peer in range(1, stats.shape[0]):
        mass = mass + stats[peer, 0:1, :]
        square = square + stats[peer, 1:2, :]
    mean = mass / live_count
    for peer in range(stats.shape[0]):
        off = stats[peer, 0:1, :] - counts[0, peer] * mean
        square = square + off * off * counts[1, peer]
    return mean, lax.rsqrt(square / live_count + batch_epsilon)


def swish_grads(scal, counts, stats, conv, cot, gain, shift):
    start, end = scal[0], scal[1]
    live_count = scal[3].astype(F32)
    mean, inv = moments(counts, stats, live_count)
    scaled = (conv[...] - mean) * inv
    pre = gain[...] * scaled + shift[...]
    sig = jax.nn.sigmoid(pre)
    live = live_rows(start - EDGE, conv.shape[0], end)
    upstream = live * cot[...].astype(F32) / ASCENT
    return scaled, upstream * sig * (1.0 + pre * (1.0 - sig)), live, mean, inv


def batch_kernel(scal, counts, stats, conv, cot, gain, shift, scaled_out, grad_out, inv_out, sums):
    scaled, grad, live, mean, inv = swish_grads(scal, counts, stats, conv, cot, gain, shift)
    scaled_out[...] = scaled
    grad_out[...] = grad
    inv_out[...] = inv
    rows = conv.shape[0] - 2 * EDGE
    own = grad[EDGE : EDGE + rows]
    both = jnp.concatenate(
        [
            jnp.sum(own, axis=0, keepdims=True),
            jnp.sum(own * scaled[EDGE : EDGE + rows], axis=0, keepdims=True),
        ],
        axis=0,
    )
    for peer in range(sums.shape[0]):
        sums[peer] = both


def batch(scal, counts, stats, conv, cot, gain, shift, peers):
    span, half_width = conv.shape
    chunk = 256 if half_width % 256 == 0 else 128
    col = lambda n: pl.BlockSpec((n, chunk), lambda i: (0, i))
    smem = pl.BlockSpec(memory_space=pltpu.SMEM)
    return pl.pallas_call(
        batch_kernel,
        grid=(half_width // chunk,),
        in_specs=[
            smem,
            smem,
            pl.BlockSpec((stats.shape[0], 2, chunk), lambda i: (0, 0, i)),
            col(span),
            col(span),
            col(1),
            col(1),
        ],
        out_specs=[col(span), col(span), col(1), pl.BlockSpec((peers, 2, chunk), lambda i: (0, 0, i))],
        out_shape=[
            jax.ShapeDtypeStruct((span, half_width), F32),
            jax.ShapeDtypeStruct((span, half_width), F32),
            jax.ShapeDtypeStruct((1, half_width), F32),
            jax.ShapeDtypeStruct((peers, 2, half_width), F32),
        ],
        compiler_params=params(),
        cost_estimate=cost(40 * span * half_width, 16 * span * half_width),
        name="batch_norm_swish",
    )(scal, counts, stats, conv, cot, gain, shift)


def backward_kernel(steps_a, scal, sums, scaled, grad, inv, gain, taps, value, gate, *refs):
    weights, (low, high), refs = refs[:8], refs[8:10], refs[10:]
    mine, other, grad_conv, totals, value_w, gate_w, plain, shifted, part = refs
    place_weights(scal, weights, low, high, steps_a, value_w, gate_w)
    start, end, core = scal[0], scal[1], scal[2]
    rows, taps_n = value.shape[0], taps.shape[0]
    half = (taps_n - 1) // 2
    live_count = scal[3].astype(F32)
    both = sums[0]
    for peer in range(1, sums.shape[0]):
        both = both + sums[peer]
    totals[...] = both
    shift_sum, gain_sum = both[0:1], both[1:2]
    live = live_rows(start - EDGE, scaled.shape[0], end)
    through = live * (inv[...] * gain[...]) * (
        grad[...] - (shift_sum + scaled[...] * gain_sum) / live_count
    )
    rounded = through.astype(BF16)
    grad_conv[...] = rounded[EDGE : EDGE + rows]
    spread(plain, shifted, rounded.astype(F32))
    grad_glu = convolve(taps, shifted, [EDGE + half - tap for tap in range(taps_n)], rows, 16)
    grad_glu = (grad_glu * live_rows(start, rows, end)).astype(BF16).astype(F32)
    sig = gate[...]
    to_value = (grad_glu * sig).astype(BF16)
    to_gate = (grad_glu * value[...] * sig * (1.0 - sig)).astype(BF16)
    product = jnp.dot(to_value, value_w[...], preferred_element_type=F32) + jnp.dot(
        to_gate, gate_w[...], preferred_element_type=F32
    )
    step, last_step = pl.program_id(0), pl.num_programs(0) - 1

    @pl.when(step == 0)
    def _():
        part[...] = product

    @pl.when(step > 0)
    def _():
        part[...] += product

    @pl.when(step == last_step)
    def _():
        count = mine.shape[0]
        mine[...] = part[pl.ds(pl.multiple_of(core * count, count), count), :]
        other[...] = part[pl.ds(pl.multiple_of((1 - core) * count, count), count), :]


def backward(scal, sums, scaled, grad, inv, gain, taps, value, gate, wide_parts, square):
    span, half_width = scaled.shape
    rows, width = value.shape[0], square.shape[1]
    chunk, steps_a, steps, specs, operands, scratch = weight_specs(wide_parts, square)
    taps_n = taps.shape[0]
    col = lambda n: pl.BlockSpec((n, chunk), lambda i: (0, i))
    own = pl.BlockSpec((rows // 2, width), lambda i: (0, 0))
    return pl.pallas_call(
        functools.partial(backward_kernel, steps_a),
        grid=(steps,),
        in_specs=[
            pl.BlockSpec(memory_space=pltpu.SMEM),
            pl.BlockSpec((sums.shape[0], 2, chunk), lambda i: (0, 0, i)),
            col(span),
            col(span),
            col(1),
            col(1),
            pl.BlockSpec((taps_n, 8, chunk), lambda i: (0, 0, i)),
            col(rows),
            col(rows),
            *specs,
        ],
        out_specs=[own, own, col(rows), col(2)],
        out_shape=[
            jax.ShapeDtypeStruct((rows // 2, width), F32),
            jax.ShapeDtypeStruct((rows // 2, width), F32),
            jax.ShapeDtypeStruct((rows, half_width), BF16),
            jax.ShapeDtypeStruct((2, half_width), F32),
        ],
        scratch_shapes=[
            *scratch,
            pltpu.VMEM((span, chunk), F32),
            pltpu.VMEM((8, span // 8 - 1, 8, chunk), F32),
            pltpu.VMEM((rows, width), F32),
        ],
        compiler_params=params(),
        cost_estimate=cost(2 * rows * width * 2 * half_width, 4 * half_width * width + 20 * span * half_width),
        name="grad_conv_project_back",
    )(scal, sums, scaled, grad, inv, gain, taps, value, gate, *operands)


def shifted_scratch(span):
    return [pltpu.VMEM((span, 128), F32), pltpu.VMEM((8, span // 8 - 1, 8, 128), F32)]


def tap_grad_kernel(taps_n, grad_conv, glu, out, plain, shifted):
    spread(plain, shifted, glu[...].astype(F32))
    first = HALO - (taps_n - 1) // 2
    out[...] = correlate(taps_n, grad_conv[...].astype(F32), shifted, first)


def tap_grad(taps_n, grad_conv, glu):
    rows, half_width = grad_conv.shape
    span = glu.shape[0]
    col = lambda n: pl.BlockSpec((n, 128), lambda i: (0, i))
    return pl.pallas_call(
        functools.partial(tap_grad_kernel, taps_n),
        grid=(half_width // 128,),
        in_specs=[col(rows), col(span)],
        out_specs=col(taps_n),
        out_shape=jax.ShapeDtypeStruct((taps_n, half_width), F32),
        scratch_shapes=shifted_scratch(span),
        compiler_params=params(),
        cost_estimate=cost(2 * taps_n * rows * half_width, 4 * span * half_width),
        name="tap_grad",
    )(grad_conv, glu)


def raw_taps_kernel(taps_n, scal, conv, glu, stats, alone, crossed, plain, shifted):
    start, end = scal[0], scal[1]
    rows, span = conv.shape[0] - 2 * EDGE, glu.shape[0]
    spread(plain, shifted, glu[...].astype(F32))
    first = HALO - (taps_n - 1) // 2
    live = live_rows(start, rows, end)
    local = stats[0, 0:1, :] / jnp.maximum(jnp.sum(live), 1.0)
    crossed[...] = correlate(taps_n, live * (conv[EDGE : EDGE + rows, :] - local), shifted, first)
    tap = lax.broadcasted_iota(jnp.int32, (taps_n, span), 0)
    at = lax.broadcasted_iota(jnp.int32, (taps_n, span), 1) - first - tap
    inside = (at >= 0) & (at < jnp.clip(end - start, 0, rows))
    alone[...] = jnp.dot(
        jnp.where(inside, 1.0, 0.0).astype(BF16), glu[...], preferred_element_type=F32
    )


def raw_taps(taps_n, scal, conv, glu, stats):
    rows, half_width = conv.shape
    span = glu.shape[0]
    col = lambda n: pl.BlockSpec((n, 128), lambda i: (0, i))
    return pl.pallas_call(
        functools.partial(raw_taps_kernel, taps_n),
        grid=(half_width // 128,),
        in_specs=[
            pl.BlockSpec(memory_space=pltpu.SMEM),
            col(rows),
            col(span),
            pl.BlockSpec((1, 2, 128), lambda i: (0, 0, i)),
        ],
        out_specs=[col(taps_n), col(taps_n)],
        out_shape=[jax.ShapeDtypeStruct((taps_n, half_width), F32)] * 2,
        scratch_shapes=shifted_scratch(span),
        compiler_params=params(),
        cost_estimate=cost(2 * taps_n * rows * half_width, 8 * span * half_width),
        name="raw_taps",
    )(scal, conv, glu, stats)


def halves(array):
    high = array.astype(BF16).astype(F32)
    return high, array - high


def last_kernel(taps_n, part_a, scal, counts, stats, conv, cot, gain, shift, glu, alone, crossed, local_stats, taps_before, out, factor_out, plain, shifted, pay):
    step = pl.program_id(0)
    scaled, grad, live, mean, inv = swish_grads(scal, counts, stats, conv, cot, gain, shift)
    rows = conv.shape[0] - 2 * EDGE
    spread(plain, shifted, glu[...].astype(F32))
    first = HALO - (taps_n - 1) // 2
    factor = inv * gain[...]
    factor_out[...] = factor
    own = grad[EDGE : EDGE + rows]
    direct = taps_before[...] + factor * correlate(taps_n, own, shifted, first)
    own_live = live[EDGE : EDGE + rows]
    local = local_stats[0, 0:1, :] / jnp.maximum(jnp.sum(own_live), 1.0)
    with_scaled = inv * (crossed[...] + (local - mean) * alone[...])
    sums = jnp.concatenate(
        [
            jnp.sum(own, axis=0, keepdims=True),
            jnp.sum(own * scaled[EDGE : EDGE + rows], axis=0, keepdims=True),
        ],
        axis=0,
    )
    pay[step] = jnp.concatenate([*halves(direct), with_scaled, alone[...], *halves(sums)], axis=0)

    @pl.when(step == pl.num_programs(0) - 1)
    def _():
        turned = jnp.concatenate([jnp.transpose(pay[s]) for s in range(pay.shape[0])], axis=0)
        peers, block = out.shape[0], out.shape[1]
        part_b = block - part_a
        for index in range(peers):
            low, high = index * part_a, peers * part_a + index * part_b
            out[index] = jnp.concatenate(
                [turned[low : low + part_a], turned[high : high + part_b]], axis=0
            ).astype(BF16)


def last(taps_n, part_a, peers, scal, counts, stats, conv, cot, gain, shift, glu, alone, crossed, local_stats, taps_before):
    span, half_width = conv.shape
    chunk = 128
    steps = half_width // chunk
    pay = 4 * taps_n + 4
    col = lambda n: pl.BlockSpec((n, chunk), lambda i: (0, i))
    smem = pl.BlockSpec(memory_space=pltpu.SMEM)
    return pl.pallas_call(
        functools.partial(last_kernel, taps_n, part_a),
        grid=(steps,),
        in_specs=[
            smem,
            smem,
            pl.BlockSpec((stats.shape[0], 2, chunk), lambda i: (0, 0, i)),
            col(span),
            col(span),
            col(1),
            col(1),
            col(glu.shape[0]),
            col(taps_n),
            col(taps_n),
            pl.BlockSpec((1, 2, chunk), lambda i: (0, 0, i)),
            col(taps_n),
        ],
        out_specs=[pl.BlockSpec((peers, half_width // peers, pay), lambda i: (0, 0, 0)), col(1)],
        out_shape=[
            jax.ShapeDtypeStruct((peers, half_width // peers, pay), BF16),
            jax.ShapeDtypeStruct((1, half_width), F32),
        ],
        scratch_shapes=[*shifted_scratch(glu.shape[0]), pltpu.VMEM((steps, pay, chunk), F32)],
        compiler_params=params(),
        cost_estimate=cost(100 * span * half_width, 10 * span * half_width),
        name="batch_norm_swish_taps",
    )(scal, counts, stats, conv, cot, gain, shift, glu, alone, crossed, local_stats, taps_before)


def finish_kernel(taps_n, scal, received, known, taps_out, norm_out):
    total = received[0].astype(F32)
    for index in range(1, received.shape[0]):
        total = total + received[index].astype(F32)
    total = jnp.transpose(total)
    n = taps_n
    sums = total[4 * n : 4 * n + 2] + total[4 * n + 2 : 4 * n + 4]
    shift_sum, gain_sum = sums[0:1], sums[1:2]
    factor = known[0:1] / scal[3].astype(F32)
    taps_out[...] = (total[:n] + total[n : 2 * n]) - factor * (
        gain_sum * total[2 * n : 3 * n] + shift_sum * total[3 * n : 4 * n]
    )
    norm_out[...] = jnp.concatenate([gain_sum + known[2:3], shift_sum + known[1:2]], axis=0)


def finish(taps_n, scal, received, known):
    width = received.shape[1]
    vmem = pl.BlockSpec(memory_space=pltpu.VMEM)
    return pl.pallas_call(
        functools.partial(finish_kernel, taps_n),
        in_specs=[pl.BlockSpec(memory_space=pltpu.SMEM), vmem, vmem],
        out_shape=[
            jax.ShapeDtypeStruct((taps_n, width), F32),
            jax.ShapeDtypeStruct((2, width), F32),
        ],
        compiler_params=params(),
        name="finish",
    )(scal, received, known)


def direction_kernel(scal, mine, other, features, noise, out, edge, squares):
    rows = mine.shape[0]
    first = scal[0] + scal[2] * rows
    block = 32
    total = jnp.zeros((1, 128), F32)
    for row in range(0, rows, block):
        at = slice(row, row + block)
        live = live_rows(first + row, block, scal[1])
        summed = features[at].astype(F32) + noise_scale * noise[at].astype(F32) * live
        normed, inverse = normalize(summed)
        grad = mine[at] + other[at]
        moved = (
            live
            * inverse
            * (
                grad
                - jnp.mean(grad, axis=-1, keepdims=True)
                - normed * jnp.mean(grad * normed, axis=-1, keepdims=True)
            )
        )
        out[at] = moved
        total = total + jnp.sum(moved * moved)
    edge[...] = jnp.where(scal[2] == 0, out[:HALO], out[rows - HALO :])
    for peer in range(squares.shape[0]):
        squares[peer] = total


def direction(scal, mine, other, features, noise, peers):
    rows, width = mine.shape
    vmem = pl.BlockSpec(memory_space=pltpu.VMEM)
    return pl.pallas_call(
        direction_kernel,
        in_specs=[pl.BlockSpec(memory_space=pltpu.SMEM)] + [vmem] * 4,
        out_shape=[
            jax.ShapeDtypeStruct((rows, width), F32),
            jax.ShapeDtypeStruct((HALO, width), F32),
            jax.ShapeDtypeStruct((peers, 1, 128), F32),
        ],
        compiler_params=params(),
        cost_estimate=cost(30 * rows * width, 16 * rows * width),
        name="direction",
    )(scal, mine, other, features, noise)


def ascend_kernel(scal, squares, features, noise, mine, partner, near, far, own_noise, perturbation, normed_out):
    start, end, core = scal[0], scal[1], scal[2]
    rows, width = mine.shape
    total = squares[0]
    for index in range(1, squares.shape[0]):
        total = total + squares[index]
    total = total[0:1, 0:1]
    length = jnp.full((1, 1), 1.0, F32) * end.astype(F32)
    rate = ascent_rate * jnp.sqrt(length * width) / (jnp.sqrt(total) + ascent_epsilon)
    block = 32
    is_first = core == 0

    def place(row, moved):
        at = slice(row, row + block)
        live = live_rows(start - HALO + row, block, end)
        summed = features[at].astype(F32) + (noise_scale * noise[at].astype(F32) * live + moved * rate)
        normed_out[at] = normalize(summed)[0].astype(BF16)

    place(0, jnp.where(is_first, far[...], near[...]))
    for row in range(0, rows, block):
        at = slice(row, row + block)
        place(HALO + row, jnp.where(is_first, mine[at], partner[at]))
        place(HALO + rows + row, jnp.where(is_first, partner[at], mine[at]))
        live = live_rows(start + core * rows + row, block, end)
        perturbation[at] = noise_scale * own_noise[at].astype(F32) * live + mine[at] * rate
    place(HALO + 2 * rows, jnp.where(is_first, near[...], far[...]))


def ascend(scal, squares, features, noise, mine, partner, near, far, own_noise):
    vmem = pl.BlockSpec(memory_space=pltpu.VMEM)
    return pl.pallas_call(
        ascend_kernel,
        in_specs=[pl.BlockSpec(memory_space=pltpu.SMEM)] + [vmem] * 8,
        out_shape=[
            jax.ShapeDtypeStruct(mine.shape, F32),
            jax.ShapeDtypeStruct(features.shape, BF16),
        ],
        compiler_params=params(),
        cost_estimate=cost(30 * features.size, 8 * features.size),
        name="ascend",
    )(scal, squares, features, noise, mine, partner, near, far, own_noise)


def on_device(on_dp, features, start_noise, cotangent, in_weight, kernel, bn_gain, bn_shift, ends):
    rows, width = features.shape[1:]
    taps_n = kernel.shape[0]
    shards = lax.axis_size("tm")
    chips = shards // 2
    index = lax.axis_index("tm")
    group = lax.axis_index("dp")
    chip, core = index // 2, index % 2
    chip_rows = 2 * rows
    half_width = width // 2
    end = lax.dynamic_index_in_dim(ends, group, 0, keepdims=False)
    scal = jnp.stack([chip * chip_rows, end, core, jnp.sum(ends), chip % 4]).astype(jnp.int32)
    held = jnp.clip(
        ends[:, None] - chip_rows * jnp.arange(chips, dtype=jnp.int32)[None, :], 0, chip_rows
    ).reshape(-1).astype(F32)
    counts = jnp.stack([held, jnp.where(held > 0, 1.0 / jnp.maximum(held, 1.0), 0.0)])

    cores = [[2 * c + k for c in range(chips)] for k in range(2)]
    columns = [[8 * z + k for z in range(shards // 8)] for k in range(8)]
    swap = [(i, i ^ 1) for i in range(shards)]
    swap_x = [(i, i ^ 2) for i in range(shards)]
    swap_y = [(i, i ^ 4) for i in range(shards)]
    near_pairs = [(2 * c, 2 * c - 2) for c in range(1, chips)] + [
        (2 * c + 1, 2 * c + 3) for c in range(chips - 1)
    ]
    far_pairs = [(2 * c, 2 * c - 1) for c in range(1, chips)] + [
        (2 * c + 1, 2 * c + 2) for c in range(chips - 1)
    ]
    first = core == 0

    def across(array, edge):
        return (
            lax.ppermute(array, "tm", swap),
            lax.ppermute(edge, "tm", near_pairs),
            lax.ppermute(edge, "tm", far_pairs),
        )

    def peers_of(array):
        array = lax.all_to_all(array, "tm", 0, 0, axis_index_groups=cores, tiled=True)
        if on_dp:
            array = lax.all_gather(array, "dp", axis=0, tiled=True)
        return array

    def around(array):
        half = array.shape[0] // 2
        from_x = lax.ppermute(array, "tm", swap_x)
        from_y = lax.ppermute(array, "tm", swap_y)
        return (
            from_x,
            from_y,
            lax.ppermute(from_y[:half], "tm", swap_x),
            lax.ppermute(from_x[half:], "tm", swap_y),
        )

    slice_width = width // shards
    part_a = 2 * slice_width // 3
    pair = in_weight.reshape(2, slice_width, width)
    kept = lax.dynamic_index_in_dim(pair, core, 0, keepdims=False)
    given = lax.ppermute(lax.dynamic_index_in_dim(pair, 1 - core, 0, keepdims=False), "tm", swap)
    one, two = jnp.where(first, kept, given), jnp.where(first, given, kept)
    weight_a = jnp.concatenate([one[:part_a], two[:part_a]], axis=0)
    weight_b = jnp.concatenate([one[part_a:], two[part_a:]], axis=0)
    column = lax.all_gather(weight_a, "tm", axis=0, axis_index_groups=columns, tiled=False)
    x_b, y_b, d_low, d_high = around(weight_b)
    four = (weight_b, x_b, y_b, jnp.concatenate([d_low, d_high], axis=0))
    spot = chip % 4
    square = jnp.stack(
        [
            jnp.where(spot == s, four[0], jnp.where(spot == s ^ 1, four[1], jnp.where(spot == s ^ 2, four[2], four[3])))
            for s in range(4)
        ]
    ).reshape(-1, width)
    square = lax.all_gather(square, "tm", axis=0, axis_index_groups=columns, tiled=True)
    wide_parts = (column, *around(column))

    packed = jnp.concatenate([features, start_noise, cotangent], axis=0)
    partner, near, far = across(
        packed, jnp.where(first, packed[:, :HALO], packed[:, rows - HALO :])
    )
    whole = jnp.concatenate(
        [
            jnp.where(first, far, near),
            jnp.where(first, packed, partner),
            jnp.where(first, partner, packed),
            jnp.where(first, near, far),
        ],
        axis=1,
    )
    wide_features, wide_noise, wide_cot = whole[0], whole[1], whole[2]

    place = jnp.arange(half_width, dtype=jnp.int32)
    part_b = slice_width - part_a
    in_a = place < chips * part_a
    rest = place - chips * part_a
    at = jnp.where(in_a, place // part_a, rest // part_b)
    within = jnp.where(in_a, place % part_a, part_a + rest % part_b)
    source = (2 * at + core) * slice_width + within
    chosen = (jnp.arange(width, dtype=jnp.int32)[:, None] == source[None, :]).astype(BF16)
    cot = jnp.dot(wide_cot[HALO - EDGE : -(HALO - EDGE)], chosen, preferred_element_type=F32).astype(BF16)

    def mine_of(array):
        parts = array.reshape(array.shape[0], chips, 2, slice_width)
        own = lax.dynamic_index_in_dim(parts, core, 2, keepdims=False)
        return jnp.concatenate(
            [
                own[..., :part_a].reshape(array.shape[0], -1),
                own[..., part_a:].reshape(array.shape[0], -1),
            ],
            axis=1,
        )

    channel = mine_of(jnp.concatenate([kernel, bn_gain[None], bn_shift[None]], axis=0))
    gain, shift = channel[taps_n : taps_n + 1], channel[taps_n + 1 :]
    taps = jnp.broadcast_to(channel[:taps_n, None], (taps_n, 8, half_width))

    frame_ids = chip * chip_rows - HALO + jnp.arange(whole.shape[1], dtype=jnp.int32)
    live = ((frame_ids >= 0) & (frame_ids < end)).astype(F32)
    summed = wide_features.astype(F32) + noise_scale * wide_noise.astype(F32) * live[:, None]
    normed_b = normalize(summed)[0].astype(BF16)

    value, gate, glu, conv, stats = forward(
        scal, normed_b, wide_parts, square, taps, chip_rows, chips, True
    )
    scaled, grad, inv, sums = batch(scal, counts, peers_of(stats), conv, cot, gain, shift, chips)
    mine, other, grad_conv, totals = backward(
        scal, peers_of(sums), scaled, grad, inv, gain, taps, value, gate, wide_parts, square
    )
    other = lax.ppermute(other, "tm", swap)
    moved, edge, squares = direction(scal, mine, other, features[0], start_noise[0], shards)
    squares = lax.all_to_all(squares, "tm", 0, 0, tiled=True)
    partner, near, far = across(moved, edge)
    taps_before = tap_grad(taps_n, grad_conv, glu)
    squares, taps_before = lax.optimization_barrier((squares, taps_before))
    perturbation, normed_b = ascend(
        scal, squares, wide_features, wide_noise, moved, partner, near, far, start_noise[0]
    )

    glu, conv, stats = forward(scal, normed_b, wide_parts, square, taps, chip_rows, chips, False)
    alone, crossed = raw_taps(taps_n, scal, conv, glu, stats)
    outgoing, factor = last(
        taps_n, part_a, chips, scal, counts, peers_of(stats), conv, cot, gain, shift, glu, alone, crossed, stats, taps_before
    )
    received = peers_of(outgoing)
    known = jnp.concatenate([factor, totals], axis=0)
    known = jnp.concatenate(
        [
            lax.dynamic_slice_in_dim(known[:, : chips * part_a], chip * part_a, part_a, 1),
            lax.dynamic_slice_in_dim(known[:, chips * part_a :], chip * part_b, part_b, 1),
        ],
        axis=1,
    )
    kernel_total, norm_total = finish(taps_n, scal, received, known)
    return (perturbation[None], kernel_total, norm_total)


def solution(mesh):
    return jax.shard_map(
        functools.partial(on_device, mesh.shape["dp"] > 1),
        mesh=mesh,
        in_specs=(
            P("dp", "tm", None),
            P("dp", "tm", None),
            P("dp", "tm", None),
            P("tm", None),
            P(),
            P(),
            P(),
            P(),
        ),
        out_specs=(P("dp", "tm", None), P(None, "tm"), P(None, "tm")),
        check_vma=False,
    )
```

```python
import functools

import jax
import jax.numpy as jnp
from jax import lax
from jax.experimental import pallas as pl
from jax.experimental.pallas import tpu as pltpu
from jax.sharding import PartitionSpec as P

ASCENT = 2

noise_scale = 0.5
ascent_rate = 0.5
layer_epsilon = 1e-05
batch_epsilon = 1e-05
ascent_epsilon = 1e-06

HALO = 32
EDGE = 16
F32 = jnp.float32
BF16 = jnp.bfloat16


def params(limit=56 * 1024 * 1024):
    return pltpu.CompilerParams(vmem_limit_bytes=limit)


def cost(flops, nbytes):
    return pl.CostEstimate(flops=int(flops), bytes_accessed=int(nbytes), transcendentals=0)


def normalize(summed):
    centre = summed - jnp.mean(summed, axis=-1, keepdims=True)
    inverse = lax.rsqrt(jnp.mean(centre * centre, axis=-1, keepdims=True) + layer_epsilon)
    return (centre * inverse, inverse)


def live_rows(first, rows, end):
    ids = first + lax.broadcasted_iota(jnp.int32, (rows, 1), 0)
    return jnp.where((ids >= 0) & (ids < end), 1.0, 0.0).astype(F32)


def spread(plain, shifted, array):
    plain[...] = array
    rows, tiles = shifted.shape[1] * 8, shifted.shape[1]
    for s in range(8):
        shifted[s] = plain[s : s + rows].reshape(tiles, 8, -1)


def tiles_at(shifted, row, tiles, lanes):
    first = (row - row % 8) // 8
    return shifted[row % 8, first : first + tiles, :, lanes]


def convolve(taps, shifted, offsets, rows, most):
    most = max(n for n in range(1, most + 1) if rows // 8 % n == 0)
    columns = []
    for lane in range(0, taps.shape[2], 128):
        lanes = slice(lane, lane + 128)
        parts = []
        for tile in range(0, rows // 8, most):
            total = jnp.zeros((most, 8, 128), F32)
            for tap, offset in enumerate(offsets):
                total = total + taps[tap, :, lanes][None] * tiles_at(
                    shifted, offset + 8 * tile, most, lanes
                )
            parts.append(total.reshape(most * 8, 128))
        columns.append(jnp.concatenate(parts, axis=0))
    return jnp.concatenate(columns, axis=1)


def correlate(taps_n, left, shifted, first):
    rows = left.shape[0]
    lanes = slice(0, 128)
    most = 16
    totals = [None] * taps_n
    for tile in range(0, rows // 8, most):
        part = left[8 * tile : 8 * (tile + most)].reshape(most, 8, 128)
        for tap in range(taps_n):
            product = jnp.sum(
                part * tiles_at(shifted, first + tap + 8 * tile, most, lanes), axis=0, keepdims=True
            )
            totals[tap] = product if totals[tap] is None else totals[tap] + product
    return jnp.sum(jnp.concatenate(totals, axis=0), axis=1)


def place_kernel(depth, scal, *refs):
    blocks, out, sems = refs[:-2], refs[-2], refs[-1]
    spot, layer = scal[4], scal[5]
    copies = []
    for number, (shift, other, first, ref) in enumerate(blocks_of(blocks, depth)):
        layer_of = lax.rem(layer - shift + depth, depth)
        chip = layer_of * 4 + (spot ^ other)
        size = blocks[0].shape[0]
        row = pl.multiple_of(chip * size + first, 16)
        copies.append(
            pltpu.make_async_copy(ref, out.at[pl.ds(row, ref.shape[0]), :], sems.at[number])
        )
    for copy in copies:
        copy.start()
    for copy in copies:
        copy.wait()


def blocks_of(refs, depth):
    cut = refs[3].shape[0]
    for shift in range(depth):
        group = refs[5 * shift : 5 * shift + 5]
        for other, first, ref in zip((0, 1, 2, 3, 3), (0, 0, 0, 0, cut), group):
            yield shift, other, first, ref


def place(scal, pieces, depth):
    rows, width = pieces[0].shape
    hbm = pl.BlockSpec(memory_space=pl.ANY)
    return pl.pallas_call(
        functools.partial(place_kernel, depth),
        in_specs=[pl.BlockSpec(memory_space=pltpu.SMEM)] + [hbm] * len(pieces),
        out_specs=hbm,
        out_shape=jax.ShapeDtypeStruct((4 * depth * rows, width), BF16),
        scratch_shapes=[pltpu.SemaphoreType.DMA((len(pieces),))],
        compiler_params=params(),
        cost_estimate=cost(0, 16 * depth * rows * width),
        name="place_weights",
    )(scal, *pieces)


def forward_kernel(keep, scal, nb, value_w, gate_w, taps, *refs):
    kept, (glu, conv, stats, plain, shifted) = refs[: 2 * keep], refs[2 * keep :]
    start, end = scal[0], scal[1]
    span, taps_n = nb.shape[0], taps.shape[0]
    rows = conv.shape[0] - 2 * EDGE
    contract = (((1,), (1,)), ((), ()))
    v = lax.dot_general(nb[...], value_w[...], contract, preferred_element_type=F32)
    s = jax.nn.sigmoid(lax.dot_general(nb[...], gate_w[...], contract, preferred_element_type=F32))
    if keep:
        kept[0][...] = v[HALO : HALO + rows]
        kept[1][...] = s[HALO : HALO + rows]
    gated = (v * s * live_rows(start - HALO, span, end)).astype(BF16)
    glu[...] = gated
    spread(plain, shifted, gated.astype(F32))
    shift = HALO - EDGE - (taps_n - 1) // 2
    conv[...] = convolve(taps, shifted, [shift + tap for tap in range(taps_n)], conv.shape[0], 12)
    live = live_rows(start, rows, end)
    own = conv[EDGE : EDGE + rows, :]
    mass = jnp.sum(live * own, axis=0, keepdims=True)
    centre = live * (own - mass / jnp.maximum(jnp.sum(live), 1.0))
    both = jnp.concatenate([mass, jnp.sum(centre * centre, axis=0, keepdims=True)], axis=0)
    for peer in range(stats.shape[0]):
        stats[peer] = both


def forward(scal, nb, weight, taps, rows, peers, keep):
    span, width = nb.shape
    taps_n, _, half_width = taps.shape
    chunk = 256 if half_width % 256 == 0 else 128
    steps = half_width // chunk
    col = lambda n: pl.BlockSpec((n, chunk), lambda i: (0, i))
    return pl.pallas_call(
        functools.partial(forward_kernel, keep),
        grid=(steps,),
        in_specs=[
            pl.BlockSpec(memory_space=pltpu.SMEM),
            pl.BlockSpec((span, width), lambda i: (0, 0)),
            pl.BlockSpec((chunk, width), lambda i: (i, 0)),
            pl.BlockSpec((chunk, width), lambda i: (i + steps, 0)),
            pl.BlockSpec((taps_n, 8, chunk), lambda i: (0, 0, i)),
        ],
        out_specs=[
            *([col(rows)] * (2 * keep)),
            col(span),
            col(rows + 2 * EDGE),
            pl.BlockSpec((peers, 2, chunk), lambda i: (0, 0, i)),
        ],
        out_shape=[
            *([jax.ShapeDtypeStruct((rows, half_width), F32)] * (2 * keep)),
            jax.ShapeDtypeStruct((span, half_width), BF16),
            jax.ShapeDtypeStruct((rows + 2 * EDGE, half_width), F32),
            jax.ShapeDtypeStruct((peers, 2, half_width), F32),
        ],
        scratch_shapes=[
            pltpu.VMEM((span, chunk), F32),
            pltpu.VMEM((8, span // 8 - 1, 8, chunk), F32),
        ],
        compiler_params=params(),
        cost_estimate=cost(2 * span * width * 2 * half_width, 4 * half_width * width + 10 * span * half_width),
        name="project_glu_conv",
    )(scal, nb, weight, weight, taps)


def moments(counts, stats, live_count):
    mass = stats[0, 0:1, :]
    square = stats[0, 1:2, :]
    for peer in range(1, stats.shape[0]):
        mass = mass + stats[peer, 0:1, :]
        square = square + stats[peer, 1:2, :]
    mean = mass / live_count
    for peer in range(stats.shape[0]):
        off = stats[peer, 0:1, :] - counts[0, peer] * mean
        square = square + off * off * counts[1, peer]
    return mean, lax.rsqrt(square / live_count + batch_epsilon)


def swish_grads(scal, counts, stats, conv, cot, gain, shift):
    start, end = scal[0], scal[1]
    live_count = scal[3].astype(F32)
    mean, inv = moments(counts, stats, live_count)
    scaled = (conv[...] - mean) * inv
    pre = gain[...] * scaled + shift[...]
    sig = jax.nn.sigmoid(pre)
    live = live_rows(start - EDGE, conv.shape[0], end)
    upstream = live * cot[...].astype(F32) / ASCENT
    return scaled, upstream * sig * (1.0 + pre * (1.0 - sig)), live, mean, inv


def batch_kernel(scal, counts, stats, conv, cot, gain, shift, scaled_out, grad_out, inv_out, sums):
    scaled, grad, live, mean, inv = swish_grads(scal, counts, stats, conv, cot, gain, shift)
    scaled_out[...] = scaled
    grad_out[...] = grad
    inv_out[...] = inv
    rows = conv.shape[0] - 2 * EDGE
    own = grad[EDGE : EDGE + rows]
    both = jnp.concatenate(
        [
            jnp.sum(own, axis=0, keepdims=True),
            jnp.sum(own * scaled[EDGE : EDGE + rows], axis=0, keepdims=True),
        ],
        axis=0,
    )
    for peer in range(sums.shape[0]):
        sums[peer] = both


def batch(scal, counts, stats, conv, cot, gain, shift, peers):
    span, half_width = conv.shape
    chunk = 256 if half_width % 256 == 0 else 128
    col = lambda n: pl.BlockSpec((n, chunk), lambda i: (0, i))
    smem = pl.BlockSpec(memory_space=pltpu.SMEM)
    return pl.pallas_call(
        batch_kernel,
        grid=(half_width // chunk,),
        in_specs=[
            smem,
            smem,
            pl.BlockSpec((stats.shape[0], 2, chunk), lambda i: (0, 0, i)),
            col(span),
            col(span),
            col(1),
            col(1),
        ],
        out_specs=[col(span), col(span), col(1), pl.BlockSpec((peers, 2, chunk), lambda i: (0, 0, i))],
        out_shape=[
            jax.ShapeDtypeStruct((span, half_width), F32),
            jax.ShapeDtypeStruct((span, half_width), F32),
            jax.ShapeDtypeStruct((1, half_width), F32),
            jax.ShapeDtypeStruct((peers, 2, half_width), F32),
        ],
        compiler_params=params(),
        cost_estimate=cost(40 * span * half_width, 16 * span * half_width),
        name="batch_norm_swish",
    )(scal, counts, stats, conv, cot, gain, shift)


def backward_kernel(scal, sums, scaled, grad, inv, gain, taps, value, gate, value_w, gate_w, mine, other, grad_conv, totals, plain, shifted, part):
    start, end, core = scal[0], scal[1], scal[2]
    rows, taps_n = value.shape[0], taps.shape[0]
    half = (taps_n - 1) // 2
    live_count = scal[3].astype(F32)
    both = sums[0]
    for peer in range(1, sums.shape[0]):
        both = both + sums[peer]
    totals[...] = both
    shift_sum, gain_sum = both[0:1], both[1:2]
    live = live_rows(start - EDGE, scaled.shape[0], end)
    through = live * (inv[...] * gain[...]) * (
        grad[...] - (shift_sum + scaled[...] * gain_sum) / live_count
    )
    rounded = through.astype(BF16)
    grad_conv[...] = rounded[EDGE : EDGE + rows]
    spread(plain, shifted, rounded.astype(F32))
    grad_glu = convolve(taps, shifted, [EDGE + half - tap for tap in range(taps_n)], rows, 16)
    grad_glu = (grad_glu * live_rows(start, rows, end)).astype(BF16).astype(F32)
    sig = gate[...]
    to_value = (grad_glu * sig).astype(BF16)
    to_gate = (grad_glu * value[...] * sig * (1.0 - sig)).astype(BF16)
    product = jnp.dot(to_value, value_w[...], preferred_element_type=F32) + jnp.dot(
        to_gate, gate_w[...], preferred_element_type=F32
    )
    step, last_step = pl.program_id(0), pl.num_programs(0) - 1

    @pl.when(step == 0)
    def _():
        part[...] = product

    @pl.when(step > 0)
    def _():
        part[...] += product

    @pl.when(step == last_step)
    def _():
        count = mine.shape[0]
        mine[...] = part[pl.ds(pl.multiple_of(core * count, count), count), :]
        other[...] = part[pl.ds(pl.multiple_of((1 - core) * count, count), count), :]


def backward(scal, sums, scaled, grad, inv, gain, taps, value, gate, weight):
    span, half_width = scaled.shape
    rows, width = value.shape[0], weight.shape[1]
    chunk = 256 if half_width % 256 == 0 else 128
    steps = half_width // chunk
    taps_n = taps.shape[0]
    col = lambda n: pl.BlockSpec((n, chunk), lambda i: (0, i))
    own = pl.BlockSpec((rows // 2, width), lambda i: (0, 0))
    return pl.pallas_call(
        backward_kernel,
        grid=(steps,),
        in_specs=[
            pl.BlockSpec(memory_space=pltpu.SMEM),
            pl.BlockSpec((sums.shape[0], 2, chunk), lambda i: (0, 0, i)),
            col(span),
            col(span),
            col(1),
            col(1),
            pl.BlockSpec((taps_n, 8, chunk), lambda i: (0, 0, i)),
            col(rows),
            col(rows),
            pl.BlockSpec((chunk, width), lambda i: (i, 0)),
            pl.BlockSpec((chunk, width), lambda i: (i + steps, 0)),
        ],
        out_specs=[own, own, col(rows), col(2)],
        out_shape=[
            jax.ShapeDtypeStruct((rows // 2, width), F32),
            jax.ShapeDtypeStruct((rows // 2, width), F32),
            jax.ShapeDtypeStruct((rows, half_width), BF16),
            jax.ShapeDtypeStruct((2, half_width), F32),
        ],
        scratch_shapes=[
            pltpu.VMEM((span, chunk), F32),
            pltpu.VMEM((8, span // 8 - 1, 8, chunk), F32),
            pltpu.VMEM((rows, width), F32),
        ],
        compiler_params=params(),
        cost_estimate=cost(2 * rows * width * 2 * half_width, 4 * half_width * width + 20 * span * half_width),
        name="grad_conv_project_back",
    )(scal, sums, scaled, grad, inv, gain, taps, value, gate, weight, weight)


def shifted_scratch(span):
    return [pltpu.VMEM((span, 128), F32), pltpu.VMEM((8, span // 8 - 1, 8, 128), F32)]


def tap_grad_kernel(taps_n, grad_conv, glu, out, plain, shifted):
    spread(plain, shifted, glu[...].astype(F32))
    first = HALO - (taps_n - 1) // 2
    out[...] = correlate(taps_n, grad_conv[...].astype(F32), shifted, first)


def tap_grad(taps_n, grad_conv, glu):
    rows, half_width = grad_conv.shape
    span = glu.shape[0]
    col = lambda n: pl.BlockSpec((n, 128), lambda i: (0, i))
    return pl.pallas_call(
        functools.partial(tap_grad_kernel, taps_n),
        grid=(half_width // 128,),
        in_specs=[col(rows), col(span)],
        out_specs=col(taps_n),
        out_shape=jax.ShapeDtypeStruct((taps_n, half_width), F32),
        scratch_shapes=shifted_scratch(span),
        compiler_params=params(),
        cost_estimate=cost(2 * taps_n * rows * half_width, 4 * span * half_width),
        name="tap_grad",
    )(grad_conv, glu)


def raw_taps_kernel(taps_n, scal, conv, glu, stats, alone, crossed, plain, shifted):
    start, end = scal[0], scal[1]
    rows, span = conv.shape[0] - 2 * EDGE, glu.shape[0]
    spread(plain, shifted, glu[...].astype(F32))
    first = HALO - (taps_n - 1) // 2
    live = live_rows(start, rows, end)
    local = stats[0, 0:1, :] / jnp.maximum(jnp.sum(live), 1.0)
    crossed[...] = correlate(taps_n, live * (conv[EDGE : EDGE + rows, :] - local), shifted, first)
    tap = lax.broadcasted_iota(jnp.int32, (taps_n, span), 0)
    at = lax.broadcasted_iota(jnp.int32, (taps_n, span), 1) - first - tap
    inside = (at >= 0) & (at < jnp.clip(end - start, 0, rows))
    alone[...] = jnp.dot(
        jnp.where(inside, 1.0, 0.0).astype(BF16), glu[...], preferred_element_type=F32
    )


def raw_taps(taps_n, scal, conv, glu, stats):
    rows, half_width = conv.shape
    span = glu.shape[0]
    col = lambda n: pl.BlockSpec((n, 128), lambda i: (0, i))
    return pl.pallas_call(
        functools.partial(raw_taps_kernel, taps_n),
        grid=(half_width // 128,),
        in_specs=[
            pl.BlockSpec(memory_space=pltpu.SMEM),
            col(rows),
            col(span),
            pl.BlockSpec((1, 2, 128), lambda i: (0, 0, i)),
        ],
        out_specs=[col(taps_n), col(taps_n)],
        out_shape=[jax.ShapeDtypeStruct((taps_n, half_width), F32)] * 2,
        scratch_shapes=shifted_scratch(span),
        compiler_params=params(),
        cost_estimate=cost(2 * taps_n * rows * half_width, 8 * span * half_width),
        name="raw_taps",
    )(scal, conv, glu, stats)


def halves(array):
    high = array.astype(BF16).astype(F32)
    return high, array - high


def last_kernel(taps_n, scal, counts, stats, conv, cot, gain, shift, glu, alone, crossed, local_stats, taps_before, out, factor_out, plain, shifted, pay):
    step = pl.program_id(0)
    scaled, grad, live, mean, inv = swish_grads(scal, counts, stats, conv, cot, gain, shift)
    rows = conv.shape[0] - 2 * EDGE
    spread(plain, shifted, glu[...].astype(F32))
    first = HALO - (taps_n - 1) // 2
    factor = inv * gain[...]
    factor_out[...] = factor
    own = grad[EDGE : EDGE + rows]
    direct = taps_before[...] + factor * correlate(taps_n, own, shifted, first)
    own_live = live[EDGE : EDGE + rows]
    local = local_stats[0, 0:1, :] / jnp.maximum(jnp.sum(own_live), 1.0)
    with_scaled = inv * (crossed[...] + (local - mean) * alone[...])
    sums = jnp.concatenate(
        [
            jnp.sum(own, axis=0, keepdims=True),
            jnp.sum(own * scaled[EDGE : EDGE + rows], axis=0, keepdims=True),
        ],
        axis=0,
    )
    pay[step] = jnp.concatenate([*halves(direct), with_scaled, alone[...], *halves(sums)], axis=0)

    @pl.when(step == pl.num_programs(0) - 1)
    def _():
        turned = jnp.concatenate([jnp.transpose(pay[s]) for s in range(pay.shape[0])], axis=0)
        block = out.shape[1]
        for index in range(out.shape[0]):
            out[index] = turned[index * block : (index + 1) * block].astype(BF16)


def last(taps_n, peers, scal, counts, stats, conv, cot, gain, shift, glu, alone, crossed, local_stats, taps_before):
    span, half_width = conv.shape
    chunk = 128
    steps = half_width // chunk
    pay = 4 * taps_n + 4
    col = lambda n: pl.BlockSpec((n, chunk), lambda i: (0, i))
    smem = pl.BlockSpec(memory_space=pltpu.SMEM)
    return pl.pallas_call(
        functools.partial(last_kernel, taps_n),
        grid=(steps,),
        in_specs=[
            smem,
            smem,
            pl.BlockSpec((stats.shape[0], 2, chunk), lambda i: (0, 0, i)),
            col(span),
            col(span),
            col(1),
            col(1),
            col(glu.shape[0]),
            col(taps_n),
            col(taps_n),
            pl.BlockSpec((1, 2, chunk), lambda i: (0, 0, i)),
            col(taps_n),
        ],
        out_specs=[pl.BlockSpec((peers, half_width // peers, pay), lambda i: (0, 0, 0)), col(1)],
        out_shape=[
            jax.ShapeDtypeStruct((peers, half_width // peers, pay), BF16),
            jax.ShapeDtypeStruct((1, half_width), F32),
        ],
        scratch_shapes=[*shifted_scratch(glu.shape[0]), pltpu.VMEM((steps, pay, chunk), F32)],
        compiler_params=params(),
        cost_estimate=cost(100 * span * half_width, 10 * span * half_width),
        name="batch_norm_swish_taps",
    )(scal, counts, stats, conv, cot, gain, shift, glu, alone, crossed, local_stats, taps_before)


def finish_kernel(taps_n, scal, received, known, taps_out, norm_out):
    total = received[0].astype(F32)
    for index in range(1, received.shape[0]):
        total = total + received[index].astype(F32)
    total = jnp.transpose(total)
    n = taps_n
    sums = total[4 * n : 4 * n + 2] + total[4 * n + 2 : 4 * n + 4]
    shift_sum, gain_sum = sums[0:1], sums[1:2]
    factor = known[0:1] / scal[3].astype(F32)
    taps_out[...] = (total[:n] + total[n : 2 * n]) - factor * (
        gain_sum * total[2 * n : 3 * n] + shift_sum * total[3 * n : 4 * n]
    )
    norm_out[...] = jnp.concatenate([gain_sum + known[2:3], shift_sum + known[1:2]], axis=0)


def finish(taps_n, scal, received, known):
    width = received.shape[1]
    vmem = pl.BlockSpec(memory_space=pltpu.VMEM)
    return pl.pallas_call(
        functools.partial(finish_kernel, taps_n),
        in_specs=[pl.BlockSpec(memory_space=pltpu.SMEM), vmem, vmem],
        out_shape=[
            jax.ShapeDtypeStruct((taps_n, width), F32),
            jax.ShapeDtypeStruct((2, width), F32),
        ],
        compiler_params=params(),
        name="finish",
    )(scal, received, known)


def direction_kernel(scal, mine, other, features, noise, out, edge, squares):
    rows = mine.shape[0]
    first = scal[0] + scal[2] * rows
    block = 32
    total = jnp.zeros((1, 128), F32)
    for row in range(0, rows, block):
        at = slice(row, row + block)
        live = live_rows(first + row, block, scal[1])
        summed = features[at].astype(F32) + noise_scale * noise[at].astype(F32) * live
        normed, inverse = normalize(summed)
        grad = mine[at] + other[at]
        moved = (
            live
            * inverse
            * (
                grad
                - jnp.mean(grad, axis=-1, keepdims=True)
                - normed * jnp.mean(grad * normed, axis=-1, keepdims=True)
            )
        )
        out[at] = moved
        total = total + jnp.sum(moved * moved)
    edge[...] = jnp.where(scal[2] == 0, out[:HALO], out[rows - HALO :])
    for peer in range(squares.shape[0]):
        squares[peer] = total


def direction(scal, mine, other, features, noise, peers):
    rows, width = mine.shape
    vmem = pl.BlockSpec(memory_space=pltpu.VMEM)
    return pl.pallas_call(
        direction_kernel,
        in_specs=[pl.BlockSpec(memory_space=pltpu.SMEM)] + [vmem] * 4,
        out_shape=[
            jax.ShapeDtypeStruct((rows, width), F32),
            jax.ShapeDtypeStruct((HALO, width), F32),
            jax.ShapeDtypeStruct((peers, 1, 128), F32),
        ],
        compiler_params=params(),
        cost_estimate=cost(30 * rows * width, 16 * rows * width),
        name="direction",
    )(scal, mine, other, features, noise)


def ascend_kernel(scal, squares, features, noise, mine, partner, near, far, own_noise, perturbation, normed_out):
    start, end, core = scal[0], scal[1], scal[2]
    rows, width = mine.shape
    total = squares[0]
    for index in range(1, squares.shape[0]):
        total = total + squares[index]
    total = total[0:1, 0:1]
    length = jnp.full((1, 1), 1.0, F32) * end.astype(F32)
    rate = ascent_rate * jnp.sqrt(length * width) / (jnp.sqrt(total) + ascent_epsilon)
    block = 32
    is_first = core == 0

    def place(row, moved):
        at = slice(row, row + block)
        live = live_rows(start - HALO + row, block, end)
        summed = features[at].astype(F32) + (noise_scale * noise[at].astype(F32) * live + moved * rate)
        normed_out[at] = normalize(summed)[0].astype(BF16)

    place(0, jnp.where(is_first, far[...], near[...]))
    for row in range(0, rows, block):
        at = slice(row, row + block)
        place(HALO + row, jnp.where(is_first, mine[at], partner[at]))
        place(HALO + rows + row, jnp.where(is_first, partner[at], mine[at]))
        live = live_rows(start + core * rows + row, block, end)
        perturbation[at] = noise_scale * own_noise[at].astype(F32) * live + mine[at] * rate
    place(HALO + 2 * rows, jnp.where(is_first, near[...], far[...]))


def ascend(scal, squares, features, noise, mine, partner, near, far, own_noise):
    vmem = pl.BlockSpec(memory_space=pltpu.VMEM)
    return pl.pallas_call(
        ascend_kernel,
        in_specs=[pl.BlockSpec(memory_space=pltpu.SMEM)] + [vmem] * 8,
        out_shape=[
            jax.ShapeDtypeStruct(mine.shape, F32),
            jax.ShapeDtypeStruct(features.shape, BF16),
        ],
        compiler_params=params(),
        cost_estimate=cost(30 * features.size, 8 * features.size),
        name="ascend",
    )(scal, squares, features, noise, mine, partner, near, far, own_noise)


def on_device(on_dp, features, start_noise, cotangent, in_weight, kernel, bn_gain, bn_shift, ends):
    rows, width = features.shape[1:]
    taps_n = kernel.shape[0]
    shards = lax.axis_size("tm")
    chips = shards // 2
    index = lax.axis_index("tm")
    group = lax.axis_index("dp")
    chip, core = index // 2, index % 2
    chip_rows = 2 * rows
    half_width = width // 2
    end = lax.dynamic_index_in_dim(ends, group, 0, keepdims=False)
    scal = jnp.stack([chip * chip_rows, end, core, jnp.sum(ends), chip % 4, chip // 4]).astype(jnp.int32)
    held = jnp.clip(
        ends[:, None] - chip_rows * jnp.arange(chips, dtype=jnp.int32)[None, :], 0, chip_rows
    ).reshape(-1).astype(F32)
    counts = jnp.stack([held, jnp.where(held > 0, 1.0 / jnp.maximum(held, 1.0), 0.0)])

    cores = [[2 * c + k for c in range(chips)] for k in range(2)]
    depth = chips // 4
    onward = [(i, (i + 8) % shards) for i in range(shards)]
    swap = [(i, i ^ 1) for i in range(shards)]
    swap_x = [(i, i ^ 2) for i in range(shards)]
    swap_y = [(i, i ^ 4) for i in range(shards)]
    near_pairs = [(2 * c, 2 * c - 2) for c in range(1, chips)] + [
        (2 * c + 1, 2 * c + 3) for c in range(chips - 1)
    ]
    far_pairs = [(2 * c, 2 * c - 1) for c in range(1, chips)] + [
        (2 * c + 1, 2 * c + 2) for c in range(chips - 1)
    ]
    first = core == 0

    def across(array, edge):
        return (
            lax.ppermute(array, "tm", swap),
            lax.ppermute(edge, "tm", near_pairs),
            lax.ppermute(edge, "tm", far_pairs),
        )

    def peers_of(array):
        array = lax.all_to_all(array, "tm", 0, 0, axis_index_groups=cores, tiled=True)
        if on_dp:
            array = lax.all_gather(array, "dp", axis=0, tiled=True)
        return array

    slice_width = width // shards
    pair = in_weight.reshape(2, slice_width, width)
    kept = lax.dynamic_index_in_dim(pair, core, 0, keepdims=False)
    given = lax.ppermute(lax.dynamic_index_in_dim(pair, 1 - core, 0, keepdims=False), "tm", swap)
    block = jnp.concatenate([jnp.where(first, kept, given), jnp.where(first, given, kept)], axis=0)
    cut = (slice_width + 15) // 16 * 16
    pieces = []
    for shift in range(depth):
        if shift:
            block = lax.ppermute(block, "tm", onward)
        from_x = lax.ppermute(block, "tm", swap_x)
        from_y = lax.ppermute(block, "tm", swap_y)
        pieces += [
            block,
            from_x,
            from_y,
            lax.ppermute(from_y[:cut], "tm", swap_x),
            lax.ppermute(from_x[cut:], "tm", swap_y),
        ]
    weight = place(scal, pieces, depth)

    packed = jnp.concatenate([features, start_noise, cotangent], axis=0)
    packed, _ = lax.optimization_barrier((packed, given))
    partner, near, far = across(
        packed, jnp.where(first, packed[:, :HALO], packed[:, rows - HALO :])
    )
    whole = jnp.concatenate(
        [
            jnp.where(first, far, near),
            jnp.where(first, packed, partner),
            jnp.where(first, partner, packed),
            jnp.where(first, near, far),
        ],
        axis=1,
    )
    wide_features, wide_noise, wide_cot = whole[0], whole[1], whole[2]

    place_of = jnp.arange(half_width, dtype=jnp.int32)
    source = (2 * (place_of // slice_width) + core) * slice_width + place_of % slice_width
    chosen = (jnp.arange(width, dtype=jnp.int32)[:, None] == source[None, :]).astype(BF16)
    cot = jnp.dot(wide_cot[HALO - EDGE : -(HALO - EDGE)], chosen, preferred_element_type=F32).astype(BF16)

    def mine_of(array):
        parts = array.reshape(array.shape[0], chips, 2, slice_width)
        return lax.dynamic_index_in_dim(parts, core, 2, keepdims=False).reshape(-1, half_width)

    channel = mine_of(jnp.concatenate([kernel, bn_gain[None], bn_shift[None]], axis=0))
    gain, shift = channel[taps_n : taps_n + 1], channel[taps_n + 1 :]
    taps = jnp.broadcast_to(channel[:taps_n, None], (taps_n, 8, half_width))

    frame_ids = chip * chip_rows - HALO + jnp.arange(whole.shape[1], dtype=jnp.int32)
    live = ((frame_ids >= 0) & (frame_ids < end)).astype(F32)
    summed = wide_features.astype(F32) + noise_scale * wide_noise.astype(F32) * live[:, None]
    normed_b = normalize(summed)[0].astype(BF16)

    value, gate, glu, conv, stats = forward(
        scal, normed_b, weight, taps, chip_rows, chips, True
    )
    scaled, grad, inv, sums = batch(scal, counts, peers_of(stats), conv, cot, gain, shift, chips)
    mine, other, grad_conv, totals = backward(
        scal, peers_of(sums), scaled, grad, inv, gain, taps, value, gate, weight
    )
    other = lax.ppermute(other, "tm", swap)
    moved, edge, squares = direction(scal, mine, other, features[0], start_noise[0], shards)
    squares = lax.all_to_all(squares, "tm", 0, 0, tiled=True)
    partner, near, far = across(moved, edge)
    taps_before = tap_grad(taps_n, grad_conv, glu)
    squares, taps_before = lax.optimization_barrier((squares, taps_before))
    perturbation, normed_b = ascend(
        scal, squares, wide_features, wide_noise, moved, partner, near, far, start_noise[0]
    )

    glu, conv, stats = forward(scal, normed_b, weight, taps, chip_rows, chips, False)
    alone, crossed = raw_taps(taps_n, scal, conv, glu, stats)
    outgoing, factor = last(
        taps_n, chips, scal, counts, peers_of(stats), conv, cot, gain, shift, glu, alone, crossed, stats, taps_before
    )
    received = peers_of(outgoing)
    known = jnp.concatenate([factor, totals], axis=0)
    known = lax.dynamic_slice_in_dim(known, chip * slice_width, slice_width, 1)
    kernel_total, norm_total = finish(taps_n, scal, received, known)
    return (perturbation[None], kernel_total, norm_total)


def solution(mesh):
    return jax.shard_map(
        functools.partial(on_device, mesh.shape["dp"] > 1),
        mesh=mesh,
        in_specs=(
            P("dp", "tm", None),
            P("dp", "tm", None),
            P("dp", "tm", None),
            P("tm", None),
            P(),
            P(),
            P(),
            P(),
        ),
        out_specs=(P("dp", "tm", None), P(None, "tm"), P(None, "tm")),
        check_vma=False,
    )
```

```python
import functools

import jax
import jax.numpy as jnp
from jax import lax
from jax.experimental import pallas as pl
from jax.experimental.pallas import tpu as pltpu
from jax.sharding import PartitionSpec as P

ASCENT = 2

noise_scale = 0.5
ascent_rate = 0.5
layer_epsilon = 1e-05
batch_epsilon = 1e-05
ascent_epsilon = 1e-06

HALO = 32
EDGE = 16
F32 = jnp.float32
BF16 = jnp.bfloat16


def params(limit=56 * 1024 * 1024):
    return pltpu.CompilerParams(vmem_limit_bytes=limit)


def cost(flops, nbytes):
    return pl.CostEstimate(flops=int(flops), bytes_accessed=int(nbytes), transcendentals=0)


def normalize(summed):
    centre = summed - jnp.mean(summed, axis=-1, keepdims=True)
    inverse = lax.rsqrt(jnp.mean(centre * centre, axis=-1, keepdims=True) + layer_epsilon)
    return (centre * inverse, inverse)


def live_rows(first, rows, end):
    ids = first + lax.broadcasted_iota(jnp.int32, (rows, 1), 0)
    return jnp.where((ids >= 0) & (ids < end), 1.0, 0.0).astype(F32)


def spread(plain, shifted, array):
    plain[...] = array
    rows, tiles = shifted.shape[1] * 8, shifted.shape[1]
    for s in range(8):
        shifted[s] = plain[s : s + rows].reshape(tiles, 8, -1)


def tiles_at(shifted, row, tiles, lanes):
    first = (row - row % 8) // 8
    return shifted[row % 8, first : first + tiles, :, lanes]


def convolve(taps, shifted, offsets, rows, most):
    most = max(n for n in range(1, most + 1) if rows // 8 % n == 0)
    columns = []
    for lane in range(0, taps.shape[2], 128):
        lanes = slice(lane, lane + 128)
        parts = []
        for tile in range(0, rows // 8, most):
            total = jnp.zeros((most, 8, 128), F32)
            for tap, offset in enumerate(offsets):
                total = total + taps[tap, :, lanes][None] * tiles_at(
                    shifted, offset + 8 * tile, most, lanes
                )
            parts.append(total.reshape(most * 8, 128))
        columns.append(jnp.concatenate(parts, axis=0))
    return jnp.concatenate(columns, axis=1)


def correlate(taps_n, left, shifted, first):
    rows = left.shape[0]
    lanes = slice(0, 128)
    most = 16
    totals = [None] * taps_n
    for tile in range(0, rows // 8, most):
        part = left[8 * tile : 8 * (tile + most)].reshape(most, 8, 128)
        for tap in range(taps_n):
            product = jnp.sum(
                part * tiles_at(shifted, first + tap + 8 * tile, most, lanes), axis=0, keepdims=True
            )
            totals[tap] = product if totals[tap] is None else totals[tap] + product
    return jnp.sum(jnp.concatenate(totals, axis=0), axis=1)


def place_kernel(shifts, size, scal, *refs):
    pieces, out = refs[:-1], refs[-1]
    spot, layer = scal[4], scal[5]
    depth = out.shape[0] // (4 * size)

    def put(ref, start, stop, shift, other, first):
        chip = lax.rem(layer - shift + depth, depth) * 4 + (spot ^ other)
        row = pl.multiple_of(chip * size + first, 16)
        out[pl.ds(row, stop - start), :] = ref[start:stop, :]

    for number, group in enumerate(shifts):
        for other, ref in enumerate(pieces[5 * number : 5 * number + 3]):
            for nth, shift in enumerate(group):
                put(ref, nth * size, (nth + 1) * size, shift, other, 0)
        at = 0
        for ref in pieces[5 * number + 3 : 5 * number + 5]:
            rows = ref.shape[0]
            start = 0
            while start < rows:
                nth, first = (at + start) // size, (at + start) % size
                stop = min(rows, start + size - first)
                put(ref, start, stop, group[nth], 3, first)
                start = stop
            at += rows


def place(scal, pieces, shifts, size):
    width = pieces[0].shape[1]
    chips = 4 * sum(len(group) for group in shifts)
    vmem = pl.BlockSpec(memory_space=pltpu.VMEM)
    return pl.pallas_call(
        functools.partial(place_kernel, shifts, size),
        in_specs=[pl.BlockSpec(memory_space=pltpu.SMEM)] + [vmem] * len(pieces),
        out_specs=vmem,
        out_shape=jax.ShapeDtypeStruct((chips * size, width), BF16),
        compiler_params=params(),
        cost_estimate=cost(0, 4 * chips * size * width),
        name="place_weights",
    )(scal, *pieces)


def forward_kernel(keep, scal, nb, value_w, gate_w, taps, *refs):
    kept, (glu, conv, stats, plain, shifted) = refs[: 2 * keep], refs[2 * keep :]
    start, end = scal[0], scal[1]
    span, taps_n = nb.shape[0], taps.shape[0]
    rows = conv.shape[0] - 2 * EDGE
    contract = (((1,), (1,)), ((), ()))
    v = lax.dot_general(nb[...], value_w[...], contract, preferred_element_type=F32)
    s = jax.nn.sigmoid(lax.dot_general(nb[...], gate_w[...], contract, preferred_element_type=F32))
    if keep:
        kept[0][...] = v[HALO : HALO + rows]
        kept[1][...] = s[HALO : HALO + rows]
    gated = (v * s * live_rows(start - HALO, span, end)).astype(BF16)
    glu[...] = gated
    spread(plain, shifted, gated.astype(F32))
    shift = HALO - EDGE - (taps_n - 1) // 2
    conv[...] = convolve(taps, shifted, [shift + tap for tap in range(taps_n)], conv.shape[0], 12)
    live = live_rows(start, rows, end)
    own = conv[EDGE : EDGE + rows, :]
    mass = jnp.sum(live * own, axis=0, keepdims=True)
    centre = live * (own - mass / jnp.maximum(jnp.sum(live), 1.0))
    both = jnp.concatenate([mass, jnp.sum(centre * centre, axis=0, keepdims=True)], axis=0)
    for peer in range(stats.shape[0]):
        stats[peer] = both


def forward(scal, nb, weight, taps, rows, peers, keep):
    span, width = nb.shape
    taps_n, _, half_width = taps.shape
    chunk = 256 if half_width % 256 == 0 else 128
    steps = half_width // chunk
    col = lambda n: pl.BlockSpec((n, chunk), lambda i: (0, i))
    return pl.pallas_call(
        functools.partial(forward_kernel, keep),
        grid=(steps,),
        in_specs=[
            pl.BlockSpec(memory_space=pltpu.SMEM),
            pl.BlockSpec((span, width), lambda i: (0, 0)),
            pl.BlockSpec((chunk, width), lambda i: (i, 0)),
            pl.BlockSpec((chunk, width), lambda i: (i + steps, 0)),
            pl.BlockSpec((taps_n, 8, chunk), lambda i: (0, 0, i)),
        ],
        out_specs=[
            *([col(rows)] * (2 * keep)),
            col(span),
            col(rows + 2 * EDGE),
            pl.BlockSpec((peers, 2, chunk), lambda i: (0, 0, i)),
        ],
        out_shape=[
            *([jax.ShapeDtypeStruct((rows, half_width), F32)] * (2 * keep)),
            jax.ShapeDtypeStruct((span, half_width), BF16),
            jax.ShapeDtypeStruct((rows + 2 * EDGE, half_width), F32),
            jax.ShapeDtypeStruct((peers, 2, half_width), F32),
        ],
        scratch_shapes=[
            pltpu.VMEM((span, chunk), F32),
            pltpu.VMEM((8, span // 8 - 1, 8, chunk), F32),
        ],
        compiler_params=params(),
        cost_estimate=cost(2 * span * width * 2 * half_width, 4 * half_width * width + 10 * span * half_width),
        name="project_glu_conv",
    )(scal, nb, weight, weight, taps)


def moments(counts, stats, live_count):
    mass = stats[0, 0:1, :]
    square = stats[0, 1:2, :]
    for peer in range(1, stats.shape[0]):
        mass = mass + stats[peer, 0:1, :]
        square = square + stats[peer, 1:2, :]
    mean = mass / live_count
    for peer in range(stats.shape[0]):
        off = stats[peer, 0:1, :] - counts[0, peer] * mean
        square = square + off * off * counts[1, peer]
    return mean, lax.rsqrt(square / live_count + batch_epsilon)


def swish_grads(scal, counts, stats, conv, cot, gain, shift):
    start, end = scal[0], scal[1]
    live_count = scal[3].astype(F32)
    mean, inv = moments(counts, stats, live_count)
    scaled = (conv[...] - mean) * inv
    pre = gain[...] * scaled + shift[...]
    sig = jax.nn.sigmoid(pre)
    live = live_rows(start - EDGE, conv.shape[0], end)
    upstream = live * cot[...].astype(F32) / ASCENT
    return scaled, upstream * sig * (1.0 + pre * (1.0 - sig)), live, mean, inv


def batch_kernel(scal, counts, stats, conv, cot, gain, shift, scaled_out, grad_out, inv_out, sums):
    scaled, grad, live, mean, inv = swish_grads(scal, counts, stats, conv, cot, gain, shift)
    scaled_out[...] = scaled
    grad_out[...] = grad
    inv_out[...] = inv
    rows = conv.shape[0] - 2 * EDGE
    own = grad[EDGE : EDGE + rows]
    both = jnp.concatenate(
        [
            jnp.sum(own, axis=0, keepdims=True),
            jnp.sum(own * scaled[EDGE : EDGE + rows], axis=0, keepdims=True),
        ],
        axis=0,
    )
    for peer in range(sums.shape[0]):
        sums[peer] = both


def batch(scal, counts, stats, conv, cot, gain, shift, peers):
    span, half_width = conv.shape
    chunk = 256 if half_width % 256 == 0 else 128
    col = lambda n: pl.BlockSpec((n, chunk), lambda i: (0, i))
    smem = pl.BlockSpec(memory_space=pltpu.SMEM)
    return pl.pallas_call(
        batch_kernel,
        grid=(half_width // chunk,),
        in_specs=[
            smem,
            smem,
            pl.BlockSpec((stats.shape[0], 2, chunk), lambda i: (0, 0, i)),
            col(span),
            col(span),
            col(1),
            col(1),
        ],
        out_specs=[col(span), col(span), col(1), pl.BlockSpec((peers, 2, chunk), lambda i: (0, 0, i))],
        out_shape=[
            jax.ShapeDtypeStruct((span, half_width), F32),
            jax.ShapeDtypeStruct((span, half_width), F32),
            jax.ShapeDtypeStruct((1, half_width), F32),
            jax.ShapeDtypeStruct((peers, 2, half_width), F32),
        ],
        compiler_params=params(),
        cost_estimate=cost(40 * span * half_width, 16 * span * half_width),
        name="batch_norm_swish",
    )(scal, counts, stats, conv, cot, gain, shift)


def backward_kernel(scal, sums, scaled, grad, inv, gain, taps, value, gate, value_w, gate_w, mine, other, grad_conv, totals, plain, shifted, part):
    start, end, core = scal[0], scal[1], scal[2]
    rows, taps_n = value.shape[0], taps.shape[0]
    half = (taps_n - 1) // 2
    live_count = scal[3].astype(F32)
    both = sums[0]
    for peer in range(1, sums.shape[0]):
        both = both + sums[peer]
    totals[...] = both
    shift_sum, gain_sum = both[0:1], both[1:2]
    live = live_rows(start - EDGE, scaled.shape[0], end)
    through = live * (inv[...] * gain[...]) * (
        grad[...] - (shift_sum + scaled[...] * gain_sum) / live_count
    )
    rounded = through.astype(BF16)
    grad_conv[...] = rounded[EDGE : EDGE + rows]
    spread(plain, shifted, rounded.astype(F32))
    grad_glu = convolve(taps, shifted, [EDGE + half - tap for tap in range(taps_n)], rows, 16)
    grad_glu = (grad_glu * live_rows(start, rows, end)).astype(BF16).astype(F32)
    sig = gate[...]
    to_value = (grad_glu * sig).astype(BF16)
    to_gate = (grad_glu * value[...] * sig * (1.0 - sig)).astype(BF16)
    product = jnp.dot(to_value, value_w[...], preferred_element_type=F32) + jnp.dot(
        to_gate, gate_w[...], preferred_element_type=F32
    )
    step, last_step = pl.program_id(0), pl.num_programs(0) - 1

    @pl.when(step == 0)
    def _():
        part[...] = product

    @pl.when(step > 0)
    def _():
        part[...] += product

    @pl.when(step == last_step)
    def _():
        count = mine.shape[0]
        mine[...] = part[pl.ds(pl.multiple_of(core * count, count), count), :]
        other[...] = part[pl.ds(pl.multiple_of((1 - core) * count, count), count), :]


def backward(scal, sums, scaled, grad, inv, gain, taps, value, gate, weight):
    span, half_width = scaled.shape
    rows, width = value.shape[0], weight.shape[1]
    chunk = 256 if half_width % 256 == 0 else 128
    steps = half_width // chunk
    taps_n = taps.shape[0]
    col = lambda n: pl.BlockSpec((n, chunk), lambda i: (0, i))
    own = pl.BlockSpec((rows // 2, width), lambda i: (0, 0))
    return pl.pallas_call(
        backward_kernel,
        grid=(steps,),
        in_specs=[
            pl.BlockSpec(memory_space=pltpu.SMEM),
            pl.BlockSpec((sums.shape[0], 2, chunk), lambda i: (0, 0, i)),
            col(span),
            col(span),
            col(1),
            col(1),
            pl.BlockSpec((taps_n, 8, chunk), lambda i: (0, 0, i)),
            col(rows),
            col(rows),
            pl.BlockSpec((chunk, width), lambda i: (i, 0)),
            pl.BlockSpec((chunk, width), lambda i: (i + steps, 0)),
        ],
        out_specs=[own, own, col(rows), col(2)],
        out_shape=[
            jax.ShapeDtypeStruct((rows // 2, width), F32),
            jax.ShapeDtypeStruct((rows // 2, width), F32),
            jax.ShapeDtypeStruct((rows, half_width), BF16),
            jax.ShapeDtypeStruct((2, half_width), F32),
        ],
        scratch_shapes=[
            pltpu.VMEM((span, chunk), F32),
            pltpu.VMEM((8, span // 8 - 1, 8, chunk), F32),
            pltpu.VMEM((rows, width), F32),
        ],
        compiler_params=params(),
        cost_estimate=cost(2 * rows * width * 2 * half_width, 4 * half_width * width + 20 * span * half_width),
        name="grad_conv_project_back",
    )(scal, sums, scaled, grad, inv, gain, taps, value, gate, weight, weight)


def shifted_scratch(span):
    return [pltpu.VMEM((span, 128), F32), pltpu.VMEM((8, span // 8 - 1, 8, 128), F32)]


def tap_grad_kernel(taps_n, grad_conv, glu, out, plain, shifted):
    spread(plain, shifted, glu[...].astype(F32))
    first = HALO - (taps_n - 1) // 2
    out[...] = correlate(taps_n, grad_conv[...].astype(F32), shifted, first)


def tap_grad(taps_n, grad_conv, glu):
    rows, half_width = grad_conv.shape
    span = glu.shape[0]
    col = lambda n: pl.BlockSpec((n, 128), lambda i: (0, i))
    return pl.pallas_call(
        functools.partial(tap_grad_kernel, taps_n),
        grid=(half_width // 128,),
        in_specs=[col(rows), col(span)],
        out_specs=col(taps_n),
        out_shape=jax.ShapeDtypeStruct((taps_n, half_width), F32),
        scratch_shapes=shifted_scratch(span),
        compiler_params=params(),
        cost_estimate=cost(2 * taps_n * rows * half_width, 4 * span * half_width),
        name="tap_grad",
    )(grad_conv, glu)


def raw_taps_kernel(taps_n, scal, conv, glu, stats, alone, crossed, plain, shifted):
    start, end = scal[0], scal[1]
    rows, span = conv.shape[0] - 2 * EDGE, glu.shape[0]
    spread(plain, shifted, glu[...].astype(F32))
    first = HALO - (taps_n - 1) // 2
    live = live_rows(start, rows, end)
    local = stats[0, 0:1, :] / jnp.maximum(jnp.sum(live), 1.0)
    crossed[...] = correlate(taps_n, live * (conv[EDGE : EDGE + rows, :] - local), shifted, first)
    tap = lax.broadcasted_iota(jnp.int32, (taps_n, span), 0)
    at = lax.broadcasted_iota(jnp.int32, (taps_n, span), 1) - first - tap
    inside = (at >= 0) & (at < jnp.clip(end - start, 0, rows))
    alone[...] = jnp.dot(
        jnp.where(inside, 1.0, 0.0).astype(BF16), glu[...], preferred_element_type=F32
    )


def raw_taps(taps_n, scal, conv, glu, stats):
    rows, half_width = conv.shape
    span = glu.shape[0]
    col = lambda n: pl.BlockSpec((n, 128), lambda i: (0, i))
    return pl.pallas_call(
        functools.partial(raw_taps_kernel, taps_n),
        grid=(half_width // 128,),
        in_specs=[
            pl.BlockSpec(memory_space=pltpu.SMEM),
            col(rows),
            col(span),
            pl.BlockSpec((1, 2, 128), lambda i: (0, 0, i)),
        ],
        out_specs=[col(taps_n), col(taps_n)],
        out_shape=[jax.ShapeDtypeStruct((taps_n, half_width), F32)] * 2,
        scratch_shapes=shifted_scratch(span),
        compiler_params=params(),
        cost_estimate=cost(2 * taps_n * rows * half_width, 8 * span * half_width),
        name="raw_taps",
    )(scal, conv, glu, stats)


def halves(array):
    high = array.astype(BF16).astype(F32)
    return high, array - high


def last_kernel(taps_n, scal, counts, stats, conv, cot, gain, shift, glu, alone, crossed, local_stats, taps_before, out, factor_out, plain, shifted, pay):
    step = pl.program_id(0)
    scaled, grad, live, mean, inv = swish_grads(scal, counts, stats, conv, cot, gain, shift)
    rows = conv.shape[0] - 2 * EDGE
    spread(plain, shifted, glu[...].astype(F32))
    first = HALO - (taps_n - 1) // 2
    factor = inv * gain[...]
    factor_out[...] = factor
    own = grad[EDGE : EDGE + rows]
    direct = taps_before[...] + factor * correlate(taps_n, own, shifted, first)
    own_live = live[EDGE : EDGE + rows]
    local = local_stats[0, 0:1, :] / jnp.maximum(jnp.sum(own_live), 1.0)
    with_scaled = inv * (crossed[...] + (local - mean) * alone[...])
    sums = jnp.concatenate(
        [
            jnp.sum(own, axis=0, keepdims=True),
            jnp.sum(own * scaled[EDGE : EDGE + rows], axis=0, keepdims=True),
        ],
        axis=0,
    )
    pay[step] = jnp.concatenate([*halves(direct), with_scaled, alone[...], *halves(sums)], axis=0)

    @pl.when(step == pl.num_programs(0) - 1)
    def _():
        turned = jnp.concatenate([jnp.transpose(pay[s]) for s in range(pay.shape[0])], axis=0)
        block = out.shape[1]
        for index in range(out.shape[0]):
            out[index] = turned[index * block : (index + 1) * block].astype(BF16)


def last(taps_n, peers, scal, counts, stats, conv, cot, gain, shift, glu, alone, crossed, local_stats, taps_before):
    span, half_width = conv.shape
    chunk = 128
    steps = half_width // chunk
    pay = 4 * taps_n + 4
    col = lambda n: pl.BlockSpec((n, chunk), lambda i: (0, i))
    smem = pl.BlockSpec(memory_space=pltpu.SMEM)
    return pl.pallas_call(
        functools.partial(last_kernel, taps_n),
        grid=(steps,),
        in_specs=[
            smem,
            smem,
            pl.BlockSpec((stats.shape[0], 2, chunk), lambda i: (0, 0, i)),
            col(span),
            col(span),
            col(1),
            col(1),
            col(glu.shape[0]),
            col(taps_n),
            col(taps_n),
            pl.BlockSpec((1, 2, chunk), lambda i: (0, 0, i)),
            col(taps_n),
        ],
        out_specs=[pl.BlockSpec((peers, half_width // peers, pay), lambda i: (0, 0, 0)), col(1)],
        out_shape=[
            jax.ShapeDtypeStruct((peers, half_width // peers, pay), BF16),
            jax.ShapeDtypeStruct((1, half_width), F32),
        ],
        scratch_shapes=[*shifted_scratch(glu.shape[0]), pltpu.VMEM((steps, pay, chunk), F32)],
        compiler_params=params(),
        cost_estimate=cost(100 * span * half_width, 10 * span * half_width),
        name="batch_norm_swish_taps",
    )(scal, counts, stats, conv, cot, gain, shift, glu, alone, crossed, local_stats, taps_before)


def finish_kernel(taps_n, scal, received, known, taps_out, norm_out):
    total = received[0].astype(F32)
    for index in range(1, received.shape[0]):
        total = total + received[index].astype(F32)
    total = jnp.transpose(total)
    n = taps_n
    sums = total[4 * n : 4 * n + 2] + total[4 * n + 2 : 4 * n + 4]
    shift_sum, gain_sum = sums[0:1], sums[1:2]
    factor = known[0:1] / scal[3].astype(F32)
    taps_out[...] = (total[:n] + total[n : 2 * n]) - factor * (
        gain_sum * total[2 * n : 3 * n] + shift_sum * total[3 * n : 4 * n]
    )
    norm_out[...] = jnp.concatenate([gain_sum + known[2:3], shift_sum + known[1:2]], axis=0)


def finish(taps_n, scal, received, known):
    width = received.shape[1]
    vmem = pl.BlockSpec(memory_space=pltpu.VMEM)
    return pl.pallas_call(
        functools.partial(finish_kernel, taps_n),
        in_specs=[pl.BlockSpec(memory_space=pltpu.SMEM), vmem, vmem],
        out_shape=[
            jax.ShapeDtypeStruct((taps_n, width), F32),
            jax.ShapeDtypeStruct((2, width), F32),
        ],
        compiler_params=params(),
        name="finish",
    )(scal, received, known)


def direction_kernel(scal, mine, other, features, noise, out, edge, squares):
    rows = mine.shape[0]
    first = scal[0] + scal[2] * rows
    block = 32
    total = jnp.zeros((1, 128), F32)
    for row in range(0, rows, block):
        at = slice(row, row + block)
        live = live_rows(first + row, block, scal[1])
        summed = features[at].astype(F32) + noise_scale * noise[at].astype(F32) * live
        normed, inverse = normalize(summed)
        grad = mine[at] + other[at]
        moved = (
            live
            * inverse
            * (
                grad
                - jnp.mean(grad, axis=-1, keepdims=True)
                - normed * jnp.mean(grad * normed, axis=-1, keepdims=True)
            )
        )
        out[at] = moved
        total = total + jnp.sum(moved * moved)
    edge[...] = jnp.where(scal[2] == 0, out[:HALO], out[rows - HALO :])
    for peer in range(squares.shape[0]):
        squares[peer] = total


def direction(scal, mine, other, features, noise, peers):
    rows, width = mine.shape
    vmem = pl.BlockSpec(memory_space=pltpu.VMEM)
    return pl.pallas_call(
        direction_kernel,
        in_specs=[pl.BlockSpec(memory_space=pltpu.SMEM)] + [vmem] * 4,
        out_shape=[
            jax.ShapeDtypeStruct((rows, width), F32),
            jax.ShapeDtypeStruct((HALO, width), F32),
            jax.ShapeDtypeStruct((peers, 1, 128), F32),
        ],
        compiler_params=params(),
        cost_estimate=cost(30 * rows * width, 16 * rows * width),
        name="direction",
    )(scal, mine, other, features, noise)


def ascend_kernel(scal, squares, features, noise, mine, partner, near, far, own_noise, perturbation, normed_out):
    start, end, core = scal[0], scal[1], scal[2]
    rows, width = mine.shape
    total = squares[0]
    for index in range(1, squares.shape[0]):
        total = total + squares[index]
    total = total[0:1, 0:1]
    length = jnp.full((1, 1), 1.0, F32) * end.astype(F32)
    rate = ascent_rate * jnp.sqrt(length * width) / (jnp.sqrt(total) + ascent_epsilon)
    block = 32
    is_first = core == 0

    def place(row, moved):
        at = slice(row, row + block)
        live = live_rows(start - HALO + row, block, end)
        summed = features[at].astype(F32) + (noise_scale * noise[at].astype(F32) * live + moved * rate)
        normed_out[at] = normalize(summed)[0].astype(BF16)

    place(0, jnp.where(is_first, far[...], near[...]))
    for row in range(0, rows, block):
        at = slice(row, row + block)
        place(HALO + row, jnp.where(is_first, mine[at], partner[at]))
        place(HALO + rows + row, jnp.where(is_first, partner[at], mine[at]))
        live = live_rows(start + core * rows + row, block, end)
        perturbation[at] = noise_scale * own_noise[at].astype(F32) * live + mine[at] * rate
    place(HALO + 2 * rows, jnp.where(is_first, near[...], far[...]))


def ascend(scal, squares, features, noise, mine, partner, near, far, own_noise):
    vmem = pl.BlockSpec(memory_space=pltpu.VMEM)
    return pl.pallas_call(
        ascend_kernel,
        in_specs=[pl.BlockSpec(memory_space=pltpu.SMEM)] + [vmem] * 8,
        out_shape=[
            jax.ShapeDtypeStruct(mine.shape, F32),
            jax.ShapeDtypeStruct(features.shape, BF16),
        ],
        compiler_params=params(),
        cost_estimate=cost(30 * features.size, 8 * features.size),
        name="ascend",
    )(scal, squares, features, noise, mine, partner, near, far, own_noise)


def on_device(on_dp, features, start_noise, cotangent, in_weight, kernel, bn_gain, bn_shift, ends):
    rows, width = features.shape[1:]
    taps_n = kernel.shape[0]
    shards = lax.axis_size("tm")
    chips = shards // 2
    index = lax.axis_index("tm")
    group = lax.axis_index("dp")
    chip, core = index // 2, index % 2
    chip_rows = 2 * rows
    half_width = width // 2
    end = lax.dynamic_index_in_dim(ends, group, 0, keepdims=False)
    scal = jnp.stack([chip * chip_rows, end, core, jnp.sum(ends), chip % 4, chip // 4]).astype(jnp.int32)
    held = jnp.clip(
        ends[:, None] - chip_rows * jnp.arange(chips, dtype=jnp.int32)[None, :], 0, chip_rows
    ).reshape(-1).astype(F32)
    counts = jnp.stack([held, jnp.where(held > 0, 1.0 / jnp.maximum(held, 1.0), 0.0)])

    cores = [[2 * c + k for c in range(chips)] for k in range(2)]
    depth = chips // 4
    swap = [(i, i ^ 1) for i in range(shards)]
    swap_x = [(i, i ^ 2) for i in range(shards)]
    swap_y = [(i, i ^ 4) for i in range(shards)]
    near_pairs = [(2 * c, 2 * c - 2) for c in range(1, chips)] + [
        (2 * c + 1, 2 * c + 3) for c in range(chips - 1)
    ]
    far_pairs = [(2 * c, 2 * c - 1) for c in range(1, chips)] + [
        (2 * c + 1, 2 * c + 2) for c in range(chips - 1)
    ]
    first = core == 0

    def across(array, edge):
        return (
            lax.ppermute(array, "tm", swap),
            lax.ppermute(edge, "tm", near_pairs),
            lax.ppermute(edge, "tm", far_pairs),
        )

    def peers_of(array):
        array = lax.all_to_all(array, "tm", 0, 0, axis_index_groups=cores, tiled=True)
        if on_dp:
            array = lax.all_gather(array, "dp", axis=0, tiled=True)
        return array

    slice_width = width // shards
    pair = in_weight.reshape(2, slice_width, width)
    kept = lax.dynamic_index_in_dim(pair, core, 0, keepdims=False)
    given = lax.ppermute(lax.dynamic_index_in_dim(pair, 1 - core, 0, keepdims=False), "tm", swap)
    block = jnp.concatenate([jnp.where(first, kept, given), jnp.where(first, given, kept)], axis=0)
    shifts = [(0,)] + [(k, depth - k) if 2 * k < depth else (k,) for k in range(1, depth // 2 + 1)]
    along = {0: block}
    for k in [k for group in shifts[1:] for k in group]:
        along[k] = lax.ppermute(block, "tm", [(i, (i + 8 * k) % shards) for i in range(shards)])
    pieces = []
    for group in shifts:
        blocks = jnp.concatenate([along[k] for k in group], axis=0)
        cut = (blocks.shape[0] // 2 + 15) // 16 * 16
        from_x = lax.ppermute(blocks, "tm", swap_x)
        from_y = lax.ppermute(blocks, "tm", swap_y)
        pieces += [
            blocks,
            from_x,
            from_y,
            lax.ppermute(from_y[:cut], "tm", swap_x),
            lax.ppermute(from_x[cut:], "tm", swap_y),
        ]
    weight = place(scal, pieces, shifts, block.shape[0])

    features, start_noise, cotangent, kernel, bn_gain, bn_shift, _ = lax.optimization_barrier(
        (features, start_noise, cotangent, kernel, bn_gain, bn_shift, pieces[5])
    )
    packed = jnp.concatenate([features, start_noise, cotangent], axis=0)
    partner, near, far = across(
        packed, jnp.where(first, packed[:, :HALO], packed[:, rows - HALO :])
    )
    whole = jnp.concatenate(
        [
            jnp.where(first, far, near),
            jnp.where(first, packed, partner),
            jnp.where(first, partner, packed),
            jnp.where(first, near, far),
        ],
        axis=1,
    )
    wide_features, wide_noise, wide_cot = whole[0], whole[1], whole[2]

    place_of = jnp.arange(half_width, dtype=jnp.int32)
    source = (2 * (place_of // slice_width) + core) * slice_width + place_of % slice_width
    chosen = (jnp.arange(width, dtype=jnp.int32)[:, None] == source[None, :]).astype(BF16)
    cot = jnp.dot(wide_cot[HALO - EDGE : -(HALO - EDGE)], chosen, preferred_element_type=F32).astype(BF16)

    def mine_of(array):
        parts = array.reshape(array.shape[0], chips, 2, slice_width)
        return lax.dynamic_index_in_dim(parts, core, 2, keepdims=False).reshape(-1, half_width)

    channel = mine_of(jnp.concatenate([kernel, bn_gain[None], bn_shift[None]], axis=0))
    gain, shift = channel[taps_n : taps_n + 1], channel[taps_n + 1 :]
    taps = jnp.broadcast_to(channel[:taps_n, None], (taps_n, 8, half_width))

    frame_ids = chip * chip_rows - HALO + jnp.arange(whole.shape[1], dtype=jnp.int32)
    live = ((frame_ids >= 0) & (frame_ids < end)).astype(F32)
    summed = wide_features.astype(F32) + noise_scale * wide_noise.astype(F32) * live[:, None]
    normed_b = normalize(summed)[0].astype(BF16)

    value, gate, glu, conv, stats = forward(
        scal, normed_b, weight, taps, chip_rows, chips, True
    )
    scaled, grad, inv, sums = batch(scal, counts, peers_of(stats), conv, cot, gain, shift, chips)
    mine, other, grad_conv, totals = backward(
        scal, peers_of(sums), scaled, grad, inv, gain, taps, value, gate, weight
    )
    other = lax.ppermute(other, "tm", swap)
    moved, edge, squares = direction(scal, mine, other, features[0], start_noise[0], shards)
    squares = lax.all_to_all(squares, "tm", 0, 0, tiled=True)
    partner, near, far = across(moved, edge)
    taps_before = tap_grad(taps_n, grad_conv, glu)
    squares, taps_before = lax.optimization_barrier((squares, taps_before))
    perturbation, normed_b = ascend(
        scal, squares, wide_features, wide_noise, moved, partner, near, far, start_noise[0]
    )

    glu, conv, stats = forward(scal, normed_b, weight, taps, chip_rows, chips, False)
    alone, crossed = raw_taps(taps_n, scal, conv, glu, stats)
    outgoing, factor = last(
        taps_n, chips, scal, counts, peers_of(stats), conv, cot, gain, shift, glu, alone, crossed, stats, taps_before
    )
    received = peers_of(outgoing)
    known = jnp.concatenate([factor, totals], axis=0)
    known = lax.dynamic_slice_in_dim(known, chip * slice_width, slice_width, 1)
    kernel_total, norm_total = finish(taps_n, scal, received, known)
    return (perturbation[None], kernel_total, norm_total)


def solution(mesh):
    return jax.shard_map(
        functools.partial(on_device, mesh.shape["dp"] > 1),
        mesh=mesh,
        in_specs=(
            P("dp", "tm", None),
            P("dp", "tm", None),
            P("dp", "tm", None),
            P("tm", None),
            P(),
            P(),
            P(),
            P(),
        ),
        out_specs=(P("dp", "tm", None), P(None, "tm"), P(None, "tm")),
        check_vma=False,
    )
```

```python
import functools

import jax
import jax.numpy as jnp
from jax import lax
from jax.experimental import pallas as pl
from jax.experimental.pallas import tpu as pltpu
from jax.sharding import PartitionSpec as P

ASCENT = 2

noise_scale = 0.5
ascent_rate = 0.5
layer_epsilon = 1e-05
batch_epsilon = 1e-05
ascent_epsilon = 1e-06

HALO = 32
EDGE = 16
F32 = jnp.float32
BF16 = jnp.bfloat16


def params(limit=56 * 1024 * 1024):
    return pltpu.CompilerParams(vmem_limit_bytes=limit)


def cost(flops, nbytes):
    return pl.CostEstimate(flops=int(flops), bytes_accessed=int(nbytes), transcendentals=0)


def normalize(summed):
    centre = summed - jnp.mean(summed, axis=-1, keepdims=True)
    inverse = lax.rsqrt(jnp.mean(centre * centre, axis=-1, keepdims=True) + layer_epsilon)
    return (centre * inverse, inverse)


def live_rows(first, rows, end):
    ids = first + lax.broadcasted_iota(jnp.int32, (rows, 1), 0)
    return jnp.where((ids >= 0) & (ids < end), 1.0, 0.0).astype(F32)


def spread(plain, shifted, array):
    plain[...] = array
    rows, tiles = shifted.shape[1] * 8, shifted.shape[1]
    for s in range(8):
        shifted[s] = plain[s : s + rows].reshape(tiles, 8, -1)


def tiles_at(shifted, row, tiles, lanes):
    first = (row - row % 8) // 8
    return shifted[row % 8, first : first + tiles, :, lanes]


def convolve(taps, shifted, offsets, rows, most):
    most = max(n for n in range(1, most + 1) if rows // 8 % n == 0)
    columns = []
    for lane in range(0, taps.shape[2], 128):
        lanes = slice(lane, lane + 128)
        parts = []
        for tile in range(0, rows // 8, most):
            total = jnp.zeros((most, 8, 128), F32)
            for tap, offset in enumerate(offsets):
                total = total + taps[tap, :, lanes][None] * tiles_at(
                    shifted, offset + 8 * tile, most, lanes
                )
            parts.append(total.reshape(most * 8, 128))
        columns.append(jnp.concatenate(parts, axis=0))
    return jnp.concatenate(columns, axis=1)


def correlate(taps_n, left, shifted, first):
    rows = left.shape[0]
    lanes = slice(0, 128)
    most = 16
    totals = [None] * taps_n
    for tile in range(0, rows // 8, most):
        part = left[8 * tile : 8 * (tile + most)].reshape(most, 8, 128)
        for tap in range(taps_n):
            product = jnp.sum(
                part * tiles_at(shifted, first + tap + 8 * tile, most, lanes), axis=0, keepdims=True
            )
            totals[tap] = product if totals[tap] is None else totals[tap] + product
    return jnp.sum(jnp.concatenate(totals, axis=0), axis=1)


def place_kernel(shifts, size, scal, *refs):
    pieces, out = refs[:-1], refs[-1]
    spot, layer = scal[4], scal[5]
    depth = out.shape[0] // (4 * size)

    for number, group in enumerate(shifts):
        for other, ref in enumerate(pieces[4 * number : 4 * number + 4]):
            for nth, shift in enumerate(group):
                chip = lax.rem(layer - shift + depth, depth) * 4 + (spot ^ other)
                row = pl.multiple_of(chip * size, 16)
                out[pl.ds(row, size), :] = ref[nth * size : (nth + 1) * size, :]


def place(scal, pieces, shifts, size):
    width = pieces[0].shape[1]
    chips = 4 * sum(len(group) for group in shifts)
    vmem = pl.BlockSpec(memory_space=pltpu.VMEM)
    return pl.pallas_call(
        functools.partial(place_kernel, shifts, size),
        in_specs=[pl.BlockSpec(memory_space=pltpu.SMEM)] + [vmem] * len(pieces),
        out_specs=vmem,
        out_shape=jax.ShapeDtypeStruct((chips * size, width), BF16),
        compiler_params=params(),
        cost_estimate=cost(0, 4 * chips * size * width),
        name="place_weights",
    )(scal, *pieces)


def forward_kernel(keep, scal, nb, value_w, gate_w, taps, *refs):
    kept, (glu, conv, stats, plain, shifted) = refs[: 2 * keep], refs[2 * keep :]
    start, end = scal[0], scal[1]
    span, taps_n = nb.shape[0], taps.shape[0]
    rows = conv.shape[0] - 2 * EDGE
    contract = (((1,), (1,)), ((), ()))
    v = lax.dot_general(nb[...], value_w[...], contract, preferred_element_type=F32)
    s = jax.nn.sigmoid(lax.dot_general(nb[...], gate_w[...], contract, preferred_element_type=F32))
    if keep:
        kept[0][...] = v[HALO : HALO + rows]
        kept[1][...] = s[HALO : HALO + rows]
    gated = (v * s * live_rows(start - HALO, span, end)).astype(BF16)
    glu[...] = gated
    spread(plain, shifted, gated.astype(F32))
    shift = HALO - EDGE - (taps_n - 1) // 2
    conv[...] = convolve(taps, shifted, [shift + tap for tap in range(taps_n)], conv.shape[0], 12)
    live = live_rows(start, rows, end)
    own = conv[EDGE : EDGE + rows, :]
    mass = jnp.sum(live * own, axis=0, keepdims=True)
    centre = live * (own - mass / jnp.maximum(jnp.sum(live), 1.0))
    both = jnp.concatenate([mass, jnp.sum(centre * centre, axis=0, keepdims=True)], axis=0)
    for peer in range(stats.shape[0]):
        stats[peer] = both


def forward(scal, nb, weight, taps, rows, peers, keep):
    span, width = nb.shape
    taps_n, _, half_width = taps.shape
    chunk = 256 if half_width % 256 == 0 else 128
    steps = half_width // chunk
    col = lambda n: pl.BlockSpec((n, chunk), lambda i: (0, i))
    return pl.pallas_call(
        functools.partial(forward_kernel, keep),
        grid=(steps,),
        in_specs=[
            pl.BlockSpec(memory_space=pltpu.SMEM),
            pl.BlockSpec((span, width), lambda i: (0, 0)),
            pl.BlockSpec((chunk, width), lambda i: (i, 0)),
            pl.BlockSpec((chunk, width), lambda i: (i + steps, 0)),
            pl.BlockSpec((taps_n, 8, chunk), lambda i: (0, 0, i)),
        ],
        out_specs=[
            *([col(rows)] * (2 * keep)),
            col(span),
            col(rows + 2 * EDGE),
            pl.BlockSpec((peers, 2, chunk), lambda i: (0, 0, i)),
        ],
        out_shape=[
            *([jax.ShapeDtypeStruct((rows, half_width), F32)] * (2 * keep)),
            jax.ShapeDtypeStruct((span, half_width), BF16),
            jax.ShapeDtypeStruct((rows + 2 * EDGE, half_width), F32),
            jax.ShapeDtypeStruct((peers, 2, half_width), F32),
        ],
        scratch_shapes=[
            pltpu.VMEM((span, chunk), F32),
            pltpu.VMEM((8, span // 8 - 1, 8, chunk), F32),
        ],
        compiler_params=params(),
        cost_estimate=cost(2 * span * width * 2 * half_width, 4 * half_width * width + 10 * span * half_width),
        name="project_glu_conv",
    )(scal, nb, weight, weight, taps)


def moments(counts, stats, live_count):
    mass = stats[0, 0:1, :]
    square = stats[0, 1:2, :]
    for peer in range(1, stats.shape[0]):
        mass = mass + stats[peer, 0:1, :]
        square = square + stats[peer, 1:2, :]
    mean = mass / live_count
    for peer in range(stats.shape[0]):
        off = stats[peer, 0:1, :] - counts[0, peer] * mean
        square = square + off * off * counts[1, peer]
    return mean, lax.rsqrt(square / live_count + batch_epsilon)


def swish_grads(scal, counts, stats, conv, cot, gain, shift):
    start, end = scal[0], scal[1]
    live_count = scal[3].astype(F32)
    mean, inv = moments(counts, stats, live_count)
    scaled = (conv[...] - mean) * inv
    pre = gain[...] * scaled + shift[...]
    sig = jax.nn.sigmoid(pre)
    live = live_rows(start - EDGE, conv.shape[0], end)
    upstream = live * cot[...].astype(F32) / ASCENT
    return scaled, upstream * sig * (1.0 + pre * (1.0 - sig)), live, mean, inv


def batch_kernel(scal, counts, stats, conv, cot, gain, shift, scaled_out, grad_out, inv_out, sums):
    scaled, grad, live, mean, inv = swish_grads(scal, counts, stats, conv, cot, gain, shift)
    scaled_out[...] = scaled
    grad_out[...] = grad
    inv_out[...] = inv
    rows = conv.shape[0] - 2 * EDGE
    own = grad[EDGE : EDGE + rows]
    both = jnp.concatenate(
        [
            jnp.sum(own, axis=0, keepdims=True),
            jnp.sum(own * scaled[EDGE : EDGE + rows], axis=0, keepdims=True),
        ],
        axis=0,
    )
    for peer in range(sums.shape[0]):
        sums[peer] = both


def batch(scal, counts, stats, conv, cot, gain, shift, peers):
    span, half_width = conv.shape
    chunk = 256 if half_width % 256 == 0 else 128
    col = lambda n: pl.BlockSpec((n, chunk), lambda i: (0, i))
    smem = pl.BlockSpec(memory_space=pltpu.SMEM)
    return pl.pallas_call(
        batch_kernel,
        grid=(half_width // chunk,),
        in_specs=[
            smem,
            smem,
            pl.BlockSpec((stats.shape[0], 2, chunk), lambda i: (0, 0, i)),
            col(span),
            col(span),
            col(1),
            col(1),
        ],
        out_specs=[col(span), col(span), col(1), pl.BlockSpec((peers, 2, chunk), lambda i: (0, 0, i))],
        out_shape=[
            jax.ShapeDtypeStruct((span, half_width), F32),
            jax.ShapeDtypeStruct((span, half_width), F32),
            jax.ShapeDtypeStruct((1, half_width), F32),
            jax.ShapeDtypeStruct((peers, 2, half_width), F32),
        ],
        compiler_params=params(),
        cost_estimate=cost(40 * span * half_width, 16 * span * half_width),
        name="batch_norm_swish",
    )(scal, counts, stats, conv, cot, gain, shift)


def backward_kernel(scal, sums, scaled, grad, inv, gain, taps, value, gate, value_w, gate_w, mine, other, grad_conv, totals, plain, shifted, part):
    start, end, core = scal[0], scal[1], scal[2]
    rows, taps_n = value.shape[0], taps.shape[0]
    half = (taps_n - 1) // 2
    live_count = scal[3].astype(F32)
    both = sums[0]
    for peer in range(1, sums.shape[0]):
        both = both + sums[peer]
    totals[...] = both
    shift_sum, gain_sum = both[0:1], both[1:2]
    live = live_rows(start - EDGE, scaled.shape[0], end)
    through = live * (inv[...] * gain[...]) * (
        grad[...] - (shift_sum + scaled[...] * gain_sum) / live_count
    )
    rounded = through.astype(BF16)
    grad_conv[...] = rounded[EDGE : EDGE + rows]
    spread(plain, shifted, rounded.astype(F32))
    grad_glu = convolve(taps, shifted, [EDGE + half - tap for tap in range(taps_n)], rows, 16)
    grad_glu = (grad_glu * live_rows(start, rows, end)).astype(BF16).astype(F32)
    sig = gate[...]
    to_value = (grad_glu * sig).astype(BF16)
    to_gate = (grad_glu * value[...] * sig * (1.0 - sig)).astype(BF16)
    product = jnp.dot(to_value, value_w[...], preferred_element_type=F32) + jnp.dot(
        to_gate, gate_w[...], preferred_element_type=F32
    )
    step, last_step = pl.program_id(0), pl.num_programs(0) - 1

    @pl.when(step == 0)
    def _():
        part[...] = product

    @pl.when(step > 0)
    def _():
        part[...] += product

    @pl.when(step == last_step)
    def _():
        count = mine.shape[0]
        mine[...] = part[pl.ds(pl.multiple_of(core * count, count), count), :]
        other[...] = part[pl.ds(pl.multiple_of((1 - core) * count, count), count), :]


def backward(scal, sums, scaled, grad, inv, gain, taps, value, gate, weight):
    span, half_width = scaled.shape
    rows, width = value.shape[0], weight.shape[1]
    chunk = 256 if half_width % 256 == 0 else 128
    steps = half_width // chunk
    taps_n = taps.shape[0]
    col = lambda n: pl.BlockSpec((n, chunk), lambda i: (0, i))
    own = pl.BlockSpec((rows // 2, width), lambda i: (0, 0))
    return pl.pallas_call(
        backward_kernel,
        grid=(steps,),
        in_specs=[
            pl.BlockSpec(memory_space=pltpu.SMEM),
            pl.BlockSpec((sums.shape[0], 2, chunk), lambda i: (0, 0, i)),
            col(span),
            col(span),
            col(1),
            col(1),
            pl.BlockSpec((taps_n, 8, chunk), lambda i: (0, 0, i)),
            col(rows),
            col(rows),
            pl.BlockSpec((chunk, width), lambda i: (i, 0)),
            pl.BlockSpec((chunk, width), lambda i: (i + steps, 0)),
        ],
        out_specs=[own, own, col(rows), col(2)],
        out_shape=[
            jax.ShapeDtypeStruct((rows // 2, width), F32),
            jax.ShapeDtypeStruct((rows // 2, width), F32),
            jax.ShapeDtypeStruct((rows, half_width), BF16),
            jax.ShapeDtypeStruct((2, half_width), F32),
        ],
        scratch_shapes=[
            pltpu.VMEM((span, chunk), F32),
            pltpu.VMEM((8, span // 8 - 1, 8, chunk), F32),
            pltpu.VMEM((rows, width), F32),
        ],
        compiler_params=params(),
        cost_estimate=cost(2 * rows * width * 2 * half_width, 4 * half_width * width + 20 * span * half_width),
        name="grad_conv_project_back",
    )(scal, sums, scaled, grad, inv, gain, taps, value, gate, weight, weight)


def shifted_scratch(span):
    return [pltpu.VMEM((span, 128), F32), pltpu.VMEM((8, span // 8 - 1, 8, 128), F32)]


def tap_grad_kernel(taps_n, grad_conv, glu, out, plain, shifted):
    spread(plain, shifted, glu[...].astype(F32))
    first = HALO - (taps_n - 1) // 2
    out[...] = correlate(taps_n, grad_conv[...].astype(F32), shifted, first)


def tap_grad(taps_n, grad_conv, glu):
    rows, half_width = grad_conv.shape
    span = glu.shape[0]
    col = lambda n: pl.BlockSpec((n, 128), lambda i: (0, i))
    return pl.pallas_call(
        functools.partial(tap_grad_kernel, taps_n),
        grid=(half_width // 128,),
        in_specs=[col(rows), col(span)],
        out_specs=col(taps_n),
        out_shape=jax.ShapeDtypeStruct((taps_n, half_width), F32),
        scratch_shapes=shifted_scratch(span),
        compiler_params=params(),
        cost_estimate=cost(2 * taps_n * rows * half_width, 4 * span * half_width),
        name="tap_grad",
    )(grad_conv, glu)


def raw_taps_kernel(taps_n, scal, conv, glu, stats, alone, crossed, plain, shifted):
    start, end = scal[0], scal[1]
    rows, span = conv.shape[0] - 2 * EDGE, glu.shape[0]
    spread(plain, shifted, glu[...].astype(F32))
    first = HALO - (taps_n - 1) // 2
    live = live_rows(start, rows, end)
    local = stats[0, 0:1, :] / jnp.maximum(jnp.sum(live), 1.0)
    crossed[...] = correlate(taps_n, live * (conv[EDGE : EDGE + rows, :] - local), shifted, first)
    tap = lax.broadcasted_iota(jnp.int32, (taps_n, span), 0)
    at = lax.broadcasted_iota(jnp.int32, (taps_n, span), 1) - first - tap
    inside = (at >= 0) & (at < jnp.clip(end - start, 0, rows))
    alone[...] = jnp.dot(
        jnp.where(inside, 1.0, 0.0).astype(BF16), glu[...], preferred_element_type=F32
    )


def raw_taps(taps_n, scal, conv, glu, stats):
    rows, half_width = conv.shape
    span = glu.shape[0]
    col = lambda n: pl.BlockSpec((n, 128), lambda i: (0, i))
    return pl.pallas_call(
        functools.partial(raw_taps_kernel, taps_n),
        grid=(half_width // 128,),
        in_specs=[
            pl.BlockSpec(memory_space=pltpu.SMEM),
            col(rows),
            col(span),
            pl.BlockSpec((1, 2, 128), lambda i: (0, 0, i)),
        ],
        out_specs=[col(taps_n), col(taps_n)],
        out_shape=[jax.ShapeDtypeStruct((taps_n, half_width), F32)] * 2,
        scratch_shapes=shifted_scratch(span),
        compiler_params=params(),
        cost_estimate=cost(2 * taps_n * rows * half_width, 8 * span * half_width),
        name="raw_taps",
    )(scal, conv, glu, stats)


def halves(array):
    high = array.astype(BF16).astype(F32)
    return high, array - high


def last_kernel(taps_n, scal, counts, stats, conv, cot, gain, shift, glu, alone, crossed, local_stats, taps_before, out, factor_out, plain, shifted, pay):
    step = pl.program_id(0)
    scaled, grad, live, mean, inv = swish_grads(scal, counts, stats, conv, cot, gain, shift)
    rows = conv.shape[0] - 2 * EDGE
    spread(plain, shifted, glu[...].astype(F32))
    first = HALO - (taps_n - 1) // 2
    factor = inv * gain[...]
    factor_out[...] = factor
    own = grad[EDGE : EDGE + rows]
    direct = taps_before[...] + factor * correlate(taps_n, own, shifted, first)
    own_live = live[EDGE : EDGE + rows]
    local = local_stats[0, 0:1, :] / jnp.maximum(jnp.sum(own_live), 1.0)
    with_scaled = inv * (crossed[...] + (local - mean) * alone[...])
    sums = jnp.concatenate(
        [
            jnp.sum(own, axis=0, keepdims=True),
            jnp.sum(own * scaled[EDGE : EDGE + rows], axis=0, keepdims=True),
        ],
        axis=0,
    )
    pay[step] = jnp.concatenate([*halves(direct), with_scaled, alone[...], *halves(sums)], axis=0)

    @pl.when(step == pl.num_programs(0) - 1)
    def _():
        turned = jnp.concatenate([jnp.transpose(pay[s]) for s in range(pay.shape[0])], axis=0)
        block = out.shape[1]
        for index in range(out.shape[0]):
            out[index] = turned[index * block : (index + 1) * block].astype(BF16)


def last(taps_n, peers, scal, counts, stats, conv, cot, gain, shift, glu, alone, crossed, local_stats, taps_before):
    span, half_width = conv.shape
    chunk = 128
    steps = half_width // chunk
    pay = 4 * taps_n + 4
    col = lambda n: pl.BlockSpec((n, chunk), lambda i: (0, i))
    smem = pl.BlockSpec(memory_space=pltpu.SMEM)
    return pl.pallas_call(
        functools.partial(last_kernel, taps_n),
        grid=(steps,),
        in_specs=[
            smem,
            smem,
            pl.BlockSpec((stats.shape[0], 2, chunk), lambda i: (0, 0, i)),
            col(span),
            col(span),
            col(1),
            col(1),
            col(glu.shape[0]),
            col(taps_n),
            col(taps_n),
            pl.BlockSpec((1, 2, chunk), lambda i: (0, 0, i)),
            col(taps_n),
        ],
        out_specs=[pl.BlockSpec((peers, half_width // peers, pay), lambda i: (0, 0, 0)), col(1)],
        out_shape=[
            jax.ShapeDtypeStruct((peers, half_width // peers, pay), BF16),
            jax.ShapeDtypeStruct((1, half_width), F32),
        ],
        scratch_shapes=[*shifted_scratch(glu.shape[0]), pltpu.VMEM((steps, pay, chunk), F32)],
        compiler_params=params(),
        cost_estimate=cost(100 * span * half_width, 10 * span * half_width),
        name="batch_norm_swish_taps",
    )(scal, counts, stats, conv, cot, gain, shift, glu, alone, crossed, local_stats, taps_before)


def finish_kernel(taps_n, scal, received, known, taps_out, norm_out):
    total = received[0].astype(F32)
    for index in range(1, received.shape[0]):
        total = total + received[index].astype(F32)
    total = jnp.transpose(total)
    n = taps_n
    sums = total[4 * n : 4 * n + 2] + total[4 * n + 2 : 4 * n + 4]
    shift_sum, gain_sum = sums[0:1], sums[1:2]
    factor = known[0:1] / scal[3].astype(F32)
    taps_out[...] = (total[:n] + total[n : 2 * n]) - factor * (
        gain_sum * total[2 * n : 3 * n] + shift_sum * total[3 * n : 4 * n]
    )
    norm_out[...] = jnp.concatenate([gain_sum + known[2:3], shift_sum + known[1:2]], axis=0)


def finish(taps_n, scal, received, known):
    width = received.shape[1]
    vmem = pl.BlockSpec(memory_space=pltpu.VMEM)
    return pl.pallas_call(
        functools.partial(finish_kernel, taps_n),
        in_specs=[pl.BlockSpec(memory_space=pltpu.SMEM), vmem, vmem],
        out_shape=[
            jax.ShapeDtypeStruct((taps_n, width), F32),
            jax.ShapeDtypeStruct((2, width), F32),
        ],
        compiler_params=params(),
        name="finish",
    )(scal, received, known)


def direction_kernel(scal, mine, other, features, noise, out, edge, squares):
    rows = mine.shape[0]
    first = scal[0] + scal[2] * rows
    block = 32
    total = jnp.zeros((1, 128), F32)
    for row in range(0, rows, block):
        at = slice(row, row + block)
        live = live_rows(first + row, block, scal[1])
        summed = features[at].astype(F32) + noise_scale * noise[at].astype(F32) * live
        normed, inverse = normalize(summed)
        grad = mine[at] + other[at]
        moved = (
            live
            * inverse
            * (
                grad
                - jnp.mean(grad, axis=-1, keepdims=True)
                - normed * jnp.mean(grad * normed, axis=-1, keepdims=True)
            )
        )
        out[at] = moved
        total = total + jnp.sum(moved * moved)
    edge[...] = jnp.where(scal[2] == 0, out[:HALO], out[rows - HALO :])
    for peer in range(squares.shape[0]):
        squares[peer] = total


def direction(scal, mine, other, features, noise, peers):
    rows, width = mine.shape
    vmem = pl.BlockSpec(memory_space=pltpu.VMEM)
    return pl.pallas_call(
        direction_kernel,
        in_specs=[pl.BlockSpec(memory_space=pltpu.SMEM)] + [vmem] * 4,
        out_shape=[
            jax.ShapeDtypeStruct((rows, width), F32),
            jax.ShapeDtypeStruct((HALO, width), F32),
            jax.ShapeDtypeStruct((peers, 1, 128), F32),
        ],
        compiler_params=params(),
        cost_estimate=cost(30 * rows * width, 16 * rows * width),
        name="direction",
    )(scal, mine, other, features, noise)


def ascend_kernel(scal, squares, features, noise, mine, partner, near, far, own_noise, perturbation, normed_out):
    start, end, core = scal[0], scal[1], scal[2]
    rows, width = mine.shape
    total = squares[0]
    for index in range(1, squares.shape[0]):
        total = total + squares[index]
    total = total[0:1, 0:1]
    length = jnp.full((1, 1), 1.0, F32) * end.astype(F32)
    rate = ascent_rate * jnp.sqrt(length * width) / (jnp.sqrt(total) + ascent_epsilon)
    block = 32
    is_first = core == 0

    def place(row, moved):
        at = slice(row, row + block)
        live = live_rows(start - HALO + row, block, end)
        summed = features[at].astype(F32) + (noise_scale * noise[at].astype(F32) * live + moved * rate)
        normed_out[at] = normalize(summed)[0].astype(BF16)

    place(0, jnp.where(is_first, far[...], near[...]))
    for row in range(0, rows, block):
        at = slice(row, row + block)
        place(HALO + row, jnp.where(is_first, mine[at], partner[at]))
        place(HALO + rows + row, jnp.where(is_first, partner[at], mine[at]))
        live = live_rows(start + core * rows + row, block, end)
        perturbation[at] = noise_scale * own_noise[at].astype(F32) * live + mine[at] * rate
    place(HALO + 2 * rows, jnp.where(is_first, near[...], far[...]))


def ascend(scal, squares, features, noise, mine, partner, near, far, own_noise):
    vmem = pl.BlockSpec(memory_space=pltpu.VMEM)
    return pl.pallas_call(
        ascend_kernel,
        in_specs=[pl.BlockSpec(memory_space=pltpu.SMEM)] + [vmem] * 8,
        out_shape=[
            jax.ShapeDtypeStruct(mine.shape, F32),
            jax.ShapeDtypeStruct(features.shape, BF16),
        ],
        compiler_params=params(),
        cost_estimate=cost(30 * features.size, 8 * features.size),
        name="ascend",
    )(scal, squares, features, noise, mine, partner, near, far, own_noise)


def on_device(on_dp, features, start_noise, cotangent, in_weight, kernel, bn_gain, bn_shift, ends):
    rows, width = features.shape[1:]
    taps_n = kernel.shape[0]
    shards = lax.axis_size("tm")
    chips = shards // 2
    index = lax.axis_index("tm")
    group = lax.axis_index("dp")
    chip, core = index // 2, index % 2
    chip_rows = 2 * rows
    half_width = width // 2
    end = lax.dynamic_index_in_dim(ends, group, 0, keepdims=False)
    scal = jnp.stack([chip * chip_rows, end, core, jnp.sum(ends), chip % 4, chip // 4]).astype(jnp.int32)
    held = jnp.clip(
        ends[:, None] - chip_rows * jnp.arange(chips, dtype=jnp.int32)[None, :], 0, chip_rows
    ).reshape(-1).astype(F32)
    counts = jnp.stack([held, jnp.where(held > 0, 1.0 / jnp.maximum(held, 1.0), 0.0)])

    cores = [[2 * c + k for c in range(chips)] for k in range(2)]
    depth = chips // 4
    swap = [(i, i ^ 1) for i in range(shards)]
    swap_x = [(i, i ^ 2) for i in range(shards)]
    swap_y = [(i, i ^ 4) for i in range(shards)]
    near_pairs = [(2 * c, 2 * c - 2) for c in range(1, chips)] + [
        (2 * c + 1, 2 * c + 3) for c in range(chips - 1)
    ]
    far_pairs = [(2 * c, 2 * c - 1) for c in range(1, chips)] + [
        (2 * c + 1, 2 * c + 2) for c in range(chips - 1)
    ]
    first = core == 0

    def across(array, edge):
        return (
            lax.ppermute(array, "tm", swap),
            lax.ppermute(edge, "tm", near_pairs),
            lax.ppermute(edge, "tm", far_pairs),
        )

    def peers_of(array):
        array = lax.all_to_all(array, "tm", 0, 0, axis_index_groups=cores, tiled=True)
        if on_dp:
            array = lax.all_gather(array, "dp", axis=0, tiled=True)
        return array

    slice_width = width // shards
    pair = in_weight.reshape(2, slice_width, width)
    kept = lax.dynamic_index_in_dim(pair, core, 0, keepdims=False)
    given = lax.ppermute(lax.dynamic_index_in_dim(pair, 1 - core, 0, keepdims=False), "tm", swap)
    block = jnp.concatenate([jnp.where(first, kept, given), jnp.where(first, given, kept)], axis=0)
    shifts = [(0,)] + [(k, depth - k) if 2 * k < depth else (k,) for k in range(1, depth // 2 + 1)]
    along = {0: block}
    for k in [k for group in shifts[1:] for k in group]:
        along[k] = lax.ppermute(block, "tm", [(i, (i + 8 * k) % shards) for i in range(shards)])
    corner = [(i, i ^ (4 if i % 2 else 2)) for i in range(shards)]
    pieces, relayed = [], None
    for number, group in enumerate(shifts):
        blocks = jnp.concatenate([along[k] for k in group], axis=0)
        if number == 1:
            blocks, relayed = lax.optimization_barrier((blocks, relayed))
        elif number > 1:
            blocks, _ = lax.optimization_barrier((blocks, pieces[4 * number - 5]))
        from_x = lax.ppermute(blocks, "tm", swap_x)
        from_y = lax.ppermute(blocks, "tm", swap_y)
        relayed = jnp.where(first, from_y, from_x)
        pieces += [blocks, from_x, from_y]
        if number + 1 < len(shifts):
            pieces.append(lax.ppermute(relayed, "tm", corner))
    features, start_noise, cotangent, kernel, bn_gain, bn_shift, _ = lax.optimization_barrier(
        (features, start_noise, cotangent, kernel, bn_gain, bn_shift, pieces[4])
    )
    packed = jnp.concatenate([features, start_noise, cotangent], axis=0)
    partner, near, far = across(
        packed, jnp.where(first, packed[:, :HALO], packed[:, rows - HALO :])
    )
    whole = jnp.concatenate(
        [
            jnp.where(first, far, near),
            jnp.where(first, packed, partner),
            jnp.where(first, partner, packed),
            jnp.where(first, near, far),
        ],
        axis=1,
    )
    wide_features, wide_noise, wide_cot = whole[0], whole[1], whole[2]

    place_of = jnp.arange(half_width, dtype=jnp.int32)
    source = (2 * (place_of // slice_width) + core) * slice_width + place_of % slice_width
    chosen = (jnp.arange(width, dtype=jnp.int32)[:, None] == source[None, :]).astype(BF16)
    cot = jnp.dot(wide_cot[HALO - EDGE : -(HALO - EDGE)], chosen, preferred_element_type=F32).astype(BF16)

    def mine_of(array):
        parts = array.reshape(array.shape[0], chips, 2, slice_width)
        return lax.dynamic_index_in_dim(parts, core, 2, keepdims=False).reshape(-1, half_width)

    channel = mine_of(jnp.concatenate([kernel, bn_gain[None], bn_shift[None]], axis=0))
    gain, shift = channel[taps_n : taps_n + 1], channel[taps_n + 1 :]
    taps = jnp.broadcast_to(channel[:taps_n, None], (taps_n, 8, half_width))

    frame_ids = chip * chip_rows - HALO + jnp.arange(whole.shape[1], dtype=jnp.int32)
    live = ((frame_ids >= 0) & (frame_ids < end)).astype(F32)
    summed = wide_features.astype(F32) + noise_scale * wide_noise.astype(F32) * live[:, None]
    normed_b = normalize(summed)[0].astype(BF16)

    relayed, normed_b, taps, gain, shift = lax.optimization_barrier(
        (relayed, normed_b, taps, gain, shift)
    )
    pieces.append(lax.ppermute(relayed, "tm", corner))
    weight = place(scal, pieces, shifts, block.shape[0])

    value, gate, glu, conv, stats = forward(
        scal, normed_b, weight, taps, chip_rows, chips, True
    )
    scaled, grad, inv, sums = batch(scal, counts, peers_of(stats), conv, cot, gain, shift, chips)
    mine, other, grad_conv, totals = backward(
        scal, peers_of(sums), scaled, grad, inv, gain, taps, value, gate, weight
    )
    other = lax.ppermute(other, "tm", swap)
    moved, edge, squares = direction(scal, mine, other, features[0], start_noise[0], shards)
    squares = lax.all_to_all(squares, "tm", 0, 0, tiled=True)
    partner, near, far = across(moved, edge)
    taps_before = tap_grad(taps_n, grad_conv, glu)
    squares, taps_before = lax.optimization_barrier((squares, taps_before))
    perturbation, normed_b = ascend(
        scal, squares, wide_features, wide_noise, moved, partner, near, far, start_noise[0]
    )

    glu, conv, stats = forward(scal, normed_b, weight, taps, chip_rows, chips, False)
    alone, crossed = raw_taps(taps_n, scal, conv, glu, stats)
    outgoing, factor = last(
        taps_n, chips, scal, counts, peers_of(stats), conv, cot, gain, shift, glu, alone, crossed, stats, taps_before
    )
    received = peers_of(outgoing)
    known = jnp.concatenate([factor, totals], axis=0)
    known = lax.dynamic_slice_in_dim(known, chip * slice_width, slice_width, 1)
    kernel_total, norm_total = finish(taps_n, scal, received, known)
    return (perturbation[None], kernel_total, norm_total)


def solution(mesh):
    return jax.shard_map(
        functools.partial(on_device, mesh.shape["dp"] > 1),
        mesh=mesh,
        in_specs=(
            P("dp", "tm", None),
            P("dp", "tm", None),
            P("dp", "tm", None),
            P("tm", None),
            P(),
            P(),
            P(),
            P(),
        ),
        out_specs=(P("dp", "tm", None), P(None, "tm"), P(None, "tm")),
        check_vma=False,
    )
```

```python
import functools

import jax
import jax.numpy as jnp
from jax import lax
from jax.experimental import pallas as pl
from jax.experimental.pallas import tpu as pltpu
from jax.sharding import PartitionSpec as P

ASCENT = 2

noise_scale = 0.5
ascent_rate = 0.5
layer_epsilon = 1e-05
batch_epsilon = 1e-05
ascent_epsilon = 1e-06

HALO = 32
EDGE = 16
F32 = jnp.float32
BF16 = jnp.bfloat16


def params(limit=56 * 1024 * 1024):
    return pltpu.CompilerParams(vmem_limit_bytes=limit)


def cost(flops, nbytes):
    return pl.CostEstimate(flops=int(flops), bytes_accessed=int(nbytes), transcendentals=0)


def normalize(summed):
    centre = summed - jnp.mean(summed, axis=-1, keepdims=True)
    inverse = lax.rsqrt(jnp.mean(centre * centre, axis=-1, keepdims=True) + layer_epsilon)
    return (centre * inverse, inverse)


def live_rows(first, rows, end):
    ids = first + lax.broadcasted_iota(jnp.int32, (rows, 1), 0)
    return jnp.where((ids >= 0) & (ids < end), 1.0, 0.0).astype(F32)


def spread(plain, shifted, array):
    plain[...] = array
    rows, tiles = shifted.shape[1] * 8, shifted.shape[1]
    for s in range(8):
        shifted[s] = plain[s : s + rows].reshape(tiles, 8, -1)


def tiles_at(shifted, row, tiles, lanes):
    first = (row - row % 8) // 8
    return shifted[row % 8, first : first + tiles, :, lanes]


def convolve(taps, shifted, offsets, rows, most):
    most = max(n for n in range(1, most + 1) if rows // 8 % n == 0)
    columns = []
    for lane in range(0, taps.shape[2], 128):
        lanes = slice(lane, lane + 128)
        parts = []
        for tile in range(0, rows // 8, most):
            total = jnp.zeros((most, 8, 128), F32)
            for tap, offset in enumerate(offsets):
                total = total + taps[tap, :, lanes][None] * tiles_at(
                    shifted, offset + 8 * tile, most, lanes
                )
            parts.append(total.reshape(most * 8, 128))
        columns.append(jnp.concatenate(parts, axis=0))
    return jnp.concatenate(columns, axis=1)


def correlate(taps_n, left, shifted, first):
    rows = left.shape[0]
    lanes = slice(0, 128)
    most = 16
    totals = [None] * taps_n
    for tile in range(0, rows // 8, most):
        part = left[8 * tile : 8 * (tile + most)].reshape(most, 8, 128)
        for tap in range(taps_n):
            product = jnp.sum(
                part * tiles_at(shifted, first + tap + 8 * tile, most, lanes), axis=0, keepdims=True
            )
            totals[tap] = product if totals[tap] is None else totals[tap] + product
    return jnp.sum(jnp.concatenate(totals, axis=0), axis=1)


def block_row(scal, size, depth, shift, other):
    chip = lax.rem(scal[5] - shift + depth, depth) * 4 + (scal[4] ^ other)
    return pl.multiple_of(chip * size, 16)


def place_kernel(kinds, size, scal, *refs):
    pieces, out = refs[:-1], refs[-1]
    depth = out.shape[0] // (4 * size)
    for (group, other), ref in zip(kinds, pieces):
        for nth, shift in enumerate(group):
            row = block_row(scal, size, depth, shift, other)
            out[pl.ds(row, size), :] = ref[nth * size : (nth + 1) * size, :]


def place_late_kernel(kinds, size, scal, *refs):
    pieces, out, sems = refs[: len(kinds)], refs[-2], refs[-1]
    depth = out.shape[0] // (4 * size)
    copies = []
    for (group, other), ref in zip(kinds, pieces):
        for nth, shift in enumerate(group):
            row = block_row(scal, size, depth, shift, other)
            copies.append(
                pltpu.make_async_copy(
                    ref.at[pl.ds(nth * size, size), :],
                    out.at[pl.ds(row, size), :],
                    sems.at[len(copies)],
                )
            )
    for copy in copies:
        copy.start()
    for copy in copies:
        copy.wait()


def place(scal, kinds, pieces, size, chips):
    width = pieces[0].shape[1]
    vmem = pl.BlockSpec(memory_space=pltpu.VMEM)
    return pl.pallas_call(
        functools.partial(place_kernel, kinds, size),
        in_specs=[pl.BlockSpec(memory_space=pltpu.SMEM)] + [vmem] * len(pieces),
        out_specs=vmem,
        out_shape=jax.ShapeDtypeStruct((chips * size, width), BF16),
        compiler_params=params(),
        cost_estimate=cost(0, 4 * chips * size * width),
        name="place_weights",
    )(scal, *pieces)


def place_late(scal, kinds, pieces, size, weight):
    count = sum(len(group) for group, _ in kinds)
    vmem = pl.BlockSpec(memory_space=pltpu.VMEM)
    hbm = pl.BlockSpec(memory_space=pl.ANY)
    return pl.pallas_call(
        functools.partial(place_late_kernel, kinds, size),
        in_specs=[pl.BlockSpec(memory_space=pltpu.SMEM)] + [vmem] * len(pieces) + [hbm],
        out_specs=hbm,
        out_shape=jax.ShapeDtypeStruct(weight.shape, BF16),
        scratch_shapes=[pltpu.SemaphoreType.DMA((count,))],
        input_output_aliases={len(pieces) + 1: 0},
        compiler_params=params(),
        cost_estimate=cost(0, 4 * count * size * weight.shape[1]),
        name="place_last_weights",
    )(scal, *pieces, weight)


def forward_kernel(keep, scal, nb, value_w, gate_w, taps, *refs):
    kept, (glu, conv, stats, plain, shifted) = refs[: 2 * keep], refs[2 * keep :]
    start, end = scal[0], scal[1]
    span, taps_n = nb.shape[0], taps.shape[0]
    rows = conv.shape[0] - 2 * EDGE
    contract = (((1,), (1,)), ((), ()))
    v = lax.dot_general(nb[...], value_w[...], contract, preferred_element_type=F32)
    s = jax.nn.sigmoid(lax.dot_general(nb[...], gate_w[...], contract, preferred_element_type=F32))
    if keep:
        kept[0][...] = v[HALO : HALO + rows]
        kept[1][...] = s[HALO : HALO + rows]
    gated = (v * s * live_rows(start - HALO, span, end)).astype(BF16)
    glu[...] = gated
    spread(plain, shifted, gated.astype(F32))
    shift = HALO - EDGE - (taps_n - 1) // 2
    conv[...] = convolve(taps, shifted, [shift + tap for tap in range(taps_n)], conv.shape[0], 12)
    live = live_rows(start, rows, end)
    own = conv[EDGE : EDGE + rows, :]
    mass = jnp.sum(live * own, axis=0, keepdims=True)
    centre = live * (own - mass / jnp.maximum(jnp.sum(live), 1.0))
    both = jnp.concatenate([mass, jnp.sum(centre * centre, axis=0, keepdims=True)], axis=0)
    for peer in range(stats.shape[0]):
        stats[peer] = both


def forward(scal, nb, weight, taps, rows, peers, keep):
    span, width = nb.shape
    taps_n, _, half_width = taps.shape
    chunk = 256 if half_width % 256 == 0 else 128
    steps = half_width // chunk
    col = lambda n: pl.BlockSpec((n, chunk), lambda i: (0, i))
    return pl.pallas_call(
        functools.partial(forward_kernel, keep),
        grid=(steps,),
        in_specs=[
            pl.BlockSpec(memory_space=pltpu.SMEM),
            pl.BlockSpec((span, width), lambda i: (0, 0)),
            pl.BlockSpec((chunk, width), lambda i: (i, 0)),
            pl.BlockSpec((chunk, width), lambda i: (i + steps, 0)),
            pl.BlockSpec((taps_n, 8, chunk), lambda i: (0, 0, i)),
        ],
        out_specs=[
            *([col(rows)] * (2 * keep)),
            col(span),
            col(rows + 2 * EDGE),
            pl.BlockSpec((peers, 2, chunk), lambda i: (0, 0, i)),
        ],
        out_shape=[
            *([jax.ShapeDtypeStruct((rows, half_width), F32)] * (2 * keep)),
            jax.ShapeDtypeStruct((span, half_width), BF16),
            jax.ShapeDtypeStruct((rows + 2 * EDGE, half_width), F32),
            jax.ShapeDtypeStruct((peers, 2, half_width), F32),
        ],
        scratch_shapes=[
            pltpu.VMEM((span, chunk), F32),
            pltpu.VMEM((8, span // 8 - 1, 8, chunk), F32),
        ],
        compiler_params=params(),
        cost_estimate=cost(2 * span * width * 2 * half_width, 4 * half_width * width + 10 * span * half_width),
        name="project_glu_conv",
    )(scal, nb, weight, weight, taps)


def moments(counts, stats, live_count):
    mass = stats[0, 0:1, :]
    square = stats[0, 1:2, :]
    for peer in range(1, stats.shape[0]):
        mass = mass + stats[peer, 0:1, :]
        square = square + stats[peer, 1:2, :]
    mean = mass / live_count
    for peer in range(stats.shape[0]):
        off = stats[peer, 0:1, :] - counts[0, peer] * mean
        square = square + off * off * counts[1, peer]
    return mean, lax.rsqrt(square / live_count + batch_epsilon)


def swish_grads(scal, counts, stats, conv, cot, gain, shift):
    start, end = scal[0], scal[1]
    live_count = scal[3].astype(F32)
    mean, inv = moments(counts, stats, live_count)
    scaled = (conv[...] - mean) * inv
    pre = gain[...] * scaled + shift[...]
    sig = jax.nn.sigmoid(pre)
    live = live_rows(start - EDGE, conv.shape[0], end)
    upstream = live * cot[...].astype(F32) / ASCENT
    return scaled, upstream * sig * (1.0 + pre * (1.0 - sig)), live, mean, inv


def batch_kernel(scal, counts, stats, conv, cot, gain, shift, scaled_out, grad_out, inv_out, sums):
    scaled, grad, live, mean, inv = swish_grads(scal, counts, stats, conv, cot, gain, shift)
    scaled_out[...] = scaled
    grad_out[...] = grad
    inv_out[...] = inv
    rows = conv.shape[0] - 2 * EDGE
    own = grad[EDGE : EDGE + rows]
    both = jnp.concatenate(
        [
            jnp.sum(own, axis=0, keepdims=True),
            jnp.sum(own * scaled[EDGE : EDGE + rows], axis=0, keepdims=True),
        ],
        axis=0,
    )
    for peer in range(sums.shape[0]):
        sums[peer] = both


def batch(scal, counts, stats, conv, cot, gain, shift, peers):
    span, half_width = conv.shape
    chunk = 256 if half_width % 256 == 0 else 128
    col = lambda n: pl.BlockSpec((n, chunk), lambda i: (0, i))
    smem = pl.BlockSpec(memory_space=pltpu.SMEM)
    return pl.pallas_call(
        batch_kernel,
        grid=(half_width // chunk,),
        in_specs=[
            smem,
            smem,
            pl.BlockSpec((stats.shape[0], 2, chunk), lambda i: (0, 0, i)),
            col(span),
            col(span),
            col(1),
            col(1),
        ],
        out_specs=[col(span), col(span), col(1), pl.BlockSpec((peers, 2, chunk), lambda i: (0, 0, i))],
        out_shape=[
            jax.ShapeDtypeStruct((span, half_width), F32),
            jax.ShapeDtypeStruct((span, half_width), F32),
            jax.ShapeDtypeStruct((1, half_width), F32),
            jax.ShapeDtypeStruct((peers, 2, half_width), F32),
        ],
        compiler_params=params(),
        cost_estimate=cost(40 * span * half_width, 16 * span * half_width),
        name="batch_norm_swish",
    )(scal, counts, stats, conv, cot, gain, shift)


def backward_kernel(scal, sums, scaled, grad, inv, gain, taps, value, gate, value_w, gate_w, mine, other, grad_conv, totals, plain, shifted, part):
    start, end, core = scal[0], scal[1], scal[2]
    rows, taps_n = value.shape[0], taps.shape[0]
    half = (taps_n - 1) // 2
    live_count = scal[3].astype(F32)
    both = sums[0]
    for peer in range(1, sums.shape[0]):
        both = both + sums[peer]
    totals[...] = both
    shift_sum, gain_sum = both[0:1], both[1:2]
    live = live_rows(start - EDGE, scaled.shape[0], end)
    through = live * (inv[...] * gain[...]) * (
        grad[...] - (shift_sum + scaled[...] * gain_sum) / live_count
    )
    rounded = through.astype(BF16)
    grad_conv[...] = rounded[EDGE : EDGE + rows]
    spread(plain, shifted, rounded.astype(F32))
    grad_glu = convolve(taps, shifted, [EDGE + half - tap for tap in range(taps_n)], rows, 16)
    grad_glu = (grad_glu * live_rows(start, rows, end)).astype(BF16).astype(F32)
    sig = gate[...]
    to_value = (grad_glu * sig).astype(BF16)
    to_gate = (grad_glu * value[...] * sig * (1.0 - sig)).astype(BF16)
    product = jnp.dot(to_value, value_w[...], preferred_element_type=F32) + jnp.dot(
        to_gate, gate_w[...], preferred_element_type=F32
    )
    step, last_step = pl.program_id(0), pl.num_programs(0) - 1

    @pl.when(step == 0)
    def _():
        part[...] = product

    @pl.when(step > 0)
    def _():
        part[...] += product

    @pl.when(step == last_step)
    def _():
        count = mine.shape[0]
        mine[...] = part[pl.ds(pl.multiple_of(core * count, count), count), :]
        other[...] = part[pl.ds(pl.multiple_of((1 - core) * count, count), count), :]


def backward(scal, sums, scaled, grad, inv, gain, taps, value, gate, weight):
    span, half_width = scaled.shape
    rows, width = value.shape[0], weight.shape[1]
    chunk = 256 if half_width % 256 == 0 else 128
    steps = half_width // chunk
    taps_n = taps.shape[0]
    col = lambda n: pl.BlockSpec((n, chunk), lambda i: (0, i))
    own = pl.BlockSpec((rows // 2, width), lambda i: (0, 0))
    return pl.pallas_call(
        backward_kernel,
        grid=(steps,),
        in_specs=[
            pl.BlockSpec(memory_space=pltpu.SMEM),
            pl.BlockSpec((sums.shape[0], 2, chunk), lambda i: (0, 0, i)),
            col(span),
            col(span),
            col(1),
            col(1),
            pl.BlockSpec((taps_n, 8, chunk), lambda i: (0, 0, i)),
            col(rows),
            col(rows),
            pl.BlockSpec((chunk, width), lambda i: (i, 0)),
            pl.BlockSpec((chunk, width), lambda i: (i + steps, 0)),
        ],
        out_specs=[own, own, col(rows), col(2)],
        out_shape=[
            jax.ShapeDtypeStruct((rows // 2, width), F32),
            jax.ShapeDtypeStruct((rows // 2, width), F32),
            jax.ShapeDtypeStruct((rows, half_width), BF16),
            jax.ShapeDtypeStruct((2, half_width), F32),
        ],
        scratch_shapes=[
            pltpu.VMEM((span, chunk), F32),
            pltpu.VMEM((8, span // 8 - 1, 8, chunk), F32),
            pltpu.VMEM((rows, width), F32),
        ],
        compiler_params=params(),
        cost_estimate=cost(2 * rows * width * 2 * half_width, 4 * half_width * width + 20 * span * half_width),
        name="grad_conv_project_back",
    )(scal, sums, scaled, grad, inv, gain, taps, value, gate, weight, weight)


def shifted_scratch(span):
    return [pltpu.VMEM((span, 128), F32), pltpu.VMEM((8, span // 8 - 1, 8, 128), F32)]


def tap_grad_kernel(taps_n, grad_conv, glu, out, plain, shifted):
    spread(plain, shifted, glu[...].astype(F32))
    first = HALO - (taps_n - 1) // 2
    out[...] = correlate(taps_n, grad_conv[...].astype(F32), shifted, first)


def tap_grad(taps_n, grad_conv, glu):
    rows, half_width = grad_conv.shape
    span = glu.shape[0]
    col = lambda n: pl.BlockSpec((n, 128), lambda i: (0, i))
    return pl.pallas_call(
        functools.partial(tap_grad_kernel, taps_n),
        grid=(half_width // 128,),
        in_specs=[col(rows), col(span)],
        out_specs=col(taps_n),
        out_shape=jax.ShapeDtypeStruct((taps_n, half_width), F32),
        scratch_shapes=shifted_scratch(span),
        compiler_params=params(),
        cost_estimate=cost(2 * taps_n * rows * half_width, 4 * span * half_width),
        name="tap_grad",
    )(grad_conv, glu)


def raw_taps_kernel(taps_n, scal, conv, glu, stats, alone, crossed, plain, shifted):
    start, end = scal[0], scal[1]
    rows, span = conv.shape[0] - 2 * EDGE, glu.shape[0]
    spread(plain, shifted, glu[...].astype(F32))
    first = HALO - (taps_n - 1) // 2
    live = live_rows(start, rows, end)
    local = stats[0, 0:1, :] / jnp.maximum(jnp.sum(live), 1.0)
    crossed[...] = correlate(taps_n, live * (conv[EDGE : EDGE + rows, :] - local), shifted, first)
    tap = lax.broadcasted_iota(jnp.int32, (taps_n, span), 0)
    at = lax.broadcasted_iota(jnp.int32, (taps_n, span), 1) - first - tap
    inside = (at >= 0) & (at < jnp.clip(end - start, 0, rows))
    alone[...] = jnp.dot(
        jnp.where(inside, 1.0, 0.0).astype(BF16), glu[...], preferred_element_type=F32
    )


def raw_taps(taps_n, scal, conv, glu, stats):
    rows, half_width = conv.shape
    span = glu.shape[0]
    col = lambda n: pl.BlockSpec((n, 128), lambda i: (0, i))
    return pl.pallas_call(
        functools.partial(raw_taps_kernel, taps_n),
        grid=(half_width // 128,),
        in_specs=[
            pl.BlockSpec(memory_space=pltpu.SMEM),
            col(rows),
            col(span),
            pl.BlockSpec((1, 2, 128), lambda i: (0, 0, i)),
        ],
        out_specs=[col(taps_n), col(taps_n)],
        out_shape=[jax.ShapeDtypeStruct((taps_n, half_width), F32)] * 2,
        scratch_shapes=shifted_scratch(span),
        compiler_params=params(),
        cost_estimate=cost(2 * taps_n * rows * half_width, 8 * span * half_width),
        name="raw_taps",
    )(scal, conv, glu, stats)


def halves(array):
    high = array.astype(BF16).astype(F32)
    return high, array - high


def last_kernel(taps_n, scal, counts, stats, conv, cot, gain, shift, glu, alone, crossed, local_stats, taps_before, out, factor_out, plain, shifted, pay):
    step = pl.program_id(0)
    scaled, grad, live, mean, inv = swish_grads(scal, counts, stats, conv, cot, gain, shift)
    rows = conv.shape[0] - 2 * EDGE
    spread(plain, shifted, glu[...].astype(F32))
    first = HALO - (taps_n - 1) // 2
    factor = inv * gain[...]
    factor_out[...] = factor
    own = grad[EDGE : EDGE + rows]
    direct = taps_before[...] + factor * correlate(taps_n, own, shifted, first)
    own_live = live[EDGE : EDGE + rows]
    local = local_stats[0, 0:1, :] / jnp.maximum(jnp.sum(own_live), 1.0)
    with_scaled = inv * (crossed[...] + (local - mean) * alone[...])
    sums = jnp.concatenate(
        [
            jnp.sum(own, axis=0, keepdims=True),
            jnp.sum(own * scaled[EDGE : EDGE + rows], axis=0, keepdims=True),
        ],
        axis=0,
    )
    pay[step] = jnp.concatenate([*halves(direct), with_scaled, alone[...], *halves(sums)], axis=0)

    @pl.when(step == pl.num_programs(0) - 1)
    def _():
        turned = jnp.concatenate([jnp.transpose(pay[s]) for s in range(pay.shape[0])], axis=0)
        block = out.shape[1]
        for index in range(out.shape[0]):
            out[index] = turned[index * block : (index + 1) * block].astype(BF16)


def last(taps_n, peers, scal, counts, stats, conv, cot, gain, shift, glu, alone, crossed, local_stats, taps_before):
    span, half_width = conv.shape
    chunk = 128
    steps = half_width // chunk
    pay = 4 * taps_n + 4
    col = lambda n: pl.BlockSpec((n, chunk), lambda i: (0, i))
    smem = pl.BlockSpec(memory_space=pltpu.SMEM)
    return pl.pallas_call(
        functools.partial(last_kernel, taps_n),
        grid=(steps,),
        in_specs=[
            smem,
            smem,
            pl.BlockSpec((stats.shape[0], 2, chunk), lambda i: (0, 0, i)),
            col(span),
            col(span),
            col(1),
            col(1),
            col(glu.shape[0]),
            col(taps_n),
            col(taps_n),
            pl.BlockSpec((1, 2, chunk), lambda i: (0, 0, i)),
            col(taps_n),
        ],
        out_specs=[pl.BlockSpec((peers, half_width // peers, pay), lambda i: (0, 0, 0)), col(1)],
        out_shape=[
            jax.ShapeDtypeStruct((peers, half_width // peers, pay), BF16),
            jax.ShapeDtypeStruct((1, half_width), F32),
        ],
        scratch_shapes=[*shifted_scratch(glu.shape[0]), pltpu.VMEM((steps, pay, chunk), F32)],
        compiler_params=params(),
        cost_estimate=cost(100 * span * half_width, 10 * span * half_width),
        name="batch_norm_swish_taps",
    )(scal, counts, stats, conv, cot, gain, shift, glu, alone, crossed, local_stats, taps_before)


def finish_kernel(taps_n, scal, received, known, taps_out, norm_out):
    total = received[0].astype(F32)
    for index in range(1, received.shape[0]):
        total = total + received[index].astype(F32)
    total = jnp.transpose(total)
    n = taps_n
    sums = total[4 * n : 4 * n + 2] + total[4 * n + 2 : 4 * n + 4]
    shift_sum, gain_sum = sums[0:1], sums[1:2]
    factor = known[0:1] / scal[3].astype(F32)
    taps_out[...] = (total[:n] + total[n : 2 * n]) - factor * (
        gain_sum * total[2 * n : 3 * n] + shift_sum * total[3 * n : 4 * n]
    )
    norm_out[...] = jnp.concatenate([gain_sum + known[2:3], shift_sum + known[1:2]], axis=0)


def finish(taps_n, scal, received, known):
    width = received.shape[1]
    vmem = pl.BlockSpec(memory_space=pltpu.VMEM)
    return pl.pallas_call(
        functools.partial(finish_kernel, taps_n),
        in_specs=[pl.BlockSpec(memory_space=pltpu.SMEM), vmem, vmem],
        out_shape=[
            jax.ShapeDtypeStruct((taps_n, width), F32),
            jax.ShapeDtypeStruct((2, width), F32),
        ],
        compiler_params=params(),
        name="finish",
    )(scal, received, known)


def direction_kernel(scal, mine, other, features, noise, out, edge, squares):
    rows = mine.shape[0]
    first = scal[0] + scal[2] * rows
    block = 32
    total = jnp.zeros((1, 128), F32)
    for row in range(0, rows, block):
        at = slice(row, row + block)
        live = live_rows(first + row, block, scal[1])
        summed = features[at].astype(F32) + noise_scale * noise[at].astype(F32) * live
        normed, inverse = normalize(summed)
        grad = mine[at] + other[at]
        moved = (
            live
            * inverse
            * (
                grad
                - jnp.mean(grad, axis=-1, keepdims=True)
                - normed * jnp.mean(grad * normed, axis=-1, keepdims=True)
            )
        )
        out[at] = moved
        total = total + jnp.sum(moved * moved)
    edge[...] = jnp.where(scal[2] == 0, out[:HALO], out[rows - HALO :])
    for peer in range(squares.shape[0]):
        squares[peer] = total


def direction(scal, mine, other, features, noise, peers):
    rows, width = mine.shape
    vmem = pl.BlockSpec(memory_space=pltpu.VMEM)
    return pl.pallas_call(
        direction_kernel,
        in_specs=[pl.BlockSpec(memory_space=pltpu.SMEM)] + [vmem] * 4,
        out_shape=[
            jax.ShapeDtypeStruct((rows, width), F32),
            jax.ShapeDtypeStruct((HALO, width), F32),
            jax.ShapeDtypeStruct((peers, 1, 128), F32),
        ],
        compiler_params=params(),
        cost_estimate=cost(30 * rows * width, 16 * rows * width),
        name="direction",
    )(scal, mine, other, features, noise)


def ascend_kernel(scal, squares, features, noise, mine, partner, near, far, own_noise, perturbation, normed_out):
    start, end, core = scal[0], scal[1], scal[2]
    rows, width = mine.shape
    total = squares[0]
    for index in range(1, squares.shape[0]):
        total = total + squares[index]
    total = total[0:1, 0:1]
    length = jnp.full((1, 1), 1.0, F32) * end.astype(F32)
    rate = ascent_rate * jnp.sqrt(length * width) / (jnp.sqrt(total) + ascent_epsilon)
    block = 32
    is_first = core == 0

    def place(row, moved):
        at = slice(row, row + block)
        live = live_rows(start - HALO + row, block, end)
        summed = features[at].astype(F32) + (noise_scale * noise[at].astype(F32) * live + moved * rate)
        normed_out[at] = normalize(summed)[0].astype(BF16)

    place(0, jnp.where(is_first, far[...], near[...]))
    for row in range(0, rows, block):
        at = slice(row, row + block)
        place(HALO + row, jnp.where(is_first, mine[at], partner[at]))
        place(HALO + rows + row, jnp.where(is_first, partner[at], mine[at]))
        live = live_rows(start + core * rows + row, block, end)
        perturbation[at] = noise_scale * own_noise[at].astype(F32) * live + mine[at] * rate
    place(HALO + 2 * rows, jnp.where(is_first, near[...], far[...]))


def ascend(scal, squares, features, noise, mine, partner, near, far, own_noise):
    vmem = pl.BlockSpec(memory_space=pltpu.VMEM)
    return pl.pallas_call(
        ascend_kernel,
        in_specs=[pl.BlockSpec(memory_space=pltpu.SMEM)] + [vmem] * 8,
        out_shape=[
            jax.ShapeDtypeStruct(mine.shape, F32),
            jax.ShapeDtypeStruct(features.shape, BF16),
        ],
        compiler_params=params(),
        cost_estimate=cost(30 * features.size, 8 * features.size),
        name="ascend",
    )(scal, squares, features, noise, mine, partner, near, far, own_noise)


def on_device(on_dp, features, start_noise, cotangent, in_weight, kernel, bn_gain, bn_shift, ends):
    rows, width = features.shape[1:]
    taps_n = kernel.shape[0]
    shards = lax.axis_size("tm")
    chips = shards // 2
    index = lax.axis_index("tm")
    group = lax.axis_index("dp")
    chip, core = index // 2, index % 2
    chip_rows = 2 * rows
    half_width = width // 2
    end = lax.dynamic_index_in_dim(ends, group, 0, keepdims=False)
    scal = jnp.stack([chip * chip_rows, end, core, jnp.sum(ends), chip % 4, chip // 4]).astype(jnp.int32)
    held = jnp.clip(
        ends[:, None] - chip_rows * jnp.arange(chips, dtype=jnp.int32)[None, :], 0, chip_rows
    ).reshape(-1).astype(F32)
    counts = jnp.stack([held, jnp.where(held > 0, 1.0 / jnp.maximum(held, 1.0), 0.0)])

    cores = [[2 * c + k for c in range(chips)] for k in range(2)]
    depth = chips // 4
    swap = [(i, i ^ 1) for i in range(shards)]
    swap_x = [(i, i ^ 2) for i in range(shards)]
    swap_y = [(i, i ^ 4) for i in range(shards)]
    near_pairs = [(2 * c, 2 * c - 2) for c in range(1, chips)] + [
        (2 * c + 1, 2 * c + 3) for c in range(chips - 1)
    ]
    far_pairs = [(2 * c, 2 * c - 1) for c in range(1, chips)] + [
        (2 * c + 1, 2 * c + 2) for c in range(chips - 1)
    ]
    first = core == 0

    def across(array, edge):
        return (
            lax.ppermute(array, "tm", swap),
            lax.ppermute(edge, "tm", near_pairs),
            lax.ppermute(edge, "tm", far_pairs),
        )

    def peers_of(array):
        array = lax.all_to_all(array, "tm", 0, 0, axis_index_groups=cores, tiled=True)
        if on_dp:
            array = lax.all_gather(array, "dp", axis=0, tiled=True)
        return array

    slice_width = width // shards
    pair = in_weight.reshape(2, slice_width, width)
    kept = lax.dynamic_index_in_dim(pair, core, 0, keepdims=False)
    given = lax.ppermute(lax.dynamic_index_in_dim(pair, 1 - core, 0, keepdims=False), "tm", swap)
    block = jnp.concatenate([jnp.where(first, kept, given), jnp.where(first, given, kept)], axis=0)
    shifts = [(0,)] + [(k, depth - k) if 2 * k < depth else (k,) for k in range(1, depth // 2 + 1)]
    forth = [(i, (i + 8) % shards) for i in range(shards)]
    back = [(i, (i - 8) % shards) for i in range(shards)]
    corner = [(i, i ^ (4 if i % 2 else 2)) for i in range(shards)]
    along = {0: block, depth: block}
    kinds, pieces, late_kinds, late_pieces = [], [], [], []
    for number, group in enumerate(shifts):
        blocks = jnp.concatenate([along[k] for k in group], axis=0)
        sent = [lax.ppermute(blocks, "tm", swap_x), lax.ppermute(blocks, "tm", swap_y)]
        if number:
            sent.append(lax.ppermute(relayed, "tm", corner))
        if number + 1 < len(shifts):
            for k in shifts[number + 1]:
                from_before = 2 * k <= depth
                sent.append(lax.ppermute(along[k - 1 if from_before else k + 1], "tm", forth if from_before else back))
        sent = list(lax.optimization_barrier(tuple(sent)))
        from_x, from_y = sent[:2]
        relayed = jnp.where(first, from_y, from_x)
        kinds += [(group, 0), (group, 1), (group, 2)]
        pieces += [blocks, from_x, from_y]
        late_kinds.append((group, 3))
        if number:
            late_pieces.append(sent[2])
        else:
            square_done = from_x
        if number + 1 < len(shifts):
            for k, arrived in zip(shifts[number + 1], sent[-len(shifts[number + 1]) :]):
                along[k] = arrived
    features, start_noise, cotangent, kernel, bn_gain, bn_shift, _ = lax.optimization_barrier(
        (features, start_noise, cotangent, kernel, bn_gain, bn_shift, square_done)
    )
    packed = jnp.concatenate([features, start_noise, cotangent], axis=0)
    partner, near, far = across(
        packed, jnp.where(first, packed[:, :HALO], packed[:, rows - HALO :])
    )
    whole = jnp.concatenate(
        [
            jnp.where(first, far, near),
            jnp.where(first, packed, partner),
            jnp.where(first, partner, packed),
            jnp.where(first, near, far),
        ],
        axis=1,
    )
    wide_features, wide_noise, wide_cot = whole[0], whole[1], whole[2]

    place_of = jnp.arange(half_width, dtype=jnp.int32)
    source = (2 * (place_of // slice_width) + core) * slice_width + place_of % slice_width
    chosen = (jnp.arange(width, dtype=jnp.int32)[:, None] == source[None, :]).astype(BF16)
    cot = jnp.dot(wide_cot[HALO - EDGE : -(HALO - EDGE)], chosen, preferred_element_type=F32).astype(BF16)

    def mine_of(array):
        parts = array.reshape(array.shape[0], chips, 2, slice_width)
        return lax.dynamic_index_in_dim(parts, core, 2, keepdims=False).reshape(-1, half_width)

    channel = mine_of(jnp.concatenate([kernel, bn_gain[None], bn_shift[None]], axis=0))
    gain, shift = channel[taps_n : taps_n + 1], channel[taps_n + 1 :]
    taps = jnp.broadcast_to(channel[:taps_n, None], (taps_n, 8, half_width))

    frame_ids = chip * chip_rows - HALO + jnp.arange(whole.shape[1], dtype=jnp.int32)
    live = ((frame_ids >= 0) & (frame_ids < end)).astype(F32)
    summed = wide_features.astype(F32) + noise_scale * wide_noise.astype(F32) * live[:, None]
    normed_b = normalize(summed)[0].astype(BF16)

    relayed, normed_b, taps, gain, shift = lax.optimization_barrier(
        (relayed, normed_b, taps, gain, shift)
    )
    late_pieces.append(lax.ppermute(relayed, "tm", corner))
    kinds, pieces = kinds + late_kinds[:1], pieces + late_pieces[:1]
    weight = place(scal, kinds, pieces, block.shape[0], chips)
    weight = place_late(scal, late_kinds[1:], late_pieces[1:], block.shape[0], weight)

    value, gate, glu, conv, stats = forward(
        scal, normed_b, weight, taps, chip_rows, chips, True
    )
    scaled, grad, inv, sums = batch(scal, counts, peers_of(stats), conv, cot, gain, shift, chips)
    mine, other, grad_conv, totals = backward(
        scal, peers_of(sums), scaled, grad, inv, gain, taps, value, gate, weight
    )
    other = lax.ppermute(other, "tm", swap)
    moved, edge, squares = direction(scal, mine, other, features[0], start_noise[0], shards)
    squares = lax.all_to_all(squares, "tm", 0, 0, tiled=True)
    partner, near, far = across(moved, edge)
    taps_before = tap_grad(taps_n, grad_conv, glu)
    squares, taps_before = lax.optimization_barrier((squares, taps_before))
    perturbation, normed_b = ascend(
        scal, squares, wide_features, wide_noise, moved, partner, near, far, start_noise[0]
    )

    glu, conv, stats = forward(scal, normed_b, weight, taps, chip_rows, chips, False)
    alone, crossed = raw_taps(taps_n, scal, conv, glu, stats)
    outgoing, factor = last(
        taps_n, chips, scal, counts, peers_of(stats), conv, cot, gain, shift, glu, alone, crossed, stats, taps_before
    )
    received = peers_of(outgoing)
    known = jnp.concatenate([factor, totals], axis=0)
    known = lax.dynamic_slice_in_dim(known, chip * slice_width, slice_width, 1)
    kernel_total, norm_total = finish(taps_n, scal, received, known)
    return (perturbation[None], kernel_total, norm_total)


def solution(mesh):
    return jax.shard_map(
        functools.partial(on_device, mesh.shape["dp"] > 1),
        mesh=mesh,
        in_specs=(
            P("dp", "tm", None),
            P("dp", "tm", None),
            P("dp", "tm", None),
            P("tm", None),
            P(),
            P(),
            P(),
            P(),
        ),
        out_specs=(P("dp", "tm", None), P(None, "tm"), P(None, "tm")),
        check_vma=False,
    )
```

```python
import functools

import jax
import jax.numpy as jnp
from jax import lax
from jax.experimental import pallas as pl
from jax.experimental.pallas import tpu as pltpu
from jax.sharding import PartitionSpec as P

ASCENT = 2

noise_scale = 0.5
ascent_rate = 0.5
layer_epsilon = 1e-05
batch_epsilon = 1e-05
ascent_epsilon = 1e-06

HALO = 32
EDGE = 16
F32 = jnp.float32
BF16 = jnp.bfloat16


def params(limit=56 * 1024 * 1024):
    return pltpu.CompilerParams(vmem_limit_bytes=limit)


def cost(flops, nbytes):
    return pl.CostEstimate(flops=int(flops), bytes_accessed=int(nbytes), transcendentals=0)


def normalize(summed):
    centre = summed - jnp.mean(summed, axis=-1, keepdims=True)
    inverse = lax.rsqrt(jnp.mean(centre * centre, axis=-1, keepdims=True) + layer_epsilon)
    return (centre * inverse, inverse)


def live_rows(first, rows, end):
    ids = first + lax.broadcasted_iota(jnp.int32, (rows, 1), 0)
    return jnp.where((ids >= 0) & (ids < end), 1.0, 0.0).astype(F32)


def spread(plain, shifted, array):
    plain[...] = array
    rows, tiles = shifted.shape[1] * 8, shifted.shape[1]
    for s in range(8):
        shifted[s] = plain[s : s + rows].reshape(tiles, 8, -1)


def tiles_at(shifted, row, tiles, lanes):
    first = (row - row % 8) // 8
    return shifted[row % 8, first : first + tiles, :, lanes]


def convolve(taps, shifted, offsets, rows, most):
    most = max(n for n in range(1, most + 1) if rows // 8 % n == 0)
    columns = []
    for lane in range(0, taps.shape[2], 128):
        lanes = slice(lane, lane + 128)
        parts = []
        for tile in range(0, rows // 8, most):
            total = jnp.zeros((most, 8, 128), F32)
            for tap, offset in enumerate(offsets):
                total = total + taps[tap, :, lanes][None] * tiles_at(
                    shifted, offset + 8 * tile, most, lanes
                )
            parts.append(total.reshape(most * 8, 128))
        columns.append(jnp.concatenate(parts, axis=0))
    return jnp.concatenate(columns, axis=1)


def correlate(taps_n, left, shifted, first):
    rows = left.shape[0]
    lanes = slice(0, 128)
    most = 16
    totals = [None] * taps_n
    for tile in range(0, rows // 8, most):
        part = left[8 * tile : 8 * (tile + most)].reshape(most, 8, 128)
        for tap in range(taps_n):
            product = jnp.sum(
                part * tiles_at(shifted, first + tap + 8 * tile, most, lanes), axis=0, keepdims=True
            )
            totals[tap] = product if totals[tap] is None else totals[tap] + product
    return jnp.sum(jnp.concatenate(totals, axis=0), axis=1)


def block_row(scal, size, depth, shift, other):
    chip = lax.rem(scal[5] - shift + depth, depth) * 4 + (scal[4] ^ other)
    return pl.multiple_of(chip * size, 16)


def place_kernel(kinds, size, scal, *refs):
    pieces, out = refs[:-1], refs[-1]
    depth = out.shape[0] // (4 * size)
    for (group, other), ref in zip(kinds, pieces):
        for nth, shift in enumerate(group):
            row = block_row(scal, size, depth, shift, other)
            out[pl.ds(row, size), :] = ref[nth * size : (nth + 1) * size, :]


def place_late_kernel(kinds, size, scal, *refs):
    pieces, out, sems = refs[: len(kinds)], refs[-2], refs[-1]
    depth = out.shape[0] // (4 * size)
    copies = []
    for (group, other), ref in zip(kinds, pieces):
        for nth, shift in enumerate(group):
            row = block_row(scal, size, depth, shift, other)
            copies.append(
                pltpu.make_async_copy(
                    ref.at[pl.ds(nth * size, size), :],
                    out.at[pl.ds(row, size), :],
                    sems.at[len(copies)],
                )
            )
    for copy in copies:
        copy.start()
    for copy in copies:
        copy.wait()


def place(scal, kinds, pieces, size, chips):
    width = pieces[0].shape[1]
    vmem = pl.BlockSpec(memory_space=pltpu.VMEM)
    return pl.pallas_call(
        functools.partial(place_kernel, kinds, size),
        in_specs=[pl.BlockSpec(memory_space=pltpu.SMEM)] + [vmem] * len(pieces),
        out_specs=vmem,
        out_shape=jax.ShapeDtypeStruct((chips * size, width), BF16),
        compiler_params=params(),
        cost_estimate=cost(0, 4 * chips * size * width),
        name="place_weights",
    )(scal, *pieces)


def place_late(scal, kinds, pieces, size, weight):
    count = sum(len(group) for group, _ in kinds)
    vmem = pl.BlockSpec(memory_space=pltpu.VMEM)
    hbm = pl.BlockSpec(memory_space=pl.ANY)
    return pl.pallas_call(
        functools.partial(place_late_kernel, kinds, size),
        in_specs=[pl.BlockSpec(memory_space=pltpu.SMEM)] + [vmem] * len(pieces) + [hbm],
        out_specs=hbm,
        out_shape=jax.ShapeDtypeStruct(weight.shape, BF16),
        scratch_shapes=[pltpu.SemaphoreType.DMA((count,))],
        input_output_aliases={len(pieces) + 1: 0},
        compiler_params=params(),
        cost_estimate=cost(0, 4 * count * size * weight.shape[1]),
        name="place_last_weights",
    )(scal, *pieces, weight)


def forward_kernel(keep, scal, nb, value_w, gate_w, taps, *refs):
    kept, (glu, conv, stats, plain, shifted) = refs[: 2 * keep], refs[2 * keep :]
    start, end = scal[0], scal[1]
    span, taps_n = nb.shape[0], taps.shape[0]
    rows = conv.shape[0] - 2 * EDGE
    contract = (((1,), (1,)), ((), ()))
    v = lax.dot_general(nb[...], value_w[...], contract, preferred_element_type=F32)
    s = jax.nn.sigmoid(lax.dot_general(nb[...], gate_w[...], contract, preferred_element_type=F32))
    if keep:
        kept[0][...] = v[HALO : HALO + rows]
        kept[1][...] = s[HALO : HALO + rows]
    gated = (v * s * live_rows(start - HALO, span, end)).astype(BF16)
    glu[...] = gated
    spread(plain, shifted, gated.astype(F32))
    shift = HALO - EDGE - (taps_n - 1) // 2
    conv[...] = convolve(taps, shifted, [shift + tap for tap in range(taps_n)], conv.shape[0], 12)
    live = live_rows(start, rows, end)
    own = conv[EDGE : EDGE + rows, :]
    mass = jnp.sum(live * own, axis=0, keepdims=True)
    centre = live * (own - mass / jnp.maximum(jnp.sum(live), 1.0))
    both = jnp.concatenate([mass, jnp.sum(centre * centre, axis=0, keepdims=True)], axis=0)
    for peer in range(stats.shape[0]):
        stats[peer] = both


def forward(scal, nb, weight, taps, rows, peers, keep):
    span, width = nb.shape
    taps_n, _, half_width = taps.shape
    chunk = 256 if half_width % 256 == 0 else 128
    steps = half_width // chunk
    col = lambda n: pl.BlockSpec((n, chunk), lambda i: (0, i))
    return pl.pallas_call(
        functools.partial(forward_kernel, keep),
        grid=(steps,),
        in_specs=[
            pl.BlockSpec(memory_space=pltpu.SMEM),
            pl.BlockSpec((span, width), lambda i: (0, 0)),
            pl.BlockSpec((chunk, width), lambda i: (i, 0)),
            pl.BlockSpec((chunk, width), lambda i: (i + steps, 0)),
            pl.BlockSpec((taps_n, 8, chunk), lambda i: (0, 0, i)),
        ],
        out_specs=[
            *([col(rows)] * (2 * keep)),
            col(span),
            col(rows + 2 * EDGE),
            pl.BlockSpec((peers, 2, chunk), lambda i: (0, 0, i)),
        ],
        out_shape=[
            *([jax.ShapeDtypeStruct((rows, half_width), F32)] * (2 * keep)),
            jax.ShapeDtypeStruct((span, half_width), BF16),
            jax.ShapeDtypeStruct((rows + 2 * EDGE, half_width), F32),
            jax.ShapeDtypeStruct((peers, 2, half_width), F32),
        ],
        scratch_shapes=[
            pltpu.VMEM((span, chunk), F32),
            pltpu.VMEM((8, span // 8 - 1, 8, chunk), F32),
        ],
        compiler_params=params(),
        cost_estimate=cost(2 * span * width * 2 * half_width, 4 * half_width * width + 10 * span * half_width),
        name="project_glu_conv",
    )(scal, nb, weight, weight, taps)


def moments(counts, stats, live_count):
    mass = stats[0, 0:1, :]
    square = stats[0, 1:2, :]
    for peer in range(1, stats.shape[0]):
        mass = mass + stats[peer, 0:1, :]
        square = square + stats[peer, 1:2, :]
    mean = mass / live_count
    for peer in range(stats.shape[0]):
        off = stats[peer, 0:1, :] - counts[0, peer] * mean
        square = square + off * off * counts[1, peer]
    return mean, lax.rsqrt(square / live_count + batch_epsilon)


def swish_grads(scal, counts, stats, conv, cot, gain, shift):
    start, end = scal[0], scal[1]
    live_count = scal[3].astype(F32)
    mean, inv = moments(counts, stats, live_count)
    scaled = (conv[...] - mean) * inv
    pre = gain[...] * scaled + shift[...]
    sig = jax.nn.sigmoid(pre)
    live = live_rows(start - EDGE, conv.shape[0], end)
    upstream = live * cot[...].astype(F32) / ASCENT
    return scaled, upstream * sig * (1.0 + pre * (1.0 - sig)), live, mean, inv


def batch_kernel(scal, counts, stats, conv, cot, gain, shift, scaled_out, grad_out, inv_out, sums):
    scaled, grad, live, mean, inv = swish_grads(scal, counts, stats, conv, cot, gain, shift)
    scaled_out[...] = scaled
    grad_out[...] = grad
    inv_out[...] = inv
    rows = conv.shape[0] - 2 * EDGE
    own = grad[EDGE : EDGE + rows]
    both = jnp.concatenate(
        [
            jnp.sum(own, axis=0, keepdims=True),
            jnp.sum(own * scaled[EDGE : EDGE + rows], axis=0, keepdims=True),
        ],
        axis=0,
    )
    for peer in range(sums.shape[0]):
        sums[peer] = both


def batch(scal, counts, stats, conv, cot, gain, shift, peers):
    span, half_width = conv.shape
    chunk = 256 if half_width % 256 == 0 else 128
    col = lambda n: pl.BlockSpec((n, chunk), lambda i: (0, i))
    smem = pl.BlockSpec(memory_space=pltpu.SMEM)
    return pl.pallas_call(
        batch_kernel,
        grid=(half_width // chunk,),
        in_specs=[
            smem,
            smem,
            pl.BlockSpec((stats.shape[0], 2, chunk), lambda i: (0, 0, i)),
            col(span),
            col(span),
            col(1),
            col(1),
        ],
        out_specs=[col(span), col(span), col(1), pl.BlockSpec((peers, 2, chunk), lambda i: (0, 0, i))],
        out_shape=[
            jax.ShapeDtypeStruct((span, half_width), F32),
            jax.ShapeDtypeStruct((span, half_width), F32),
            jax.ShapeDtypeStruct((1, half_width), F32),
            jax.ShapeDtypeStruct((peers, 2, half_width), F32),
        ],
        compiler_params=params(),
        cost_estimate=cost(40 * span * half_width, 16 * span * half_width),
        name="batch_norm_swish",
    )(scal, counts, stats, conv, cot, gain, shift)


def backward_kernel(scal, sums, scaled, grad, inv, gain, taps, value, gate, value_w, gate_w, mine, other, grad_conv, totals, plain, shifted, part):
    start, end, core = scal[0], scal[1], scal[2]
    rows, taps_n = value.shape[0], taps.shape[0]
    half = (taps_n - 1) // 2
    live_count = scal[3].astype(F32)
    both = sums[0]
    for peer in range(1, sums.shape[0]):
        both = both + sums[peer]
    totals[...] = both
    shift_sum, gain_sum = both[0:1], both[1:2]
    live = live_rows(start - EDGE, scaled.shape[0], end)
    through = live * (inv[...] * gain[...]) * (
        grad[...] - (shift_sum + scaled[...] * gain_sum) / live_count
    )
    rounded = through.astype(BF16)
    grad_conv[...] = rounded[EDGE : EDGE + rows]
    spread(plain, shifted, rounded.astype(F32))
    grad_glu = convolve(taps, shifted, [EDGE + half - tap for tap in range(taps_n)], rows, 16)
    grad_glu = (grad_glu * live_rows(start, rows, end)).astype(BF16).astype(F32)
    sig = gate[...]
    to_value = (grad_glu * sig).astype(BF16)
    to_gate = (grad_glu * value[...] * sig * (1.0 - sig)).astype(BF16)
    product = jnp.dot(to_value, value_w[...], preferred_element_type=F32) + jnp.dot(
        to_gate, gate_w[...], preferred_element_type=F32
    )
    step, last_step = pl.program_id(0), pl.num_programs(0) - 1

    @pl.when(step == 0)
    def _():
        part[...] = product

    @pl.when(step > 0)
    def _():
        part[...] += product

    @pl.when(step == last_step)
    def _():
        count = mine.shape[0]
        mine[...] = part[pl.ds(pl.multiple_of(core * count, count), count), :]
        other[...] = part[pl.ds(pl.multiple_of((1 - core) * count, count), count), :]


def backward(scal, sums, scaled, grad, inv, gain, taps, value, gate, weight):
    span, half_width = scaled.shape
    rows, width = value.shape[0], weight.shape[1]
    chunk = 256 if half_width % 256 == 0 else 128
    steps = half_width // chunk
    taps_n = taps.shape[0]
    col = lambda n: pl.BlockSpec((n, chunk), lambda i: (0, i))
    own = pl.BlockSpec((rows // 2, width), lambda i: (0, 0))
    return pl.pallas_call(
        backward_kernel,
        grid=(steps,),
        in_specs=[
            pl.BlockSpec(memory_space=pltpu.SMEM),
            pl.BlockSpec((sums.shape[0], 2, chunk), lambda i: (0, 0, i)),
            col(span),
            col(span),
            col(1),
            col(1),
            pl.BlockSpec((taps_n, 8, chunk), lambda i: (0, 0, i)),
            col(rows),
            col(rows),
            pl.BlockSpec((chunk, width), lambda i: (i, 0)),
            pl.BlockSpec((chunk, width), lambda i: (i + steps, 0)),
        ],
        out_specs=[own, own, col(rows), col(2)],
        out_shape=[
            jax.ShapeDtypeStruct((rows // 2, width), F32),
            jax.ShapeDtypeStruct((rows // 2, width), F32),
            jax.ShapeDtypeStruct((rows, half_width), BF16),
            jax.ShapeDtypeStruct((2, half_width), F32),
        ],
        scratch_shapes=[
            pltpu.VMEM((span, chunk), F32),
            pltpu.VMEM((8, span // 8 - 1, 8, chunk), F32),
            pltpu.VMEM((rows, width), F32),
        ],
        compiler_params=params(),
        cost_estimate=cost(2 * rows * width * 2 * half_width, 4 * half_width * width + 20 * span * half_width),
        name="grad_conv_project_back",
    )(scal, sums, scaled, grad, inv, gain, taps, value, gate, weight, weight)


def shifted_scratch(span):
    return [pltpu.VMEM((span, 128), F32), pltpu.VMEM((8, span // 8 - 1, 8, 128), F32)]


def tap_grad_kernel(taps_n, grad_conv, glu, out, plain, shifted):
    spread(plain, shifted, glu[...].astype(F32))
    first = HALO - (taps_n - 1) // 2
    out[...] = correlate(taps_n, grad_conv[...].astype(F32), shifted, first)


def tap_grad(taps_n, grad_conv, glu):
    rows, half_width = grad_conv.shape
    span = glu.shape[0]
    col = lambda n: pl.BlockSpec((n, 128), lambda i: (0, i))
    return pl.pallas_call(
        functools.partial(tap_grad_kernel, taps_n),
        grid=(half_width // 128,),
        in_specs=[col(rows), col(span)],
        out_specs=col(taps_n),
        out_shape=jax.ShapeDtypeStruct((taps_n, half_width), F32),
        scratch_shapes=shifted_scratch(span),
        compiler_params=params(),
        cost_estimate=cost(2 * taps_n * rows * half_width, 4 * span * half_width),
        name="tap_grad",
    )(grad_conv, glu)


def raw_taps_kernel(taps_n, scal, conv, glu, stats, alone, crossed, plain, shifted):
    start, end = scal[0], scal[1]
    rows, span = conv.shape[0] - 2 * EDGE, glu.shape[0]
    spread(plain, shifted, glu[...].astype(F32))
    first = HALO - (taps_n - 1) // 2
    live = live_rows(start, rows, end)
    local = stats[0, 0:1, :] / jnp.maximum(jnp.sum(live), 1.0)
    crossed[...] = correlate(taps_n, live * (conv[EDGE : EDGE + rows, :] - local), shifted, first)
    tap = lax.broadcasted_iota(jnp.int32, (taps_n, span), 0)
    at = lax.broadcasted_iota(jnp.int32, (taps_n, span), 1) - first - tap
    inside = (at >= 0) & (at < jnp.clip(end - start, 0, rows))
    alone[...] = jnp.dot(
        jnp.where(inside, 1.0, 0.0).astype(BF16), glu[...], preferred_element_type=F32
    )


def raw_taps(taps_n, scal, conv, glu, stats):
    rows, half_width = conv.shape
    span = glu.shape[0]
    col = lambda n: pl.BlockSpec((n, 128), lambda i: (0, i))
    return pl.pallas_call(
        functools.partial(raw_taps_kernel, taps_n),
        grid=(half_width // 128,),
        in_specs=[
            pl.BlockSpec(memory_space=pltpu.SMEM),
            col(rows),
            col(span),
            pl.BlockSpec((1, 2, 128), lambda i: (0, 0, i)),
        ],
        out_specs=[col(taps_n), col(taps_n)],
        out_shape=[jax.ShapeDtypeStruct((taps_n, half_width), F32)] * 2,
        scratch_shapes=shifted_scratch(span),
        compiler_params=params(),
        cost_estimate=cost(2 * taps_n * rows * half_width, 8 * span * half_width),
        name="raw_taps",
    )(scal, conv, glu, stats)


def halves(array):
    high = array.astype(BF16).astype(F32)
    return high, array - high


def last_kernel(taps_n, scal, counts, stats, conv, cot, gain, shift, glu, alone, crossed, local_stats, taps_before, out, factor_out, plain, shifted, pay):
    step = pl.program_id(0)
    scaled, grad, live, mean, inv = swish_grads(scal, counts, stats, conv, cot, gain, shift)
    rows = conv.shape[0] - 2 * EDGE
    spread(plain, shifted, glu[...].astype(F32))
    first = HALO - (taps_n - 1) // 2
    factor = inv * gain[...]
    factor_out[...] = factor
    own = grad[EDGE : EDGE + rows]
    direct = taps_before[...] + factor * correlate(taps_n, own, shifted, first)
    own_live = live[EDGE : EDGE + rows]
    local = local_stats[0, 0:1, :] / jnp.maximum(jnp.sum(own_live), 1.0)
    with_scaled = inv * (crossed[...] + (local - mean) * alone[...])
    sums = jnp.concatenate(
        [
            jnp.sum(own, axis=0, keepdims=True),
            jnp.sum(own * scaled[EDGE : EDGE + rows], axis=0, keepdims=True),
        ],
        axis=0,
    )
    pay[step] = jnp.concatenate([*halves(direct), with_scaled, alone[...], *halves(sums)], axis=0)

    @pl.when(step == pl.num_programs(0) - 1)
    def _():
        turned = jnp.concatenate([jnp.transpose(pay[s]) for s in range(pay.shape[0])], axis=0)
        block = out.shape[1]
        for index in range(out.shape[0]):
            out[index] = turned[index * block : (index + 1) * block].astype(BF16)


def last(taps_n, peers, scal, counts, stats, conv, cot, gain, shift, glu, alone, crossed, local_stats, taps_before):
    span, half_width = conv.shape
    chunk = 128
    steps = half_width // chunk
    pay = 4 * taps_n + 4
    col = lambda n: pl.BlockSpec((n, chunk), lambda i: (0, i))
    smem = pl.BlockSpec(memory_space=pltpu.SMEM)
    return pl.pallas_call(
        functools.partial(last_kernel, taps_n),
        grid=(steps,),
        in_specs=[
            smem,
            smem,
            pl.BlockSpec((stats.shape[0], 2, chunk), lambda i: (0, 0, i)),
            col(span),
            col(span),
            col(1),
            col(1),
            col(glu.shape[0]),
            col(taps_n),
            col(taps_n),
            pl.BlockSpec((1, 2, chunk), lambda i: (0, 0, i)),
            col(taps_n),
        ],
        out_specs=[pl.BlockSpec((peers, half_width // peers, pay), lambda i: (0, 0, 0)), col(1)],
        out_shape=[
            jax.ShapeDtypeStruct((peers, half_width // peers, pay), BF16),
            jax.ShapeDtypeStruct((1, half_width), F32),
        ],
        scratch_shapes=[*shifted_scratch(glu.shape[0]), pltpu.VMEM((steps, pay, chunk), F32)],
        compiler_params=params(),
        cost_estimate=cost(100 * span * half_width, 10 * span * half_width),
        name="batch_norm_swish_taps",
    )(scal, counts, stats, conv, cot, gain, shift, glu, alone, crossed, local_stats, taps_before)


def finish_kernel(taps_n, scal, received, known, taps_out, norm_out):
    total = received[0].astype(F32)
    for index in range(1, received.shape[0]):
        total = total + received[index].astype(F32)
    total = jnp.transpose(total)
    n = taps_n
    sums = total[4 * n : 4 * n + 2] + total[4 * n + 2 : 4 * n + 4]
    shift_sum, gain_sum = sums[0:1], sums[1:2]
    factor = known[0:1] / scal[3].astype(F32)
    taps_out[...] = (total[:n] + total[n : 2 * n]) - factor * (
        gain_sum * total[2 * n : 3 * n] + shift_sum * total[3 * n : 4 * n]
    )
    norm_out[...] = jnp.concatenate([gain_sum + known[2:3], shift_sum + known[1:2]], axis=0)


def finish(taps_n, scal, received, known):
    width = received.shape[1]
    vmem = pl.BlockSpec(memory_space=pltpu.VMEM)
    return pl.pallas_call(
        functools.partial(finish_kernel, taps_n),
        in_specs=[pl.BlockSpec(memory_space=pltpu.SMEM), vmem, vmem],
        out_shape=[
            jax.ShapeDtypeStruct((taps_n, width), F32),
            jax.ShapeDtypeStruct((2, width), F32),
        ],
        compiler_params=params(),
        name="finish",
    )(scal, received, known)


def direction_kernel(scal, mine, other, features, noise, out, edge, squares):
    rows = mine.shape[0]
    first = scal[0] + scal[2] * rows
    block = 32
    total = jnp.zeros((1, 128), F32)
    for row in range(0, rows, block):
        at = slice(row, row + block)
        live = live_rows(first + row, block, scal[1])
        summed = features[at].astype(F32) + noise_scale * noise[at].astype(F32) * live
        normed, inverse = normalize(summed)
        grad = mine[at] + other[at]
        moved = (
            live
            * inverse
            * (
                grad
                - jnp.mean(grad, axis=-1, keepdims=True)
                - normed * jnp.mean(grad * normed, axis=-1, keepdims=True)
            )
        )
        out[at] = moved
        total = total + jnp.sum(moved * moved)
    edge[...] = jnp.where(scal[2] == 0, out[:HALO], out[rows - HALO :])
    for peer in range(squares.shape[0]):
        squares[peer] = total


def direction(scal, mine, other, features, noise, peers):
    rows, width = mine.shape
    vmem = pl.BlockSpec(memory_space=pltpu.VMEM)
    return pl.pallas_call(
        direction_kernel,
        in_specs=[pl.BlockSpec(memory_space=pltpu.SMEM)] + [vmem] * 4,
        out_shape=[
            jax.ShapeDtypeStruct((rows, width), F32),
            jax.ShapeDtypeStruct((HALO, width), F32),
            jax.ShapeDtypeStruct((peers, 1, 128), F32),
        ],
        compiler_params=params(),
        cost_estimate=cost(30 * rows * width, 16 * rows * width),
        name="direction",
    )(scal, mine, other, features, noise)


def ascend_kernel(scal, squares, features, noise, mine, partner, near, far, own_noise, perturbation, normed_out):
    start, end, core = scal[0], scal[1], scal[2]
    rows, width = mine.shape
    total = squares[0]
    for index in range(1, squares.shape[0]):
        total = total + squares[index]
    total = total[0:1, 0:1]
    length = jnp.full((1, 1), 1.0, F32) * end.astype(F32)
    rate = ascent_rate * jnp.sqrt(length * width) / (jnp.sqrt(total) + ascent_epsilon)
    block = 32
    is_first = core == 0

    def place(row, moved):
        at = slice(row, row + block)
        live = live_rows(start - HALO + row, block, end)
        summed = features[at].astype(F32) + (noise_scale * noise[at].astype(F32) * live + moved * rate)
        normed_out[at] = normalize(summed)[0].astype(BF16)

    place(0, jnp.where(is_first, far[...], near[...]))
    for row in range(0, rows, block):
        at = slice(row, row + block)
        place(HALO + row, jnp.where(is_first, mine[at], partner[at]))
        place(HALO + rows + row, jnp.where(is_first, partner[at], mine[at]))
        live = live_rows(start + core * rows + row, block, end)
        perturbation[at] = noise_scale * own_noise[at].astype(F32) * live + mine[at] * rate
    place(HALO + 2 * rows, jnp.where(is_first, near[...], far[...]))


def ascend(scal, squares, features, noise, mine, partner, near, far, own_noise):
    vmem = pl.BlockSpec(memory_space=pltpu.VMEM)
    return pl.pallas_call(
        ascend_kernel,
        in_specs=[pl.BlockSpec(memory_space=pltpu.SMEM)] + [vmem] * 8,
        out_shape=[
            jax.ShapeDtypeStruct(mine.shape, F32),
            jax.ShapeDtypeStruct(features.shape, BF16),
        ],
        compiler_params=params(),
        cost_estimate=cost(30 * features.size, 8 * features.size),
        name="ascend",
    )(scal, squares, features, noise, mine, partner, near, far, own_noise)


def on_device(on_dp, features, start_noise, cotangent, in_weight, kernel, bn_gain, bn_shift, ends):
    rows, width = features.shape[1:]
    taps_n = kernel.shape[0]
    shards = lax.axis_size("tm")
    chips = shards // 2
    index = lax.axis_index("tm")
    group = lax.axis_index("dp")
    chip, core = index // 2, index % 2
    chip_rows = 2 * rows
    half_width = width // 2
    end = lax.dynamic_index_in_dim(ends, group, 0, keepdims=False)
    scal = jnp.stack([chip * chip_rows, end, core, jnp.sum(ends), chip % 4, chip // 4]).astype(jnp.int32)
    held = jnp.clip(
        ends[:, None] - chip_rows * jnp.arange(chips, dtype=jnp.int32)[None, :], 0, chip_rows
    ).reshape(-1).astype(F32)
    counts = jnp.stack([held, jnp.where(held > 0, 1.0 / jnp.maximum(held, 1.0), 0.0)])

    cores = [[2 * c + k for c in range(chips)] for k in range(2)]
    depth = chips // 4
    swap = [(i, i ^ 1) for i in range(shards)]
    swap_x = [(i, i ^ 2) for i in range(shards)]
    swap_y = [(i, i ^ 4) for i in range(shards)]
    near_pairs = [(2 * c, 2 * c - 2) for c in range(1, chips)] + [
        (2 * c + 1, 2 * c + 3) for c in range(chips - 1)
    ]
    far_pairs = [(2 * c, 2 * c - 1) for c in range(1, chips)] + [
        (2 * c + 1, 2 * c + 2) for c in range(chips - 1)
    ]
    first = core == 0

    def across(array, edge):
        return (
            lax.ppermute(array, "tm", swap),
            lax.ppermute(edge, "tm", near_pairs),
            lax.ppermute(edge, "tm", far_pairs),
        )

    def peers_of(array):
        array = lax.all_to_all(array, "tm", 0, 0, axis_index_groups=cores, tiled=True)
        if on_dp:
            array = lax.all_gather(array, "dp", axis=0, tiled=True)
        return array

    slice_width = width // shards
    pair = in_weight.reshape(2, slice_width, width)
    kept = lax.dynamic_index_in_dim(pair, core, 0, keepdims=False)
    given = lax.ppermute(lax.dynamic_index_in_dim(pair, 1 - core, 0, keepdims=False), "tm", swap)
    block = jnp.concatenate([jnp.where(first, kept, given), jnp.where(first, given, kept)], axis=0)
    shifts = [(0,)] + [(k, depth - k) if 2 * k < depth else (k,) for k in range(1, depth // 2 + 1)]
    forth = [(i, (i + 8) % shards) for i in range(shards)]
    back = [(i, (i - 8) % shards) for i in range(shards)]
    corner = [(i, i ^ (4 if i % 2 else 2)) for i in range(shards)]
    def mine_of(array):
        parts = array.reshape(array.shape[0], chips, 2, slice_width)
        return lax.dynamic_index_in_dim(parts, core, 2, keepdims=False).reshape(-1, half_width)

    def prepare_first():
        own_ids = chip * chip_rows + core * rows + jnp.arange(rows, dtype=jnp.int32)
        own_live = (own_ids < end).astype(F32)[:, None]
        summed = features[0].astype(F32) + noise_scale * start_noise[0].astype(F32) * own_live
        return [normalize(summed)[0].astype(BF16)]

    def prepare_second():
        channel = mine_of(jnp.concatenate([kernel, bn_gain[None], bn_shift[None]], axis=0))
        taps = jnp.broadcast_to(channel[:taps_n, None], (taps_n, 8, half_width))
        return [taps, channel[taps_n : taps_n + 1], channel[taps_n + 1 :], counts, scal]

    def assemble(own, partner, near, far):
        return jnp.concatenate(
            [
                jnp.where(first, far, near),
                jnp.where(first, own, partner),
                jnp.where(first, partner, own),
                jnp.where(first, near, far),
            ],
            axis=0,
        )

    along = {0: block, depth: block}
    kinds, pieces = [], []
    cot_own = cotangent[0]
    final = len(shifts) - 1
    for number, group in enumerate(shifts):
        blocks = jnp.concatenate([along[k] for k in group], axis=0)
        kinds.append((group, 0))
        pieces.append(blocks)
        sent = [lax.ppermute(blocks, "tm", swap_x), lax.ppermute(blocks, "tm", swap_y)]
        sent_kinds = [(group, 1), (group, 2)]
        if number:
            sent.append(lax.ppermute(relayed, "tm", corner))
            sent_kinds.append((shifts[number - 1], 3))
        onward = shifts[number + 1] if number < final else ()
        for k in onward:
            from_before = 2 * k <= depth
            sent.append(lax.ppermute(along[k - 1 if from_before else k + 1], "tm", forth if from_before else back))
        beside = []
        if number == 0:
            beside = prepare_first()
        elif number == 1:
            both = jnp.stack([normed_own, cot_own])
            edge = jnp.concatenate(
                [
                    jnp.where(first, normed_own[:HALO], normed_own[rows - HALO :]),
                    jnp.where(first, cot_own[:EDGE], cot_own[rows - EDGE :]),
                ],
                axis=0,
            )
            beside = [*across(both, edge), *prepare_second()]
        if number == final:
            (partner, near, far), ready = (beside or crossing)[:3], beside[3:]
            beside = [
                assemble(normed_own, partner[0], near[:HALO], far[:HALO]),
                assemble(cot_own, partner[1], near[HALO:], far[HALO:]),
                place(scal, kinds, pieces, block.shape[0], chips),
                *ready,
            ]
        sent, beside = lax.optimization_barrier((sent, beside))
        relayed = jnp.where(first, sent[1], sent[0])
        if number == 0:
            (normed_own,) = beside
        elif number == 1:
            crossing, (taps, gain, shift, counts, scal) = beside[:3], beside[3:8]
        if number == final:
            normed_b, wide_cot, weight = beside[:3]
            late_kinds, late_pieces = sent_kinds, sent
        else:
            kinds += sent_kinds
            pieces += sent[: len(sent_kinds)]
            for k, arrived in zip(onward, sent[len(sent_kinds) :]):
                along[k] = arrived
    late_kinds.append((shifts[final], 3))
    late_pieces.append(lax.ppermute(relayed, "tm", corner))
    weight = place_late(scal, late_kinds, late_pieces, block.shape[0], weight)

    place_of = jnp.arange(half_width, dtype=jnp.int32)
    source = (2 * (place_of // slice_width) + core) * slice_width + place_of % slice_width
    chosen = (jnp.arange(width, dtype=jnp.int32)[:, None] == source[None, :]).astype(BF16)
    cot = jnp.dot(wide_cot, chosen, preferred_element_type=F32).astype(BF16)

    value, gate, glu, conv, stats = forward(
        scal, normed_b, weight, taps, chip_rows, chips, True
    )
    gathered, base = peers_of(stats), jnp.stack([features[0], start_noise[0]])
    base, _ = lax.optimization_barrier((base, stats))
    partner, near, far = across(base, jnp.where(first, base[:, :HALO], base[:, rows - HALO :]))
    wide_features, wide_noise = (
        assemble(base[n], partner[n], near[n], far[n]) for n in range(2)
    )
    scaled, grad, inv, sums = batch(scal, counts, gathered, conv, cot, gain, shift, chips)
    sums, wide_features, wide_noise = lax.optimization_barrier((sums, wide_features, wide_noise))
    mine, other, grad_conv, totals = backward(
        scal, peers_of(sums), scaled, grad, inv, gain, taps, value, gate, weight
    )
    other = lax.ppermute(other, "tm", swap)
    moved, edge, squares = direction(scal, mine, other, features[0], start_noise[0], shards)
    squares = lax.all_to_all(squares, "tm", 0, 0, tiled=True)
    partner, near, far = across(moved, edge)
    taps_before = tap_grad(taps_n, grad_conv, glu)
    squares, taps_before = lax.optimization_barrier((squares, taps_before))
    perturbation, normed_b = ascend(
        scal, squares, wide_features, wide_noise, moved, partner, near, far, start_noise[0]
    )

    glu, conv, stats = forward(scal, normed_b, weight, taps, chip_rows, chips, False)
    alone, crossed = raw_taps(taps_n, scal, conv, glu, stats)
    outgoing, factor = last(
        taps_n, chips, scal, counts, peers_of(stats), conv, cot, gain, shift, glu, alone, crossed, stats, taps_before
    )
    received = peers_of(outgoing)
    known = jnp.concatenate([factor, totals], axis=0)
    known = lax.dynamic_slice_in_dim(known, chip * slice_width, slice_width, 1)
    kernel_total, norm_total = finish(taps_n, scal, received, known)
    return (perturbation[None], kernel_total, norm_total)


def solution(mesh):
    return jax.shard_map(
        functools.partial(on_device, mesh.shape["dp"] > 1),
        mesh=mesh,
        in_specs=(
            P("dp", "tm", None),
            P("dp", "tm", None),
            P("dp", "tm", None),
            P("tm", None),
            P(),
            P(),
            P(),
            P(),
        ),
        out_specs=(P("dp", "tm", None), P(None, "tm"), P(None, "tm")),
        check_vma=False,
    )
```

```python
import functools

import jax
import jax.numpy as jnp
from jax import lax
from jax.experimental import pallas as pl
from jax.experimental.pallas import tpu as pltpu
from jax.sharding import PartitionSpec as P

ASCENT = 2

noise_scale = 0.5
ascent_rate = 0.5
layer_epsilon = 1e-05
batch_epsilon = 1e-05
ascent_epsilon = 1e-06

HALO = 32
EDGE = 16
F32 = jnp.float32
BF16 = jnp.bfloat16


def params(limit=56 * 1024 * 1024):
    return pltpu.CompilerParams(vmem_limit_bytes=limit)


def cost(flops, nbytes):
    return pl.CostEstimate(flops=int(flops), bytes_accessed=int(nbytes), transcendentals=0)


def normalize(summed):
    centre = summed - jnp.mean(summed, axis=-1, keepdims=True)
    inverse = lax.rsqrt(jnp.mean(centre * centre, axis=-1, keepdims=True) + layer_epsilon)
    return (centre * inverse, inverse)


def live_rows(first, rows, end):
    ids = first + lax.broadcasted_iota(jnp.int32, (rows, 1), 0)
    return jnp.where((ids >= 0) & (ids < end), 1.0, 0.0).astype(F32)


def spread(plain, shifted, array):
    plain[...] = array
    rows, tiles = shifted.shape[1] * 8, shifted.shape[1]
    for s in range(8):
        shifted[s] = plain[s : s + rows].reshape(tiles, 8, -1)


def tiles_at(shifted, row, tiles, lanes):
    first = (row - row % 8) // 8
    return shifted[row % 8, first : first + tiles, :, lanes]


def convolve(taps, shifted, offsets, rows, most):
    most = max(n for n in range(1, most + 1) if rows // 8 % n == 0)
    columns = []
    for lane in range(0, taps.shape[2], 128):
        lanes = slice(lane, lane + 128)
        parts = []
        for tile in range(0, rows // 8, most):
            total = jnp.zeros((most, 8, 128), F32)
            for tap, offset in enumerate(offsets):
                total = total + taps[tap, :, lanes][None] * tiles_at(
                    shifted, offset + 8 * tile, most, lanes
                )
            parts.append(total.reshape(most * 8, 128))
        columns.append(jnp.concatenate(parts, axis=0))
    return jnp.concatenate(columns, axis=1)


def correlate(taps_n, left, shifted, first):
    rows = left.shape[0]
    lanes = slice(0, 128)
    most = 16
    totals = [None] * taps_n
    for tile in range(0, rows // 8, most):
        part = left[8 * tile : 8 * (tile + most)].reshape(most, 8, 128)
        for tap in range(taps_n):
            product = jnp.sum(
                part * tiles_at(shifted, first + tap + 8 * tile, most, lanes), axis=0, keepdims=True
            )
            totals[tap] = product if totals[tap] is None else totals[tap] + product
    return jnp.sum(jnp.concatenate(totals, axis=0), axis=1)


def block_row(scal, size, depth, shift, other):
    chip = lax.rem(scal[5] - shift + depth, depth) * 4 + (scal[4] ^ other)
    return pl.multiple_of(chip * size, 16)


def place_kernel(kinds, size, scal, *refs):
    pieces, out = refs[:-1], refs[-1]
    depth = out.shape[0] // (4 * size)
    for (group, other), ref in zip(kinds, pieces):
        for nth, shift in enumerate(group):
            row = block_row(scal, size, depth, shift, other)
            out[pl.ds(row, size), :] = ref[nth * size : (nth + 1) * size, :]


def place_late_kernel(kinds, size, scal, *refs):
    pieces, out, sems = refs[: len(kinds)], refs[-2], refs[-1]
    depth = out.shape[0] // (4 * size)
    copies = []
    for (group, other), ref in zip(kinds, pieces):
        for nth, shift in enumerate(group):
            row = block_row(scal, size, depth, shift, other)
            copies.append(
                pltpu.make_async_copy(
                    ref.at[pl.ds(nth * size, size), :],
                    out.at[pl.ds(row, size), :],
                    sems.at[len(copies)],
                )
            )
    for copy in copies:
        copy.start()
    for copy in copies:
        copy.wait()


def place(scal, kinds, pieces, size, chips):
    width = pieces[0].shape[1]
    vmem = pl.BlockSpec(memory_space=pltpu.VMEM)
    return pl.pallas_call(
        functools.partial(place_kernel, kinds, size),
        in_specs=[pl.BlockSpec(memory_space=pltpu.SMEM)] + [vmem] * len(pieces),
        out_specs=vmem,
        out_shape=jax.ShapeDtypeStruct((chips * size, width), BF16),
        compiler_params=params(),
        cost_estimate=cost(0, 4 * chips * size * width),
        name="place_weights",
    )(scal, *pieces)


def place_late(scal, kinds, pieces, size, weight):
    count = sum(len(group) for group, _ in kinds)
    vmem = pl.BlockSpec(memory_space=pltpu.VMEM)
    hbm = pl.BlockSpec(memory_space=pl.ANY)
    return pl.pallas_call(
        functools.partial(place_late_kernel, kinds, size),
        in_specs=[pl.BlockSpec(memory_space=pltpu.SMEM)] + [vmem] * len(pieces) + [hbm],
        out_specs=hbm,
        out_shape=jax.ShapeDtypeStruct(weight.shape, BF16),
        scratch_shapes=[pltpu.SemaphoreType.DMA((count,))],
        input_output_aliases={len(pieces) + 1: 0},
        compiler_params=params(),
        cost_estimate=cost(0, 4 * count * size * weight.shape[1]),
        name="place_last_weights",
    )(scal, *pieces, weight)


def forward_kernel(keep, scal, nb, value_w, gate_w, taps, *refs):
    kept, (glu, conv, stats, plain, shifted) = refs[: 2 * keep], refs[2 * keep :]
    start, end = scal[0], scal[1]
    span, taps_n = nb.shape[0], taps.shape[0]
    rows = conv.shape[0] - 2 * EDGE
    contract = (((1,), (1,)), ((), ()))
    v = lax.dot_general(nb[...], value_w[...], contract, preferred_element_type=F32)
    s = jax.nn.sigmoid(lax.dot_general(nb[...], gate_w[...], contract, preferred_element_type=F32))
    if keep:
        kept[0][...] = v[HALO : HALO + rows]
        kept[1][...] = s[HALO : HALO + rows]
    gated = (v * s * live_rows(start - HALO, span, end)).astype(BF16)
    glu[...] = gated
    spread(plain, shifted, gated.astype(F32))
    shift = HALO - EDGE - (taps_n - 1) // 2
    conv[...] = convolve(taps, shifted, [shift + tap for tap in range(taps_n)], conv.shape[0], 12)
    live = live_rows(start, rows, end)
    own = conv[EDGE : EDGE + rows, :]
    mass = jnp.sum(live * own, axis=0, keepdims=True)
    centre = live * (own - mass / jnp.maximum(jnp.sum(live), 1.0))
    both = jnp.concatenate([mass, jnp.sum(centre * centre, axis=0, keepdims=True)], axis=0)
    for peer in range(stats.shape[0]):
        stats[peer] = both


def forward(scal, nb, weight, taps, rows, peers, keep):
    span, width = nb.shape
    taps_n, _, half_width = taps.shape
    chunk = 256 if half_width % 256 == 0 else 128
    steps = half_width // chunk
    col = lambda n: pl.BlockSpec((n, chunk), lambda i: (0, i))
    return pl.pallas_call(
        functools.partial(forward_kernel, keep),
        grid=(steps,),
        in_specs=[
            pl.BlockSpec(memory_space=pltpu.SMEM),
            pl.BlockSpec((span, width), lambda i: (0, 0)),
            pl.BlockSpec((chunk, width), lambda i: (i, 0)),
            pl.BlockSpec((chunk, width), lambda i: (i + steps, 0)),
            pl.BlockSpec((taps_n, 8, chunk), lambda i: (0, 0, i)),
        ],
        out_specs=[
            *([col(rows)] * (2 * keep)),
            col(span),
            col(rows + 2 * EDGE),
            pl.BlockSpec((peers, 2, chunk), lambda i: (0, 0, i)),
        ],
        out_shape=[
            *([jax.ShapeDtypeStruct((rows, half_width), F32)] * (2 * keep)),
            jax.ShapeDtypeStruct((span, half_width), BF16),
            jax.ShapeDtypeStruct((rows + 2 * EDGE, half_width), F32),
            jax.ShapeDtypeStruct((peers, 2, half_width), F32),
        ],
        scratch_shapes=[
            pltpu.VMEM((span, chunk), F32),
            pltpu.VMEM((8, span // 8 - 1, 8, chunk), F32),
        ],
        compiler_params=params(),
        cost_estimate=cost(2 * span * width * 2 * half_width, 4 * half_width * width + 10 * span * half_width),
        name="project_glu_conv",
    )(scal, nb, weight, weight, taps)


def moments(counts, stats, live_count):
    mass = stats[0, 0:1, :]
    square = stats[0, 1:2, :]
    for peer in range(1, stats.shape[0]):
        mass = mass + stats[peer, 0:1, :]
        square = square + stats[peer, 1:2, :]
    mean = mass / live_count
    for peer in range(stats.shape[0]):
        off = stats[peer, 0:1, :] - counts[0, peer] * mean
        square = square + off * off * counts[1, peer]
    return mean, lax.rsqrt(square / live_count + batch_epsilon)


def swish_grads(scal, counts, stats, conv, cot, gain, shift):
    start, end = scal[0], scal[1]
    live_count = scal[3].astype(F32)
    mean, inv = moments(counts, stats, live_count)
    scaled = (conv[...] - mean) * inv
    pre = gain[...] * scaled + shift[...]
    sig = jax.nn.sigmoid(pre)
    live = live_rows(start - EDGE, conv.shape[0], end)
    upstream = live * cot[...].astype(F32) / ASCENT
    return scaled, upstream * sig * (1.0 + pre * (1.0 - sig)), live, mean, inv


def batch_kernel(scal, counts, stats, conv, cot, gain, shift, scaled_out, grad_out, inv_out, sums):
    scaled, grad, live, mean, inv = swish_grads(scal, counts, stats, conv, cot, gain, shift)
    scaled_out[...] = scaled
    grad_out[...] = grad
    inv_out[...] = inv
    rows = conv.shape[0] - 2 * EDGE
    own = grad[EDGE : EDGE + rows]
    both = jnp.concatenate(
        [
            jnp.sum(own, axis=0, keepdims=True),
            jnp.sum(own * scaled[EDGE : EDGE + rows], axis=0, keepdims=True),
        ],
        axis=0,
    )
    for peer in range(sums.shape[0]):
        sums[peer] = both


def batch(scal, counts, stats, conv, cot, gain, shift, peers):
    span, half_width = conv.shape
    chunk = 256 if half_width % 256 == 0 else 128
    col = lambda n: pl.BlockSpec((n, chunk), lambda i: (0, i))
    smem = pl.BlockSpec(memory_space=pltpu.SMEM)
    return pl.pallas_call(
        batch_kernel,
        grid=(half_width // chunk,),
        in_specs=[
            smem,
            smem,
            pl.BlockSpec((stats.shape[0], 2, chunk), lambda i: (0, 0, i)),
            col(span),
            col(span),
            col(1),
            col(1),
        ],
        out_specs=[col(span), col(span), col(1), pl.BlockSpec((peers, 2, chunk), lambda i: (0, 0, i))],
        out_shape=[
            jax.ShapeDtypeStruct((span, half_width), F32),
            jax.ShapeDtypeStruct((span, half_width), F32),
            jax.ShapeDtypeStruct((1, half_width), F32),
            jax.ShapeDtypeStruct((peers, 2, half_width), F32),
        ],
        compiler_params=params(),
        cost_estimate=cost(40 * span * half_width, 16 * span * half_width),
        name="batch_norm_swish",
    )(scal, counts, stats, conv, cot, gain, shift)


def backward_kernel(scal, sums, scaled, grad, inv, gain, taps, value, gate, value_w, gate_w, mine, other, grad_conv, totals, plain, shifted, part):
    start, end, core = scal[0], scal[1], scal[2]
    rows, taps_n = value.shape[0], taps.shape[0]
    half = (taps_n - 1) // 2
    live_count = scal[3].astype(F32)
    both = sums[0]
    for peer in range(1, sums.shape[0]):
        both = both + sums[peer]
    totals[...] = both
    shift_sum, gain_sum = both[0:1], both[1:2]
    live = live_rows(start - EDGE, scaled.shape[0], end)
    through = live * (inv[...] * gain[...]) * (
        grad[...] - (shift_sum + scaled[...] * gain_sum) / live_count
    )
    rounded = through.astype(BF16)
    grad_conv[...] = rounded[EDGE : EDGE + rows]
    spread(plain, shifted, rounded.astype(F32))
    grad_glu = convolve(taps, shifted, [EDGE + half - tap for tap in range(taps_n)], rows, 16)
    grad_glu = (grad_glu * live_rows(start, rows, end)).astype(BF16).astype(F32)
    sig = gate[...]
    to_value = (grad_glu * sig).astype(BF16)
    to_gate = (grad_glu * value[...] * sig * (1.0 - sig)).astype(BF16)
    product = jnp.dot(to_value, value_w[...], preferred_element_type=F32) + jnp.dot(
        to_gate, gate_w[...], preferred_element_type=F32
    )
    step, last_step = pl.program_id(0), pl.num_programs(0) - 1

    @pl.when(step == 0)
    def _():
        part[...] = product

    @pl.when(step > 0)
    def _():
        part[...] += product

    @pl.when(step == last_step)
    def _():
        count = mine.shape[0]
        mine[...] = part[pl.ds(pl.multiple_of(core * count, count), count), :]
        other[...] = part[pl.ds(pl.multiple_of((1 - core) * count, count), count), :]


def backward(scal, sums, scaled, grad, inv, gain, taps, value, gate, weight):
    span, half_width = scaled.shape
    rows, width = value.shape[0], weight.shape[1]
    chunk = 256 if half_width % 256 == 0 else 128
    steps = half_width // chunk
    taps_n = taps.shape[0]
    col = lambda n: pl.BlockSpec((n, chunk), lambda i: (0, i))
    own = pl.BlockSpec((rows // 2, width), lambda i: (0, 0))
    return pl.pallas_call(
        backward_kernel,
        grid=(steps,),
        in_specs=[
            pl.BlockSpec(memory_space=pltpu.SMEM),
            pl.BlockSpec((sums.shape[0], 2, chunk), lambda i: (0, 0, i)),
            col(span),
            col(span),
            col(1),
            col(1),
            pl.BlockSpec((taps_n, 8, chunk), lambda i: (0, 0, i)),
            col(rows),
            col(rows),
            pl.BlockSpec((chunk, width), lambda i: (i, 0)),
            pl.BlockSpec((chunk, width), lambda i: (i + steps, 0)),
        ],
        out_specs=[own, own, col(rows), col(2)],
        out_shape=[
            jax.ShapeDtypeStruct((rows // 2, width), F32),
            jax.ShapeDtypeStruct((rows // 2, width), F32),
            jax.ShapeDtypeStruct((rows, half_width), BF16),
            jax.ShapeDtypeStruct((2, half_width), F32),
        ],
        scratch_shapes=[
            pltpu.VMEM((span, chunk), F32),
            pltpu.VMEM((8, span // 8 - 1, 8, chunk), F32),
            pltpu.VMEM((rows, width), F32),
        ],
        compiler_params=params(),
        cost_estimate=cost(2 * rows * width * 2 * half_width, 4 * half_width * width + 20 * span * half_width),
        name="grad_conv_project_back",
    )(scal, sums, scaled, grad, inv, gain, taps, value, gate, weight, weight)


def shifted_scratch(span):
    return [pltpu.VMEM((span, 128), F32), pltpu.VMEM((8, span // 8 - 1, 8, 128), F32)]


def tap_grad_kernel(taps_n, grad_conv, glu, out, plain, shifted):
    spread(plain, shifted, glu[...].astype(F32))
    first = HALO - (taps_n - 1) // 2
    out[...] = correlate(taps_n, grad_conv[...].astype(F32), shifted, first)


def tap_grad(taps_n, grad_conv, glu):
    rows, half_width = grad_conv.shape
    span = glu.shape[0]
    col = lambda n: pl.BlockSpec((n, 128), lambda i: (0, i))
    return pl.pallas_call(
        functools.partial(tap_grad_kernel, taps_n),
        grid=(half_width // 128,),
        in_specs=[col(rows), col(span)],
        out_specs=col(taps_n),
        out_shape=jax.ShapeDtypeStruct((taps_n, half_width), F32),
        scratch_shapes=shifted_scratch(span),
        compiler_params=params(),
        cost_estimate=cost(2 * taps_n * rows * half_width, 4 * span * half_width),
        name="tap_grad",
    )(grad_conv, glu)


def raw_taps_kernel(taps_n, scal, conv, glu, stats, alone, crossed, plain, shifted):
    start, end = scal[0], scal[1]
    rows, span = conv.shape[0] - 2 * EDGE, glu.shape[0]
    spread(plain, shifted, glu[...].astype(F32))
    first = HALO - (taps_n - 1) // 2
    live = live_rows(start, rows, end)
    local = stats[0, 0:1, :] / jnp.maximum(jnp.sum(live), 1.0)
    crossed[...] = correlate(taps_n, live * (conv[EDGE : EDGE + rows, :] - local), shifted, first)
    tap = lax.broadcasted_iota(jnp.int32, (taps_n, span), 0)
    at = lax.broadcasted_iota(jnp.int32, (taps_n, span), 1) - first - tap
    inside = (at >= 0) & (at < jnp.clip(end - start, 0, rows))
    alone[...] = jnp.dot(
        jnp.where(inside, 1.0, 0.0).astype(BF16), glu[...], preferred_element_type=F32
    )


def raw_taps(taps_n, scal, conv, glu, stats):
    rows, half_width = conv.shape
    span = glu.shape[0]
    col = lambda n: pl.BlockSpec((n, 128), lambda i: (0, i))
    return pl.pallas_call(
        functools.partial(raw_taps_kernel, taps_n),
        grid=(half_width // 128,),
        in_specs=[
            pl.BlockSpec(memory_space=pltpu.SMEM),
            col(rows),
            col(span),
            pl.BlockSpec((1, 2, 128), lambda i: (0, 0, i)),
        ],
        out_specs=[col(taps_n), col(taps_n)],
        out_shape=[jax.ShapeDtypeStruct((taps_n, half_width), F32)] * 2,
        scratch_shapes=shifted_scratch(span),
        compiler_params=params(),
        cost_estimate=cost(2 * taps_n * rows * half_width, 8 * span * half_width),
        name="raw_taps",
    )(scal, conv, glu, stats)


def halves(array):
    high = array.astype(BF16).astype(F32)
    return high, array - high


def last_kernel(taps_n, scal, counts, stats, conv, cot, gain, shift, glu, alone, crossed, local_stats, taps_before, out, factor_out, plain, shifted, pay):
    step = pl.program_id(0)
    scaled, grad, live, mean, inv = swish_grads(scal, counts, stats, conv, cot, gain, shift)
    rows = conv.shape[0] - 2 * EDGE
    spread(plain, shifted, glu[...].astype(F32))
    first = HALO - (taps_n - 1) // 2
    factor = inv * gain[...]
    factor_out[...] = factor
    own = grad[EDGE : EDGE + rows]
    direct = taps_before[...] + factor * correlate(taps_n, own, shifted, first)
    own_live = live[EDGE : EDGE + rows]
    local = local_stats[0, 0:1, :] / jnp.maximum(jnp.sum(own_live), 1.0)
    with_scaled = inv * (crossed[...] + (local - mean) * alone[...])
    sums = jnp.concatenate(
        [
            jnp.sum(own, axis=0, keepdims=True),
            jnp.sum(own * scaled[EDGE : EDGE + rows], axis=0, keepdims=True),
        ],
        axis=0,
    )
    pay[step] = jnp.concatenate([*halves(direct), with_scaled, alone[...], *halves(sums)], axis=0)

    @pl.when(step == pl.num_programs(0) - 1)
    def _():
        turned = jnp.concatenate([jnp.transpose(pay[s]) for s in range(pay.shape[0])], axis=0)
        block = out.shape[1]
        for index in range(out.shape[0]):
            out[index] = turned[index * block : (index + 1) * block].astype(BF16)


def last(taps_n, peers, scal, counts, stats, conv, cot, gain, shift, glu, alone, crossed, local_stats, taps_before):
    span, half_width = conv.shape
    chunk = 128
    steps = half_width // chunk
    pay = 4 * taps_n + 4
    col = lambda n: pl.BlockSpec((n, chunk), lambda i: (0, i))
    smem = pl.BlockSpec(memory_space=pltpu.SMEM)
    return pl.pallas_call(
        functools.partial(last_kernel, taps_n),
        grid=(steps,),
        in_specs=[
            smem,
            smem,
            pl.BlockSpec((stats.shape[0], 2, chunk), lambda i: (0, 0, i)),
            col(span),
            col(span),
            col(1),
            col(1),
            col(glu.shape[0]),
            col(taps_n),
            col(taps_n),
            pl.BlockSpec((1, 2, chunk), lambda i: (0, 0, i)),
            col(taps_n),
        ],
        out_specs=[pl.BlockSpec((peers, half_width // peers, pay), lambda i: (0, 0, 0)), col(1)],
        out_shape=[
            jax.ShapeDtypeStruct((peers, half_width // peers, pay), BF16),
            jax.ShapeDtypeStruct((1, half_width), F32),
        ],
        scratch_shapes=[*shifted_scratch(glu.shape[0]), pltpu.VMEM((steps, pay, chunk), F32)],
        compiler_params=params(),
        cost_estimate=cost(100 * span * half_width, 10 * span * half_width),
        name="batch_norm_swish_taps",
    )(scal, counts, stats, conv, cot, gain, shift, glu, alone, crossed, local_stats, taps_before)


def finish_kernel(taps_n, scal, received, known, taps_out, norm_out):
    total = received[0].astype(F32)
    for index in range(1, received.shape[0]):
        total = total + received[index].astype(F32)
    total = jnp.transpose(total)
    n = taps_n
    sums = total[4 * n : 4 * n + 2] + total[4 * n + 2 : 4 * n + 4]
    shift_sum, gain_sum = sums[0:1], sums[1:2]
    factor = known[0:1] / scal[3].astype(F32)
    taps_out[...] = (total[:n] + total[n : 2 * n]) - factor * (
        gain_sum * total[2 * n : 3 * n] + shift_sum * total[3 * n : 4 * n]
    )
    norm_out[...] = jnp.concatenate([gain_sum + known[2:3], shift_sum + known[1:2]], axis=0)


def finish(taps_n, scal, received, known):
    width = received.shape[1]
    vmem = pl.BlockSpec(memory_space=pltpu.VMEM)
    return pl.pallas_call(
        functools.partial(finish_kernel, taps_n),
        in_specs=[pl.BlockSpec(memory_space=pltpu.SMEM), vmem, vmem],
        out_shape=[
            jax.ShapeDtypeStruct((taps_n, width), F32),
            jax.ShapeDtypeStruct((2, width), F32),
        ],
        compiler_params=params(),
        name="finish",
    )(scal, received, known)


def direction_kernel(scal, mine, other, features, noise, out, edge, squares):
    rows = mine.shape[0]
    first = scal[0] + scal[2] * rows
    block = 32
    total = jnp.zeros((1, 128), F32)
    for row in range(0, rows, block):
        at = slice(row, row + block)
        live = live_rows(first + row, block, scal[1])
        summed = features[at].astype(F32) + noise_scale * noise[at].astype(F32) * live
        normed, inverse = normalize(summed)
        grad = mine[at] + other[at]
        moved = (
            live
            * inverse
            * (
                grad
                - jnp.mean(grad, axis=-1, keepdims=True)
                - normed * jnp.mean(grad * normed, axis=-1, keepdims=True)
            )
        )
        out[at] = moved
        total = total + jnp.sum(moved * moved)
    edge[...] = jnp.where(scal[2] == 0, out[:HALO], out[rows - HALO :])
    for peer in range(squares.shape[0]):
        squares[peer] = total


def direction(scal, mine, other, features, noise, peers):
    rows, width = mine.shape
    vmem = pl.BlockSpec(memory_space=pltpu.VMEM)
    return pl.pallas_call(
        direction_kernel,
        in_specs=[pl.BlockSpec(memory_space=pltpu.SMEM)] + [vmem] * 4,
        out_shape=[
            jax.ShapeDtypeStruct((rows, width), F32),
            jax.ShapeDtypeStruct((HALO, width), F32),
            jax.ShapeDtypeStruct((peers, 1, 128), F32),
        ],
        compiler_params=params(),
        cost_estimate=cost(30 * rows * width, 16 * rows * width),
        name="direction",
    )(scal, mine, other, features, noise)


def ascend_kernel(scal, squares, features, noise, mine, partner, near, far, own_noise, perturbation, normed_out):
    start, end, core = scal[0], scal[1], scal[2]
    rows, width = mine.shape
    total = squares[0]
    for index in range(1, squares.shape[0]):
        total = total + squares[index]
    total = total[0:1, 0:1]
    length = jnp.full((1, 1), 1.0, F32) * end.astype(F32)
    rate = ascent_rate * jnp.sqrt(length * width) / (jnp.sqrt(total) + ascent_epsilon)
    block = 32
    is_first = core == 0

    def place(row, moved):
        at = slice(row, row + block)
        live = live_rows(start - HALO + row, block, end)
        summed = features[at].astype(F32) + (noise_scale * noise[at].astype(F32) * live + moved * rate)
        normed_out[at] = normalize(summed)[0].astype(BF16)

    place(0, jnp.where(is_first, far[...], near[...]))
    for row in range(0, rows, block):
        at = slice(row, row + block)
        place(HALO + row, jnp.where(is_first, mine[at], partner[at]))
        place(HALO + rows + row, jnp.where(is_first, partner[at], mine[at]))
        live = live_rows(start + core * rows + row, block, end)
        perturbation[at] = noise_scale * own_noise[at].astype(F32) * live + mine[at] * rate
    place(HALO + 2 * rows, jnp.where(is_first, near[...], far[...]))


def ascend(scal, squares, features, noise, mine, partner, near, far, own_noise):
    vmem = pl.BlockSpec(memory_space=pltpu.VMEM)
    return pl.pallas_call(
        ascend_kernel,
        in_specs=[pl.BlockSpec(memory_space=pltpu.SMEM)] + [vmem] * 8,
        out_shape=[
            jax.ShapeDtypeStruct(mine.shape, F32),
            jax.ShapeDtypeStruct(features.shape, BF16),
        ],
        compiler_params=params(),
        cost_estimate=cost(30 * features.size, 8 * features.size),
        name="ascend",
    )(scal, squares, features, noise, mine, partner, near, far, own_noise)


def on_device(on_dp, features, start_noise, cotangent, in_weight, kernel, bn_gain, bn_shift, ends):
    rows, width = features.shape[1:]
    taps_n = kernel.shape[0]
    shards = lax.axis_size("tm")
    chips = shards // 2
    index = lax.axis_index("tm")
    group = lax.axis_index("dp")
    chip, core = index // 2, index % 2
    chip_rows = 2 * rows
    half_width = width // 2
    end = lax.dynamic_index_in_dim(ends, group, 0, keepdims=False)
    scal = jnp.stack([chip * chip_rows, end, core, jnp.sum(ends), chip % 4, chip // 4]).astype(jnp.int32)
    held = jnp.clip(
        ends[:, None] - chip_rows * jnp.arange(chips, dtype=jnp.int32)[None, :], 0, chip_rows
    ).reshape(-1).astype(F32)
    counts = jnp.stack([held, jnp.where(held > 0, 1.0 / jnp.maximum(held, 1.0), 0.0)])

    cores = [[2 * c + k for c in range(chips)] for k in range(2)]
    depth = chips // 4
    swap = [(i, i ^ 1) for i in range(shards)]
    swap_x = [(i, i ^ 2) for i in range(shards)]
    swap_y = [(i, i ^ 4) for i in range(shards)]
    near_pairs = [(2 * c, 2 * c - 2) for c in range(1, chips)] + [
        (2 * c + 1, 2 * c + 3) for c in range(chips - 1)
    ]
    far_pairs = [(2 * c, 2 * c - 1) for c in range(1, chips)] + [
        (2 * c + 1, 2 * c + 2) for c in range(chips - 1)
    ]
    first = core == 0

    def across(array, edge):
        return (
            lax.ppermute(array, "tm", swap),
            lax.ppermute(edge, "tm", near_pairs),
            lax.ppermute(edge, "tm", far_pairs),
        )

    def peers_of(array):
        array = lax.all_to_all(array, "tm", 0, 0, axis_index_groups=cores, tiled=True)
        if on_dp:
            array = lax.all_gather(array, "dp", axis=0, tiled=True)
        return array

    slice_width = width // shards
    pair = in_weight.reshape(2, slice_width, width)
    kept = lax.dynamic_index_in_dim(pair, core, 0, keepdims=False)
    given = lax.ppermute(lax.dynamic_index_in_dim(pair, 1 - core, 0, keepdims=False), "tm", swap)
    block = jnp.concatenate([jnp.where(first, kept, given), jnp.where(first, given, kept)], axis=0)
    shifts = [(0,)] + [(k, depth - k) if 2 * k < depth else (k,) for k in range(1, depth // 2 + 1)]
    forth = [(i, (i + 8) % shards) for i in range(shards)]
    back = [(i, (i - 8) % shards) for i in range(shards)]
    corner = [(i, i ^ (4 if i % 2 else 2)) for i in range(shards)]
    def mine_of(array):
        parts = array.reshape(array.shape[0], chips, 2, slice_width)
        return lax.dynamic_index_in_dim(parts, core, 2, keepdims=False).reshape(-1, half_width)

    def prepare_first(after):
        ours, noise, _ = lax.optimization_barrier((features[0], start_noise[0], after))
        own_ids = chip * chip_rows + core * rows + jnp.arange(rows, dtype=jnp.int32)
        own_live = (own_ids < end).astype(F32)[:, None]
        summed = ours.astype(F32) + noise_scale * noise.astype(F32) * own_live
        return [normalize(summed)[0].astype(BF16)]

    def prepare_second(after):
        own_taps, own_gain, own_shift, _ = lax.optimization_barrier((kernel, bn_gain, bn_shift, after))
        channel = mine_of(jnp.concatenate([own_taps, own_gain[None], own_shift[None]], axis=0))
        taps = jnp.broadcast_to(channel[:taps_n, None], (taps_n, 8, half_width))
        return [taps, channel[taps_n : taps_n + 1], channel[taps_n + 1 :], counts, scal]

    def assemble(own, partner, near, far):
        return jnp.concatenate(
            [
                jnp.where(first, far, near),
                jnp.where(first, own, partner),
                jnp.where(first, partner, own),
                jnp.where(first, near, far),
            ],
            axis=0,
        )

    along = {0: block, depth: block}
    kinds, pieces = [], []
    cot_own = cotangent[0]
    final = len(shifts) - 1
    for number, group in enumerate(shifts):
        blocks = jnp.concatenate([along[k] for k in group], axis=0)
        kinds.append((group, 0))
        pieces.append(blocks)
        sent = [lax.ppermute(blocks, "tm", swap_x), lax.ppermute(blocks, "tm", swap_y)]
        sent_kinds = [(group, 1), (group, 2)]
        if number:
            sent.append(lax.ppermute(relayed, "tm", corner))
            sent_kinds.append((shifts[number - 1], 3))
        onward = shifts[number + 1] if number < final else ()
        for k in onward:
            from_before = 2 * k <= depth
            sent.append(lax.ppermute(along[k - 1 if from_before else k + 1], "tm", forth if from_before else back))
        beside = []
        if number == 0:
            beside = prepare_first(sent[0])
        elif number == 1:
            both, *_ = lax.optimization_barrier((jnp.stack([normed_own, cot_own]), *sent[2:]))
            edge = jnp.concatenate(
                [
                    jnp.where(first, both[0, :HALO], both[0, rows - HALO :]),
                    jnp.where(first, both[1, :EDGE], both[1, rows - EDGE :]),
                ],
                axis=0,
            )
            beside = [*across(both, edge), *prepare_second(sent[-1])]
        if number == final:
            (partner, near, far), ready = (beside or crossing)[:3], beside[3:]
            beside = [
                assemble(normed_own, partner[0], near[:HALO], far[:HALO]),
                assemble(cot_own, partner[1], near[HALO:], far[HALO:]),
                place(scal, kinds, pieces, block.shape[0], chips),
                *ready,
            ]
        sent, beside = lax.optimization_barrier((sent, beside))
        relayed = jnp.where(first, sent[1], sent[0])
        if number == 0:
            (normed_own,) = beside
        elif number == 1:
            crossing, (taps, gain, shift, counts, scal) = beside[:3], beside[3:8]
        if number == final:
            normed_b, wide_cot, weight = beside[:3]
            late_kinds, late_pieces = sent_kinds, sent
        else:
            kinds += sent_kinds
            pieces += sent[: len(sent_kinds)]
            for k, arrived in zip(onward, sent[len(sent_kinds) :]):
                along[k] = arrived
    late_kinds.append((shifts[final], 3))
    late_pieces.append(lax.ppermute(relayed, "tm", corner))
    weight = place_late(scal, late_kinds, late_pieces, block.shape[0], weight)

    value, gate, glu, conv, stats = forward(
        scal, normed_b, weight, taps, chip_rows, chips, True
    )
    place_of = jnp.arange(half_width, dtype=jnp.int32)
    source = (2 * (place_of // slice_width) + core) * slice_width + place_of % slice_width
    chosen = (jnp.arange(width, dtype=jnp.int32)[:, None] == source[None, :]).astype(BF16)
    chosen, _ = lax.optimization_barrier((chosen, stats))
    cot = jnp.dot(wide_cot, chosen, preferred_element_type=F32).astype(BF16)
    gathered, base = peers_of(stats), jnp.stack([features[0], start_noise[0]])
    base, _ = lax.optimization_barrier((base, cot))
    partner, near, far = across(base, jnp.where(first, base[:, :HALO], base[:, rows - HALO :]))
    wide_features, wide_noise = (
        assemble(base[n], partner[n], near[n], far[n]) for n in range(2)
    )
    scaled, grad, inv, sums = batch(scal, counts, gathered, conv, cot, gain, shift, chips)
    sums, wide_features, wide_noise = lax.optimization_barrier((sums, wide_features, wide_noise))
    mine, other, grad_conv, totals = backward(
        scal, peers_of(sums), scaled, grad, inv, gain, taps, value, gate, weight
    )
    other = lax.ppermute(other, "tm", swap)
    moved, edge, squares = direction(scal, mine, other, features[0], start_noise[0], shards)
    squares = lax.all_to_all(squares, "tm", 0, 0, tiled=True)
    partner, near, far = across(moved, edge)
    taps_before = tap_grad(taps_n, grad_conv, glu)
    squares, taps_before = lax.optimization_barrier((squares, taps_before))
    perturbation, normed_b = ascend(
        scal, squares, wide_features, wide_noise, moved, partner, near, far, start_noise[0]
    )

    glu, conv, stats = forward(scal, normed_b, weight, taps, chip_rows, chips, False)
    alone, crossed = raw_taps(taps_n, scal, conv, glu, stats)
    outgoing, factor = last(
        taps_n, chips, scal, counts, peers_of(stats), conv, cot, gain, shift, glu, alone, crossed, stats, taps_before
    )
    received = peers_of(outgoing)
    known = jnp.concatenate([factor, totals], axis=0)
    known = lax.dynamic_slice_in_dim(known, chip * slice_width, slice_width, 1)
    kernel_total, norm_total = finish(taps_n, scal, received, known)
    return (perturbation[None], kernel_total, norm_total)


def solution(mesh):
    return jax.shard_map(
        functools.partial(on_device, mesh.shape["dp"] > 1),
        mesh=mesh,
        in_specs=(
            P("dp", "tm", None),
            P("dp", "tm", None),
            P("dp", "tm", None),
            P("tm", None),
            P(),
            P(),
            P(),
            P(),
        ),
        out_specs=(P("dp", "tm", None), P(None, "tm"), P(None, "tm")),
        check_vma=False,
    )
```

```python
import functools

import jax
import jax.numpy as jnp
from jax import lax
from jax.experimental import pallas as pl
from jax.experimental.pallas import tpu as pltpu
from jax.sharding import PartitionSpec as P

ASCENT = 2

noise_scale = 0.5
ascent_rate = 0.5
layer_epsilon = 1e-05
batch_epsilon = 1e-05
ascent_epsilon = 1e-06

HALO = 32
EDGE = 16
F32 = jnp.float32
BF16 = jnp.bfloat16


def params(limit=56 * 1024 * 1024):
    return pltpu.CompilerParams(vmem_limit_bytes=limit)


def cost(flops, nbytes):
    return pl.CostEstimate(flops=int(flops), bytes_accessed=int(nbytes), transcendentals=0)


def normalize(summed):
    centre = summed - jnp.mean(summed, axis=-1, keepdims=True)
    inverse = lax.rsqrt(jnp.mean(centre * centre, axis=-1, keepdims=True) + layer_epsilon)
    return (centre * inverse, inverse)


def live_rows(first, rows, end):
    ids = first + lax.broadcasted_iota(jnp.int32, (rows, 1), 0)
    return jnp.where((ids >= 0) & (ids < end), 1.0, 0.0).astype(F32)


def spread(plain, shifted, array):
    plain[...] = array
    rows, tiles = shifted.shape[1] * 8, shifted.shape[1]
    for s in range(8):
        shifted[s] = plain[s : s + rows].reshape(tiles, 8, -1)


def tiles_at(shifted, row, tiles, lanes):
    first = (row - row % 8) // 8
    return shifted[row % 8, first : first + tiles, :, lanes]


def convolve(taps, shifted, offsets, rows, most):
    most = max(n for n in range(1, most + 1) if rows // 8 % n == 0)
    columns = []
    for lane in range(0, taps.shape[2], 128):
        lanes = slice(lane, lane + 128)
        parts = []
        for tile in range(0, rows // 8, most):
            total = jnp.zeros((most, 8, 128), F32)
            for tap, offset in enumerate(offsets):
                total = total + taps[tap, :, lanes][None] * tiles_at(
                    shifted, offset + 8 * tile, most, lanes
                )
            parts.append(total.reshape(most * 8, 128))
        columns.append(jnp.concatenate(parts, axis=0))
    return jnp.concatenate(columns, axis=1)


def correlate(taps_n, left, shifted, first):
    rows = left.shape[0]
    lanes = slice(0, 128)
    most = 16
    totals = [None] * taps_n
    for tile in range(0, rows // 8, most):
        part = left[8 * tile : 8 * (tile + most)].reshape(most, 8, 128)
        for tap in range(taps_n):
            product = jnp.sum(
                part * tiles_at(shifted, first + tap + 8 * tile, most, lanes), axis=0, keepdims=True
            )
            totals[tap] = product if totals[tap] is None else totals[tap] + product
    return jnp.sum(jnp.concatenate(totals, axis=0), axis=1)


def block_row(scal, size, depth, shift, other):
    chip = lax.rem(scal[5] - shift + depth, depth) * 4 + (scal[4] ^ other)
    return pl.multiple_of(chip * size, 16)


def place_kernel(kinds, size, scal, *refs):
    pieces, out = refs[:-1], refs[-1]
    depth = out.shape[0] // (4 * size)
    for (group, other), ref in zip(kinds, pieces):
        for nth, shift in enumerate(group):
            row = block_row(scal, size, depth, shift, other)
            out[pl.ds(row, size), :] = ref[nth * size : (nth + 1) * size, :]


def place_late_kernel(kinds, size, scal, *refs):
    pieces, out, sems = refs[: len(kinds)], refs[-2], refs[-1]
    depth = out.shape[0] // (4 * size)
    copies = []
    for (group, other), ref in zip(kinds, pieces):
        for nth, shift in enumerate(group):
            row = block_row(scal, size, depth, shift, other)
            copies.append(
                pltpu.make_async_copy(
                    ref.at[pl.ds(nth * size, size), :],
                    out.at[pl.ds(row, size), :],
                    sems.at[len(copies)],
                )
            )
    for copy in copies:
        copy.start()
    for copy in copies:
        copy.wait()


def place(scal, kinds, pieces, size, chips):
    width = pieces[0].shape[1]
    vmem = pl.BlockSpec(memory_space=pltpu.VMEM)
    return pl.pallas_call(
        functools.partial(place_kernel, kinds, size),
        in_specs=[pl.BlockSpec(memory_space=pltpu.SMEM)] + [vmem] * len(pieces),
        out_specs=vmem,
        out_shape=jax.ShapeDtypeStruct((chips * size, width), BF16),
        compiler_params=params(),
        cost_estimate=cost(0, 4 * chips * size * width),
        name="place_weights",
    )(scal, *pieces)


def place_late(scal, kinds, pieces, size, weight):
    count = sum(len(group) for group, _ in kinds)
    vmem = pl.BlockSpec(memory_space=pltpu.VMEM)
    hbm = pl.BlockSpec(memory_space=pl.ANY)
    return pl.pallas_call(
        functools.partial(place_late_kernel, kinds, size),
        in_specs=[pl.BlockSpec(memory_space=pltpu.SMEM)] + [vmem] * len(pieces) + [hbm],
        out_specs=hbm,
        out_shape=jax.ShapeDtypeStruct(weight.shape, BF16),
        scratch_shapes=[pltpu.SemaphoreType.DMA((count,))],
        input_output_aliases={len(pieces) + 1: 0},
        compiler_params=params(),
        cost_estimate=cost(0, 4 * count * size * weight.shape[1]),
        name="place_last_weights",
    )(scal, *pieces, weight)


def forward_kernel(keep, scal, nb, value_w, gate_w, taps, *refs):
    kept, (glu, conv, stats, plain, shifted) = refs[: 2 * keep], refs[2 * keep :]
    start, end = scal[0], scal[1]
    span, taps_n = nb.shape[0], taps.shape[0]
    rows = conv.shape[0] - 2 * EDGE
    contract = (((1,), (1,)), ((), ()))
    v = lax.dot_general(nb[...], value_w[...], contract, preferred_element_type=F32)
    s = jax.nn.sigmoid(lax.dot_general(nb[...], gate_w[...], contract, preferred_element_type=F32))
    if keep:
        kept[0][...] = v[HALO : HALO + rows]
        kept[1][...] = s[HALO : HALO + rows]
    gated = (v * s * live_rows(start - HALO, span, end)).astype(BF16)
    glu[...] = gated
    spread(plain, shifted, gated.astype(F32))
    shift = HALO - EDGE - (taps_n - 1) // 2
    conv[...] = convolve(taps, shifted, [shift + tap for tap in range(taps_n)], conv.shape[0], 12)
    live = live_rows(start, rows, end)
    own = conv[EDGE : EDGE + rows, :]
    mass = jnp.sum(live * own, axis=0, keepdims=True)
    centre = live * (own - mass / jnp.maximum(jnp.sum(live), 1.0))
    both = jnp.concatenate([mass, jnp.sum(centre * centre, axis=0, keepdims=True)], axis=0)
    for peer in range(stats.shape[0]):
        stats[peer] = both


def forward(scal, nb, weight, taps, rows, peers, keep):
    span, width = nb.shape
    taps_n, _, half_width = taps.shape
    chunk = 256 if half_width % 256 == 0 else 128
    steps = half_width // chunk
    col = lambda n: pl.BlockSpec((n, chunk), lambda i: (0, i))
    return pl.pallas_call(
        functools.partial(forward_kernel, keep),
        grid=(steps,),
        in_specs=[
            pl.BlockSpec(memory_space=pltpu.SMEM),
            pl.BlockSpec((span, width), lambda i: (0, 0)),
            pl.BlockSpec((chunk, width), lambda i: (i, 0)),
            pl.BlockSpec((chunk, width), lambda i: (i + steps, 0)),
            pl.BlockSpec((taps_n, 8, chunk), lambda i: (0, 0, i)),
        ],
        out_specs=[
            *([col(rows)] * (2 * keep)),
            col(span),
            col(rows + 2 * EDGE),
            pl.BlockSpec((peers, 2, chunk), lambda i: (0, 0, i)),
        ],
        out_shape=[
            *([jax.ShapeDtypeStruct((rows, half_width), F32)] * (2 * keep)),
            jax.ShapeDtypeStruct((span, half_width), BF16),
            jax.ShapeDtypeStruct((rows + 2 * EDGE, half_width), F32),
            jax.ShapeDtypeStruct((peers, 2, half_width), F32),
        ],
        scratch_shapes=[
            pltpu.VMEM((span, chunk), F32),
            pltpu.VMEM((8, span // 8 - 1, 8, chunk), F32),
        ],
        compiler_params=params(),
        cost_estimate=cost(2 * span * width * 2 * half_width, 4 * half_width * width + 10 * span * half_width),
        name="project_glu_conv",
    )(scal, nb, weight, weight, taps)


def moments(counts, stats, live_count):
    mass = stats[0, 0:1, :]
    square = stats[0, 1:2, :]
    for peer in range(1, stats.shape[0]):
        mass = mass + stats[peer, 0:1, :]
        square = square + stats[peer, 1:2, :]
    mean = mass / live_count
    for peer in range(stats.shape[0]):
        off = stats[peer, 0:1, :] - counts[0, peer] * mean
        square = square + off * off * counts[1, peer]
    return mean, lax.rsqrt(square / live_count + batch_epsilon)


def swish_grads(scal, counts, stats, conv, cot, gain, shift):
    start, end = scal[0], scal[1]
    live_count = scal[3].astype(F32)
    mean, inv = moments(counts, stats, live_count)
    scaled = (conv[...] - mean) * inv
    pre = gain[...] * scaled + shift[...]
    sig = jax.nn.sigmoid(pre)
    live = live_rows(start - EDGE, conv.shape[0], end)
    upstream = live * cot[...].astype(F32) / ASCENT
    return scaled, upstream * sig * (1.0 + pre * (1.0 - sig)), live, mean, inv


def batch_kernel(scal, counts, stats, conv, cot, gain, shift, scaled_out, grad_out, inv_out, sums):
    scaled, grad, live, mean, inv = swish_grads(scal, counts, stats, conv, cot, gain, shift)
    scaled_out[...] = scaled
    grad_out[...] = grad
    inv_out[...] = inv
    rows = conv.shape[0] - 2 * EDGE
    own = grad[EDGE : EDGE + rows]
    both = jnp.concatenate(
        [
            jnp.sum(own, axis=0, keepdims=True),
            jnp.sum(own * scaled[EDGE : EDGE + rows], axis=0, keepdims=True),
        ],
        axis=0,
    )
    for peer in range(sums.shape[0]):
        sums[peer] = both


def batch(scal, counts, stats, conv, cot, gain, shift, peers):
    span, half_width = conv.shape
    chunk = 256 if half_width % 256 == 0 else 128
    col = lambda n: pl.BlockSpec((n, chunk), lambda i: (0, i))
    smem = pl.BlockSpec(memory_space=pltpu.SMEM)
    return pl.pallas_call(
        batch_kernel,
        grid=(half_width // chunk,),
        in_specs=[
            smem,
            smem,
            pl.BlockSpec((stats.shape[0], 2, chunk), lambda i: (0, 0, i)),
            col(span),
            col(span),
            col(1),
            col(1),
        ],
        out_specs=[col(span), col(span), col(1), pl.BlockSpec((peers, 2, chunk), lambda i: (0, 0, i))],
        out_shape=[
            jax.ShapeDtypeStruct((span, half_width), F32),
            jax.ShapeDtypeStruct((span, half_width), F32),
            jax.ShapeDtypeStruct((1, half_width), F32),
            jax.ShapeDtypeStruct((peers, 2, half_width), F32),
        ],
        compiler_params=params(),
        cost_estimate=cost(40 * span * half_width, 16 * span * half_width),
        name="batch_norm_swish",
    )(scal, counts, stats, conv, cot, gain, shift)


def backward_kernel(scal, sums, scaled, grad, inv, gain, taps, value, gate, value_w, gate_w, mine, other, grad_conv, totals, plain, shifted, part):
    start, end, core = scal[0], scal[1], scal[2]
    rows, taps_n = value.shape[0], taps.shape[0]
    half = (taps_n - 1) // 2
    live_count = scal[3].astype(F32)
    both = sums[0]
    for peer in range(1, sums.shape[0]):
        both = both + sums[peer]
    totals[...] = both
    shift_sum, gain_sum = both[0:1], both[1:2]
    live = live_rows(start - EDGE, scaled.shape[0], end)
    through = live * (inv[...] * gain[...]) * (
        grad[...] - (shift_sum + scaled[...] * gain_sum) / live_count
    )
    rounded = through.astype(BF16)
    grad_conv[...] = rounded[EDGE : EDGE + rows]
    spread(plain, shifted, rounded.astype(F32))
    grad_glu = convolve(taps, shifted, [EDGE + half - tap for tap in range(taps_n)], rows, 16)
    grad_glu = (grad_glu * live_rows(start, rows, end)).astype(BF16).astype(F32)
    sig = gate[...]
    to_value = (grad_glu * sig).astype(BF16)
    to_gate = (grad_glu * value[...] * sig * (1.0 - sig)).astype(BF16)
    product = jnp.dot(to_value, value_w[...], preferred_element_type=F32) + jnp.dot(
        to_gate, gate_w[...], preferred_element_type=F32
    )
    step, last_step = pl.program_id(0), pl.num_programs(0) - 1

    @pl.when(step == 0)
    def _():
        part[...] = product

    @pl.when(step > 0)
    def _():
        part[...] += product

    @pl.when(step == last_step)
    def _():
        count = mine.shape[0]
        mine[...] = part[pl.ds(pl.multiple_of(core * count, count), count), :]
        other[...] = part[pl.ds(pl.multiple_of((1 - core) * count, count), count), :]


def backward(scal, sums, scaled, grad, inv, gain, taps, value, gate, weight):
    span, half_width = scaled.shape
    rows, width = value.shape[0], weight.shape[1]
    chunk = 256 if half_width % 256 == 0 else 128
    steps = half_width // chunk
    taps_n = taps.shape[0]
    col = lambda n: pl.BlockSpec((n, chunk), lambda i: (0, i))
    own = pl.BlockSpec((rows // 2, width), lambda i: (0, 0))
    return pl.pallas_call(
        backward_kernel,
        grid=(steps,),
        in_specs=[
            pl.BlockSpec(memory_space=pltpu.SMEM),
            pl.BlockSpec((sums.shape[0], 2, chunk), lambda i: (0, 0, i)),
            col(span),
            col(span),
            col(1),
            col(1),
            pl.BlockSpec((taps_n, 8, chunk), lambda i: (0, 0, i)),
            col(rows),
            col(rows),
            pl.BlockSpec((chunk, width), lambda i: (i, 0)),
            pl.BlockSpec((chunk, width), lambda i: (i + steps, 0)),
        ],
        out_specs=[own, own, col(rows), col(2)],
        out_shape=[
            jax.ShapeDtypeStruct((rows // 2, width), F32),
            jax.ShapeDtypeStruct((rows // 2, width), F32),
            jax.ShapeDtypeStruct((rows, half_width), BF16),
            jax.ShapeDtypeStruct((2, half_width), F32),
        ],
        scratch_shapes=[
            pltpu.VMEM((span, chunk), F32),
            pltpu.VMEM((8, span // 8 - 1, 8, chunk), F32),
            pltpu.VMEM((rows, width), F32),
        ],
        compiler_params=params(),
        cost_estimate=cost(2 * rows * width * 2 * half_width, 4 * half_width * width + 20 * span * half_width),
        name="grad_conv_project_back",
    )(scal, sums, scaled, grad, inv, gain, taps, value, gate, weight, weight)


def shifted_scratch(span):
    return [pltpu.VMEM((span, 128), F32), pltpu.VMEM((8, span // 8 - 1, 8, 128), F32)]


def tap_grad_kernel(taps_n, grad_conv, glu, out, plain, shifted):
    spread(plain, shifted, glu[...].astype(F32))
    first = HALO - (taps_n - 1) // 2
    out[...] = correlate(taps_n, grad_conv[...].astype(F32), shifted, first)


def tap_grad(taps_n, grad_conv, glu):
    rows, half_width = grad_conv.shape
    span = glu.shape[0]
    col = lambda n: pl.BlockSpec((n, 128), lambda i: (0, i))
    return pl.pallas_call(
        functools.partial(tap_grad_kernel, taps_n),
        grid=(half_width // 128,),
        in_specs=[col(rows), col(span)],
        out_specs=col(taps_n),
        out_shape=jax.ShapeDtypeStruct((taps_n, half_width), F32),
        scratch_shapes=shifted_scratch(span),
        compiler_params=params(),
        cost_estimate=cost(2 * taps_n * rows * half_width, 4 * span * half_width),
        name="tap_grad",
    )(grad_conv, glu)


def raw_taps_kernel(taps_n, scal, conv, glu, stats, alone, crossed, plain, shifted):
    start, end = scal[0], scal[1]
    rows, span = conv.shape[0] - 2 * EDGE, glu.shape[0]
    spread(plain, shifted, glu[...].astype(F32))
    first = HALO - (taps_n - 1) // 2
    live = live_rows(start, rows, end)
    local = stats[0, 0:1, :] / jnp.maximum(jnp.sum(live), 1.0)
    crossed[...] = correlate(taps_n, live * (conv[EDGE : EDGE + rows, :] - local), shifted, first)
    tap = lax.broadcasted_iota(jnp.int32, (taps_n, span), 0)
    at = lax.broadcasted_iota(jnp.int32, (taps_n, span), 1) - first - tap
    inside = (at >= 0) & (at < jnp.clip(end - start, 0, rows))
    alone[...] = jnp.dot(
        jnp.where(inside, 1.0, 0.0).astype(BF16), glu[...], preferred_element_type=F32
    )


def raw_taps(taps_n, scal, conv, glu, stats):
    rows, half_width = conv.shape
    span = glu.shape[0]
    col = lambda n: pl.BlockSpec((n, 128), lambda i: (0, i))
    return pl.pallas_call(
        functools.partial(raw_taps_kernel, taps_n),
        grid=(half_width // 128,),
        in_specs=[
            pl.BlockSpec(memory_space=pltpu.SMEM),
            col(rows),
            col(span),
            pl.BlockSpec((1, 2, 128), lambda i: (0, 0, i)),
        ],
        out_specs=[col(taps_n), col(taps_n)],
        out_shape=[jax.ShapeDtypeStruct((taps_n, half_width), F32)] * 2,
        scratch_shapes=shifted_scratch(span),
        compiler_params=params(),
        cost_estimate=cost(2 * taps_n * rows * half_width, 8 * span * half_width),
        name="raw_taps",
    )(scal, conv, glu, stats)


def halves(array):
    high = array.astype(BF16).astype(F32)
    return high, array - high


def last_kernel(taps_n, scal, counts, stats, conv, cot, gain, shift, glu, alone, crossed, local_stats, taps_before, out, factor_out, plain, shifted, pay):
    step = pl.program_id(0)
    scaled, grad, live, mean, inv = swish_grads(scal, counts, stats, conv, cot, gain, shift)
    rows = conv.shape[0] - 2 * EDGE
    spread(plain, shifted, glu[...].astype(F32))
    first = HALO - (taps_n - 1) // 2
    factor = inv * gain[...]
    factor_out[...] = factor
    own = grad[EDGE : EDGE + rows]
    direct = taps_before[...] + factor * correlate(taps_n, own, shifted, first)
    own_live = live[EDGE : EDGE + rows]
    local = local_stats[0, 0:1, :] / jnp.maximum(jnp.sum(own_live), 1.0)
    with_scaled = inv * (crossed[...] + (local - mean) * alone[...])
    sums = jnp.concatenate(
        [
            jnp.sum(own, axis=0, keepdims=True),
            jnp.sum(own * scaled[EDGE : EDGE + rows], axis=0, keepdims=True),
        ],
        axis=0,
    )
    pay[step] = jnp.concatenate([*halves(direct), with_scaled, alone[...], *halves(sums)], axis=0)

    @pl.when(step == pl.num_programs(0) - 1)
    def _():
        turned = jnp.concatenate([jnp.transpose(pay[s]) for s in range(pay.shape[0])], axis=0)
        block = out.shape[1]
        for index in range(out.shape[0]):
            out[index] = turned[index * block : (index + 1) * block].astype(BF16)


def last(taps_n, peers, scal, counts, stats, conv, cot, gain, shift, glu, alone, crossed, local_stats, taps_before):
    span, half_width = conv.shape
    chunk = 128
    steps = half_width // chunk
    pay = 4 * taps_n + 4
    col = lambda n: pl.BlockSpec((n, chunk), lambda i: (0, i))
    smem = pl.BlockSpec(memory_space=pltpu.SMEM)
    return pl.pallas_call(
        functools.partial(last_kernel, taps_n),
        grid=(steps,),
        in_specs=[
            smem,
            smem,
            pl.BlockSpec((stats.shape[0], 2, chunk), lambda i: (0, 0, i)),
            col(span),
            col(span),
            col(1),
            col(1),
            col(glu.shape[0]),
            col(taps_n),
            col(taps_n),
            pl.BlockSpec((1, 2, chunk), lambda i: (0, 0, i)),
            col(taps_n),
        ],
        out_specs=[pl.BlockSpec((peers, half_width // peers, pay), lambda i: (0, 0, 0)), col(1)],
        out_shape=[
            jax.ShapeDtypeStruct((peers, half_width // peers, pay), BF16),
            jax.ShapeDtypeStruct((1, half_width), F32),
        ],
        scratch_shapes=[*shifted_scratch(glu.shape[0]), pltpu.VMEM((steps, pay, chunk), F32)],
        compiler_params=params(),
        cost_estimate=cost(100 * span * half_width, 10 * span * half_width),
        name="batch_norm_swish_taps",
    )(scal, counts, stats, conv, cot, gain, shift, glu, alone, crossed, local_stats, taps_before)


def finish_kernel(taps_n, scal, received, known, taps_out, norm_out):
    total = received[0].astype(F32)
    for index in range(1, received.shape[0]):
        total = total + received[index].astype(F32)
    total = jnp.transpose(total)
    n = taps_n
    sums = total[4 * n : 4 * n + 2] + total[4 * n + 2 : 4 * n + 4]
    shift_sum, gain_sum = sums[0:1], sums[1:2]
    factor = known[0:1] / scal[3].astype(F32)
    taps_out[...] = (total[:n] + total[n : 2 * n]) - factor * (
        gain_sum * total[2 * n : 3 * n] + shift_sum * total[3 * n : 4 * n]
    )
    norm_out[...] = jnp.concatenate([gain_sum + known[2:3], shift_sum + known[1:2]], axis=0)


def finish(taps_n, scal, received, known):
    width = received.shape[1]
    vmem = pl.BlockSpec(memory_space=pltpu.VMEM)
    return pl.pallas_call(
        functools.partial(finish_kernel, taps_n),
        in_specs=[pl.BlockSpec(memory_space=pltpu.SMEM), vmem, vmem],
        out_shape=[
            jax.ShapeDtypeStruct((taps_n, width), F32),
            jax.ShapeDtypeStruct((2, width), F32),
        ],
        compiler_params=params(),
        name="finish",
    )(scal, received, known)


def direction_kernel(scal, mine, other, features, noise, out, edge, squares):
    rows = mine.shape[0]
    first = scal[0] + scal[2] * rows
    block = 32
    total = jnp.zeros((1, 128), F32)
    for row in range(0, rows, block):
        at = slice(row, row + block)
        live = live_rows(first + row, block, scal[1])
        summed = features[at].astype(F32) + noise_scale * noise[at].astype(F32) * live
        normed, inverse = normalize(summed)
        grad = mine[at] + other[at]
        moved = (
            live
            * inverse
            * (
                grad
                - jnp.mean(grad, axis=-1, keepdims=True)
                - normed * jnp.mean(grad * normed, axis=-1, keepdims=True)
            )
        )
        out[at] = moved
        total = total + jnp.sum(moved * moved)
    edge[...] = jnp.where(scal[2] == 0, out[:HALO], out[rows - HALO :])
    for peer in range(squares.shape[0]):
        squares[peer] = total


def direction(scal, mine, other, features, noise, peers):
    rows, width = mine.shape
    vmem = pl.BlockSpec(memory_space=pltpu.VMEM)
    return pl.pallas_call(
        direction_kernel,
        in_specs=[pl.BlockSpec(memory_space=pltpu.SMEM)] + [vmem] * 4,
        out_shape=[
            jax.ShapeDtypeStruct((rows, width), F32),
            jax.ShapeDtypeStruct((HALO, width), F32),
            jax.ShapeDtypeStruct((peers, 1, 128), F32),
        ],
        compiler_params=params(),
        cost_estimate=cost(30 * rows * width, 16 * rows * width),
        name="direction",
    )(scal, mine, other, features, noise)


def ascend_kernel(scal, squares, features, noise, mine, partner, near, far, own_noise, perturbation, normed_out):
    start, end, core = scal[0], scal[1], scal[2]
    rows, width = mine.shape
    total = squares[0]
    for index in range(1, squares.shape[0]):
        total = total + squares[index]
    total = total[0:1, 0:1]
    length = jnp.full((1, 1), 1.0, F32) * end.astype(F32)
    rate = ascent_rate * jnp.sqrt(length * width) / (jnp.sqrt(total) + ascent_epsilon)
    block = 32
    is_first = core == 0

    def place(row, moved):
        at = slice(row, row + block)
        live = live_rows(start - HALO + row, block, end)
        summed = features[at].astype(F32) + (noise_scale * noise[at].astype(F32) * live + moved * rate)
        normed_out[at] = normalize(summed)[0].astype(BF16)

    place(0, jnp.where(is_first, far[...], near[...]))
    for row in range(0, rows, block):
        at = slice(row, row + block)
        place(HALO + row, jnp.where(is_first, mine[at], partner[at]))
        place(HALO + rows + row, jnp.where(is_first, partner[at], mine[at]))
        live = live_rows(start + core * rows + row, block, end)
        perturbation[at] = noise_scale * own_noise[at].astype(F32) * live + mine[at] * rate
    place(HALO + 2 * rows, jnp.where(is_first, near[...], far[...]))


def ascend(scal, squares, features, noise, mine, partner, near, far, own_noise):
    vmem = pl.BlockSpec(memory_space=pltpu.VMEM)
    return pl.pallas_call(
        ascend_kernel,
        in_specs=[pl.BlockSpec(memory_space=pltpu.SMEM)] + [vmem] * 8,
        out_shape=[
            jax.ShapeDtypeStruct(mine.shape, F32),
            jax.ShapeDtypeStruct(features.shape, BF16),
        ],
        compiler_params=params(),
        cost_estimate=cost(30 * features.size, 8 * features.size),
        name="ascend",
    )(scal, squares, features, noise, mine, partner, near, far, own_noise)


def on_device(on_dp, features, start_noise, cotangent, in_weight, kernel, bn_gain, bn_shift, ends):
    rows, width = features.shape[1:]
    taps_n = kernel.shape[0]
    shards = lax.axis_size("tm")
    chips = shards // 2
    index = lax.axis_index("tm")
    group = lax.axis_index("dp")
    chip, core = index // 2, index % 2
    chip_rows = 2 * rows
    half_width = width // 2
    end = lax.dynamic_index_in_dim(ends, group, 0, keepdims=False)
    scal = jnp.stack([chip * chip_rows, end, core, jnp.sum(ends), chip % 4, chip // 4]).astype(jnp.int32)
    held = jnp.clip(
        ends[:, None] - chip_rows * jnp.arange(chips, dtype=jnp.int32)[None, :], 0, chip_rows
    ).reshape(-1).astype(F32)
    counts = jnp.stack([held, jnp.where(held > 0, 1.0 / jnp.maximum(held, 1.0), 0.0)])

    cores = [[2 * c + k for c in range(chips)] for k in range(2)]
    depth = chips // 4
    swap = [(i, i ^ 1) for i in range(shards)]
    swap_x = [(i, i ^ 2) for i in range(shards)]
    swap_y = [(i, i ^ 4) for i in range(shards)]
    near_pairs = [(2 * c, 2 * c - 2) for c in range(1, chips)] + [
        (2 * c + 1, 2 * c + 3) for c in range(chips - 1)
    ]
    far_pairs = [(2 * c, 2 * c - 1) for c in range(1, chips)] + [
        (2 * c + 1, 2 * c + 2) for c in range(chips - 1)
    ]
    first = core == 0

    def across(array, edge):
        return (
            lax.ppermute(array, "tm", swap),
            lax.ppermute(edge, "tm", near_pairs),
            lax.ppermute(edge, "tm", far_pairs),
        )

    def peers_of(array):
        array = lax.all_to_all(array, "tm", 0, 0, axis_index_groups=cores, tiled=True)
        if on_dp:
            array = lax.all_gather(array, "dp", axis=0, tiled=True)
        return array

    slice_width = width // shards
    pair = in_weight.reshape(2, slice_width, width)
    kept = lax.dynamic_index_in_dim(pair, core, 0, keepdims=False)
    given = lax.ppermute(lax.dynamic_index_in_dim(pair, 1 - core, 0, keepdims=False), "tm", swap)
    block = jnp.concatenate([jnp.where(first, kept, given), jnp.where(first, given, kept)], axis=0)
    shifts = [(0,)] + [(k, depth - k) if 2 * k < depth else (k,) for k in range(1, depth // 2 + 1)]
    forth = [(i, (i + 8) % shards) for i in range(shards)]
    back = [(i, (i - 8) % shards) for i in range(shards)]
    corner = [(i, i ^ (4 if i % 2 else 2)) for i in range(shards)]
    def mine_of(array):
        parts = array.reshape(array.shape[0], chips, 2, slice_width)
        return lax.dynamic_index_in_dim(parts, core, 2, keepdims=False).reshape(-1, half_width)

    def prepare_first(after):
        ours, noise, _ = lax.optimization_barrier((features[0], start_noise[0], after))
        own_ids = chip * chip_rows + core * rows + jnp.arange(rows, dtype=jnp.int32)
        own_live = (own_ids < end).astype(F32)[:, None]
        summed = ours.astype(F32) + noise_scale * noise.astype(F32) * own_live
        return [normalize(summed)[0].astype(BF16)]

    def prepare_second(after):
        own_taps, own_gain, own_shift, _ = lax.optimization_barrier((kernel, bn_gain, bn_shift, after))
        channel = mine_of(jnp.concatenate([own_taps, own_gain[None], own_shift[None]], axis=0))
        taps = jnp.broadcast_to(channel[:taps_n, None], (taps_n, 8, half_width))
        return [taps, channel[taps_n : taps_n + 1], channel[taps_n + 1 :], counts, scal]

    def assemble(own, partner, near, far):
        return jnp.concatenate(
            [
                jnp.where(first, far, near),
                jnp.where(first, own, partner),
                jnp.where(first, partner, own),
                jnp.where(first, near, far),
            ],
            axis=0,
        )

    along = {0: block, depth: block}
    kinds, pieces = [], []
    cot_own = cotangent[0]
    final = len(shifts) - 1
    for number, group in enumerate(shifts):
        blocks = jnp.concatenate([along[k] for k in group], axis=0)
        kinds.append((group, 0))
        pieces.append(blocks)
        sent = [lax.ppermute(blocks, "tm", swap_x), lax.ppermute(blocks, "tm", swap_y)]
        sent_kinds = [(group, 1), (group, 2)]
        if number:
            sent.append(lax.ppermute(relayed, "tm", corner))
            sent_kinds.append((shifts[number - 1], 3))
        onward = shifts[number + 1] if number < final else ()
        for k in onward:
            from_before = 2 * k <= depth
            sent.append(lax.ppermute(along[k - 1 if from_before else k + 1], "tm", forth if from_before else back))
        beside = []
        if number == 0:
            beside = prepare_first(sent[0])
        elif number == 1:
            both, *_ = lax.optimization_barrier((jnp.stack([normed_own, cot_own]), *sent[2:]))
            edge = jnp.concatenate(
                [
                    jnp.where(first, both[0, :HALO], both[0, rows - HALO :]),
                    jnp.where(first, both[1, :EDGE], both[1, rows - EDGE :]),
                ],
                axis=0,
            )
            beside = [*across(both, edge), *prepare_second(sent[-1])]
        if number == final:
            (partner, near, far), ready = (beside or crossing)[:3], beside[3:]
            beside = [
                assemble(normed_own, partner[0], near[:HALO], far[:HALO]),
                assemble(cot_own, partner[1], near[HALO:], far[HALO:]),
                place(scal, kinds, pieces, block.shape[0], chips),
                *ready,
            ]
        sent, beside = lax.optimization_barrier((sent, beside))
        relayed = jnp.where(first, sent[1], sent[0])
        if number == 0:
            (normed_own,) = beside
        elif number == 1:
            crossing, (taps, gain, shift, counts, scal) = beside[:3], beside[3:8]
        if number == final:
            normed_b, wide_cot, weight = beside[:3]
            late_kinds, late_pieces = sent_kinds, sent
        else:
            kinds += sent_kinds
            pieces += sent[: len(sent_kinds)]
            for k, arrived in zip(onward, sent[len(sent_kinds) :]):
                along[k] = arrived
    base, _ = lax.optimization_barrier((jnp.stack([features[0], start_noise[0]]), relayed))
    base_crossing = across(base, jnp.where(first, base[:, :HALO], base[:, rows - HALO :]))
    late_kinds.append((shifts[final], 3))
    late_pieces.append(lax.ppermute(relayed, "tm", corner))
    weight = place_late(scal, late_kinds, late_pieces, block.shape[0], weight)

    value, gate, glu, conv, stats = forward(
        scal, normed_b, weight, taps, chip_rows, chips, True
    )
    stats, base_crossing = lax.optimization_barrier((stats, base_crossing))
    place_of = jnp.arange(half_width, dtype=jnp.int32)
    source = (2 * (place_of // slice_width) + core) * slice_width + place_of % slice_width
    chosen = (jnp.arange(width, dtype=jnp.int32)[:, None] == source[None, :]).astype(BF16)
    cot = jnp.dot(wide_cot, chosen, preferred_element_type=F32).astype(BF16)
    gathered = peers_of(stats)
    partner, near, far = base_crossing
    wide_features, wide_noise = (
        assemble(base[n], partner[n], near[n], far[n]) for n in range(2)
    )
    scaled, grad, inv, sums = batch(scal, counts, gathered, conv, cot, gain, shift, chips)
    mine, other, grad_conv, totals = backward(
        scal, peers_of(sums), scaled, grad, inv, gain, taps, value, gate, weight
    )
    other = lax.ppermute(other, "tm", swap)
    moved, edge, squares = direction(scal, mine, other, features[0], start_noise[0], shards)
    squares = lax.all_to_all(squares, "tm", 0, 0, tiled=True)
    partner, near, far = across(moved, edge)
    taps_before = tap_grad(taps_n, grad_conv, glu)
    squares, taps_before = lax.optimization_barrier((squares, taps_before))
    perturbation, normed_b = ascend(
        scal, squares, wide_features, wide_noise, moved, partner, near, far, start_noise[0]
    )

    glu, conv, stats = forward(scal, normed_b, weight, taps, chip_rows, chips, False)
    alone, crossed = raw_taps(taps_n, scal, conv, glu, stats)
    outgoing, factor = last(
        taps_n, chips, scal, counts, peers_of(stats), conv, cot, gain, shift, glu, alone, crossed, stats, taps_before
    )
    received = peers_of(outgoing)
    known = jnp.concatenate([factor, totals], axis=0)
    known = lax.dynamic_slice_in_dim(known, chip * slice_width, slice_width, 1)
    kernel_total, norm_total = finish(taps_n, scal, received, known)
    return (perturbation[None], kernel_total, norm_total)


def solution(mesh):
    return jax.shard_map(
        functools.partial(on_device, mesh.shape["dp"] > 1),
        mesh=mesh,
        in_specs=(
            P("dp", "tm", None),
            P("dp", "tm", None),
            P("dp", "tm", None),
            P("tm", None),
            P(),
            P(),
            P(),
            P(),
        ),
        out_specs=(P("dp", "tm", None), P(None, "tm"), P(None, "tm")),
        check_vma=False,
    )
```

```python
import functools

import jax
import jax.numpy as jnp
from jax import lax
from jax.experimental import pallas as pl
from jax.experimental.pallas import tpu as pltpu
from jax.sharding import PartitionSpec as P

ASCENT = 2

noise_scale = 0.5
ascent_rate = 0.5
layer_epsilon = 1e-05
batch_epsilon = 1e-05
ascent_epsilon = 1e-06

HALO = 32
EDGE = 16
F32 = jnp.float32
BF16 = jnp.bfloat16


def params(limit=56 * 1024 * 1024):
    return pltpu.CompilerParams(vmem_limit_bytes=limit)


def cost(flops, nbytes):
    return pl.CostEstimate(flops=int(flops), bytes_accessed=int(nbytes), transcendentals=0)


def normalize(summed):
    centre = summed - jnp.mean(summed, axis=-1, keepdims=True)
    inverse = lax.rsqrt(jnp.mean(centre * centre, axis=-1, keepdims=True) + layer_epsilon)
    return (centre * inverse, inverse)


def live_rows(first, rows, end):
    ids = first + lax.broadcasted_iota(jnp.int32, (rows, 1), 0)
    return jnp.where((ids >= 0) & (ids < end), 1.0, 0.0).astype(F32)


def spread(plain, shifted, array):
    plain[...] = array
    rows, tiles = shifted.shape[1] * 8, shifted.shape[1]
    for s in range(8):
        shifted[s] = plain[s : s + rows].reshape(tiles, 8, -1)


def tiles_at(shifted, row, tiles, lanes):
    first = (row - row % 8) // 8
    return shifted[row % 8, first : first + tiles, :, lanes]


def convolve(taps, shifted, offsets, rows, most):
    most = max(n for n in range(1, most + 1) if rows // 8 % n == 0)
    columns = []
    for lane in range(0, taps.shape[2], 128):
        lanes = slice(lane, lane + 128)
        parts = []
        for tile in range(0, rows // 8, most):
            total = jnp.zeros((most, 8, 128), F32)
            for tap, offset in enumerate(offsets):
                total = total + taps[tap, :, lanes][None] * tiles_at(
                    shifted, offset + 8 * tile, most, lanes
                )
            parts.append(total.reshape(most * 8, 128))
        columns.append(jnp.concatenate(parts, axis=0))
    return jnp.concatenate(columns, axis=1)


def correlate(taps_n, left, shifted, first):
    rows = left.shape[0]
    lanes = slice(0, 128)
    most = 16
    totals = [None] * taps_n
    for tile in range(0, rows // 8, most):
        part = left[8 * tile : 8 * (tile + most)].reshape(most, 8, 128)
        for tap in range(taps_n):
            product = jnp.sum(
                part * tiles_at(shifted, first + tap + 8 * tile, most, lanes), axis=0, keepdims=True
            )
            totals[tap] = product if totals[tap] is None else totals[tap] + product
    return jnp.sum(jnp.concatenate(totals, axis=0), axis=1)


def block_row(scal, size, depth, shift, other):
    chip = lax.rem(scal[5] - shift + depth, depth) * 4 + (scal[4] ^ other)
    return pl.multiple_of(chip * size, 16)


def place_kernel(kinds, size, scal, *refs):
    pieces, out = refs[:-1], refs[-1]
    depth = out.shape[0] // (4 * size)
    for (group, other), ref in zip(kinds, pieces):
        for nth, shift in enumerate(group):
            row = block_row(scal, size, depth, shift, other)
            out[pl.ds(row, size), :] = ref[nth * size : (nth + 1) * size, :]


def place_late_kernel(kinds, size, scal, *refs):
    pieces, out, sems = refs[: len(kinds)], refs[-2], refs[-1]
    depth = out.shape[0] // (4 * size)
    copies = []
    for (group, other), ref in zip(kinds, pieces):
        for nth, shift in enumerate(group):
            row = block_row(scal, size, depth, shift, other)
            copies.append(
                pltpu.make_async_copy(
                    ref.at[pl.ds(nth * size, size), :],
                    out.at[pl.ds(row, size), :],
                    sems.at[len(copies)],
                )
            )
    for copy in copies:
        copy.start()
    for copy in copies:
        copy.wait()


def place(scal, kinds, pieces, size, chips):
    width = pieces[0].shape[1]
    vmem = pl.BlockSpec(memory_space=pltpu.VMEM)
    return pl.pallas_call(
        functools.partial(place_kernel, kinds, size),
        in_specs=[pl.BlockSpec(memory_space=pltpu.SMEM)] + [vmem] * len(pieces),
        out_specs=vmem,
        out_shape=jax.ShapeDtypeStruct((chips * size, width), BF16),
        compiler_params=params(),
        cost_estimate=cost(0, 4 * chips * size * width),
        name="place_weights",
    )(scal, *pieces)


def place_late(scal, kinds, pieces, size, weight):
    count = sum(len(group) for group, _ in kinds)
    vmem = pl.BlockSpec(memory_space=pltpu.VMEM)
    hbm = pl.BlockSpec(memory_space=pl.ANY)
    return pl.pallas_call(
        functools.partial(place_late_kernel, kinds, size),
        in_specs=[pl.BlockSpec(memory_space=pltpu.SMEM)] + [vmem] * len(pieces) + [hbm],
        out_specs=hbm,
        out_shape=jax.ShapeDtypeStruct(weight.shape, BF16),
        scratch_shapes=[pltpu.SemaphoreType.DMA((count,))],
        input_output_aliases={len(pieces) + 1: 0},
        compiler_params=params(),
        cost_estimate=cost(0, 4 * count * size * weight.shape[1]),
        name="place_last_weights",
    )(scal, *pieces, weight)


def forward_kernel(keep, scal, nb, value_w, gate_w, taps, *refs):
    kept, (glu, conv, stats, plain, shifted) = refs[: 2 * keep], refs[2 * keep :]
    start, end = scal[0], scal[1]
    span, taps_n = nb.shape[0], taps.shape[0]
    rows = conv.shape[0] - 2 * EDGE
    contract = (((1,), (1,)), ((), ()))
    v = lax.dot_general(nb[...], value_w[...], contract, preferred_element_type=F32)
    s = jax.nn.sigmoid(lax.dot_general(nb[...], gate_w[...], contract, preferred_element_type=F32))
    if keep:
        kept[0][...] = v[HALO : HALO + rows]
        kept[1][...] = s[HALO : HALO + rows]
    gated = (v * s * live_rows(start - HALO, span, end)).astype(BF16)
    glu[...] = gated
    spread(plain, shifted, gated.astype(F32))
    shift = HALO - EDGE - (taps_n - 1) // 2
    conv[...] = convolve(taps, shifted, [shift + tap for tap in range(taps_n)], conv.shape[0], 12)
    live = live_rows(start, rows, end)
    own = conv[EDGE : EDGE + rows, :]
    mass = jnp.sum(live * own, axis=0, keepdims=True)
    centre = live * (own - mass / jnp.maximum(jnp.sum(live), 1.0))
    both = jnp.concatenate([mass, jnp.sum(centre * centre, axis=0, keepdims=True)], axis=0)
    for peer in range(stats.shape[0]):
        stats[peer] = both


def forward(scal, nb, weight, taps, rows, peers, keep):
    span, width = nb.shape
    taps_n, _, half_width = taps.shape
    chunk = 256 if half_width % 256 == 0 else 128
    steps = half_width // chunk
    col = lambda n: pl.BlockSpec((n, chunk), lambda i: (0, i))
    return pl.pallas_call(
        functools.partial(forward_kernel, keep),
        grid=(steps,),
        in_specs=[
            pl.BlockSpec(memory_space=pltpu.SMEM),
            pl.BlockSpec((span, width), lambda i: (0, 0)),
            pl.BlockSpec((chunk, width), lambda i: (i, 0)),
            pl.BlockSpec((chunk, width), lambda i: (i + steps, 0)),
            pl.BlockSpec((taps_n, 8, chunk), lambda i: (0, 0, i)),
        ],
        out_specs=[
            *([col(rows)] * (2 * keep)),
            col(span),
            col(rows + 2 * EDGE),
            pl.BlockSpec((peers, 2, chunk), lambda i: (0, 0, i)),
        ],
        out_shape=[
            *([jax.ShapeDtypeStruct((rows, half_width), F32)] * (2 * keep)),
            jax.ShapeDtypeStruct((span, half_width), BF16),
            jax.ShapeDtypeStruct((rows + 2 * EDGE, half_width), F32),
            jax.ShapeDtypeStruct((peers, 2, half_width), F32),
        ],
        scratch_shapes=[
            pltpu.VMEM((span, chunk), F32),
            pltpu.VMEM((8, span // 8 - 1, 8, chunk), F32),
        ],
        compiler_params=params(),
        cost_estimate=cost(2 * span * width * 2 * half_width, 4 * half_width * width + 10 * span * half_width),
        name="project_glu_conv",
    )(scal, nb, weight, weight, taps)


def moments(counts, stats, live_count):
    mass = stats[0, 0:1, :]
    square = stats[0, 1:2, :]
    for peer in range(1, stats.shape[0]):
        mass = mass + stats[peer, 0:1, :]
        square = square + stats[peer, 1:2, :]
    mean = mass / live_count
    for peer in range(stats.shape[0]):
        off = stats[peer, 0:1, :] - counts[0, peer] * mean
        square = square + off * off * counts[1, peer]
    return mean, lax.rsqrt(square / live_count + batch_epsilon)


def swish_grads(scal, counts, stats, conv, cot, gain, shift):
    start, end = scal[0], scal[1]
    live_count = scal[3].astype(F32)
    mean, inv = moments(counts, stats, live_count)
    scaled = (conv[...] - mean) * inv
    pre = gain[...] * scaled + shift[...]
    sig = jax.nn.sigmoid(pre)
    live = live_rows(start - EDGE, conv.shape[0], end)
    upstream = live * cot[...].astype(F32) / ASCENT
    return scaled, upstream * sig * (1.0 + pre * (1.0 - sig)), live, mean, inv


def batch_kernel(scal, counts, stats, conv, cot, gain, shift, scaled_out, grad_out, inv_out, sums):
    scaled, grad, live, mean, inv = swish_grads(scal, counts, stats, conv, cot, gain, shift)
    scaled_out[...] = scaled
    grad_out[...] = grad
    inv_out[...] = inv
    rows = conv.shape[0] - 2 * EDGE
    own = grad[EDGE : EDGE + rows]
    both = jnp.concatenate(
        [
            jnp.sum(own, axis=0, keepdims=True),
            jnp.sum(own * scaled[EDGE : EDGE + rows], axis=0, keepdims=True),
        ],
        axis=0,
    )
    for peer in range(sums.shape[0]):
        sums[peer] = both


def batch(scal, counts, stats, conv, cot, gain, shift, peers):
    span, half_width = conv.shape
    chunk = 256 if half_width % 256 == 0 else 128
    col = lambda n: pl.BlockSpec((n, chunk), lambda i: (0, i))
    smem = pl.BlockSpec(memory_space=pltpu.SMEM)
    return pl.pallas_call(
        batch_kernel,
        grid=(half_width // chunk,),
        in_specs=[
            smem,
            smem,
            pl.BlockSpec((stats.shape[0], 2, chunk), lambda i: (0, 0, i)),
            col(span),
            col(span),
            col(1),
            col(1),
        ],
        out_specs=[col(span), col(span), col(1), pl.BlockSpec((peers, 2, chunk), lambda i: (0, 0, i))],
        out_shape=[
            jax.ShapeDtypeStruct((span, half_width), F32),
            jax.ShapeDtypeStruct((span, half_width), F32),
            jax.ShapeDtypeStruct((1, half_width), F32),
            jax.ShapeDtypeStruct((peers, 2, half_width), F32),
        ],
        compiler_params=params(),
        cost_estimate=cost(40 * span * half_width, 16 * span * half_width),
        name="batch_norm_swish",
    )(scal, counts, stats, conv, cot, gain, shift)


def backward_kernel(scal, sums, scaled, grad, inv, gain, taps, value, gate, value_w, gate_w, mine, other, grad_conv, totals, plain, shifted, part):
    start, end, core = scal[0], scal[1], scal[2]
    rows, taps_n = value.shape[0], taps.shape[0]
    half = (taps_n - 1) // 2
    live_count = scal[3].astype(F32)
    both = sums[0]
    for peer in range(1, sums.shape[0]):
        both = both + sums[peer]
    totals[...] = both
    shift_sum, gain_sum = both[0:1], both[1:2]
    live = live_rows(start - EDGE, scaled.shape[0], end)
    through = live * (inv[...] * gain[...]) * (
        grad[...] - (shift_sum + scaled[...] * gain_sum) / live_count
    )
    rounded = through.astype(BF16)
    grad_conv[...] = rounded[EDGE : EDGE + rows]
    spread(plain, shifted, rounded.astype(F32))
    grad_glu = convolve(taps, shifted, [EDGE + half - tap for tap in range(taps_n)], rows, 16)
    grad_glu = (grad_glu * live_rows(start, rows, end)).astype(BF16).astype(F32)
    sig = gate[...]
    to_value = (grad_glu * sig).astype(BF16)
    to_gate = (grad_glu * value[...] * sig * (1.0 - sig)).astype(BF16)
    product = jnp.dot(to_value, value_w[...], preferred_element_type=F32) + jnp.dot(
        to_gate, gate_w[...], preferred_element_type=F32
    )
    step, last_step = pl.program_id(0), pl.num_programs(0) - 1

    @pl.when(step == 0)
    def _():
        part[...] = product

    @pl.when(step > 0)
    def _():
        part[...] += product

    @pl.when(step == last_step)
    def _():
        count = mine.shape[0]
        mine[...] = part[pl.ds(pl.multiple_of(core * count, count), count), :]
        other[...] = part[pl.ds(pl.multiple_of((1 - core) * count, count), count), :]


def backward(scal, sums, scaled, grad, inv, gain, taps, value, gate, weight):
    span, half_width = scaled.shape
    rows, width = value.shape[0], weight.shape[1]
    chunk = 256 if half_width % 256 == 0 else 128
    steps = half_width // chunk
    taps_n = taps.shape[0]
    col = lambda n: pl.BlockSpec((n, chunk), lambda i: (0, i))
    own = pl.BlockSpec((rows // 2, width), lambda i: (0, 0))
    return pl.pallas_call(
        backward_kernel,
        grid=(steps,),
        in_specs=[
            pl.BlockSpec(memory_space=pltpu.SMEM),
            pl.BlockSpec((sums.shape[0], 2, chunk), lambda i: (0, 0, i)),
            col(span),
            col(span),
            col(1),
            col(1),
            pl.BlockSpec((taps_n, 8, chunk), lambda i: (0, 0, i)),
            col(rows),
            col(rows),
            pl.BlockSpec((chunk, width), lambda i: (i, 0)),
            pl.BlockSpec((chunk, width), lambda i: (i + steps, 0)),
        ],
        out_specs=[own, own, col(rows), col(2)],
        out_shape=[
            jax.ShapeDtypeStruct((rows // 2, width), F32),
            jax.ShapeDtypeStruct((rows // 2, width), F32),
            jax.ShapeDtypeStruct((rows, half_width), BF16),
            jax.ShapeDtypeStruct((2, half_width), F32),
        ],
        scratch_shapes=[
            pltpu.VMEM((span, chunk), F32),
            pltpu.VMEM((8, span // 8 - 1, 8, chunk), F32),
            pltpu.VMEM((rows, width), F32),
        ],
        compiler_params=params(),
        cost_estimate=cost(2 * rows * width * 2 * half_width, 4 * half_width * width + 20 * span * half_width),
        name="grad_conv_project_back",
    )(scal, sums, scaled, grad, inv, gain, taps, value, gate, weight, weight)


def shifted_scratch(span):
    return [pltpu.VMEM((span, 128), F32), pltpu.VMEM((8, span // 8 - 1, 8, 128), F32)]


def tap_grad_kernel(taps_n, grad_conv, glu, out, plain, shifted):
    spread(plain, shifted, glu[...].astype(F32))
    first = HALO - (taps_n - 1) // 2
    out[...] = correlate(taps_n, grad_conv[...].astype(F32), shifted, first)


def tap_grad(taps_n, grad_conv, glu):
    rows, half_width = grad_conv.shape
    span = glu.shape[0]
    col = lambda n: pl.BlockSpec((n, 128), lambda i: (0, i))
    return pl.pallas_call(
        functools.partial(tap_grad_kernel, taps_n),
        grid=(half_width // 128,),
        in_specs=[col(rows), col(span)],
        out_specs=col(taps_n),
        out_shape=jax.ShapeDtypeStruct((taps_n, half_width), F32),
        scratch_shapes=shifted_scratch(span),
        compiler_params=params(),
        cost_estimate=cost(2 * taps_n * rows * half_width, 4 * span * half_width),
        name="tap_grad",
    )(grad_conv, glu)


def raw_taps_kernel(taps_n, scal, conv, glu, stats, alone, crossed, plain, shifted):
    start, end = scal[0], scal[1]
    rows, span = conv.shape[0] - 2 * EDGE, glu.shape[0]
    spread(plain, shifted, glu[...].astype(F32))
    first = HALO - (taps_n - 1) // 2
    live = live_rows(start, rows, end)
    local = stats[0, 0:1, :] / jnp.maximum(jnp.sum(live), 1.0)
    crossed[...] = correlate(taps_n, live * (conv[EDGE : EDGE + rows, :] - local), shifted, first)
    tap = lax.broadcasted_iota(jnp.int32, (taps_n, span), 0)
    at = lax.broadcasted_iota(jnp.int32, (taps_n, span), 1) - first - tap
    inside = (at >= 0) & (at < jnp.clip(end - start, 0, rows))
    alone[...] = jnp.dot(
        jnp.where(inside, 1.0, 0.0).astype(BF16), glu[...], preferred_element_type=F32
    )


def raw_taps(taps_n, scal, conv, glu, stats):
    rows, half_width = conv.shape
    span = glu.shape[0]
    col = lambda n: pl.BlockSpec((n, 128), lambda i: (0, i))
    return pl.pallas_call(
        functools.partial(raw_taps_kernel, taps_n),
        grid=(half_width // 128,),
        in_specs=[
            pl.BlockSpec(memory_space=pltpu.SMEM),
            col(rows),
            col(span),
            pl.BlockSpec((1, 2, 128), lambda i: (0, 0, i)),
        ],
        out_specs=[col(taps_n), col(taps_n)],
        out_shape=[jax.ShapeDtypeStruct((taps_n, half_width), F32)] * 2,
        scratch_shapes=shifted_scratch(span),
        compiler_params=params(),
        cost_estimate=cost(2 * taps_n * rows * half_width, 8 * span * half_width),
        name="raw_taps",
    )(scal, conv, glu, stats)


def halves(array):
    high = array.astype(BF16).astype(F32)
    return high, array - high


def last_kernel(taps_n, scal, counts, stats, conv, cot, gain, shift, glu, alone, crossed, local_stats, taps_before, out, factor_out, plain, shifted, pay):
    step = pl.program_id(0)
    scaled, grad, live, mean, inv = swish_grads(scal, counts, stats, conv, cot, gain, shift)
    rows = conv.shape[0] - 2 * EDGE
    spread(plain, shifted, glu[...].astype(F32))
    first = HALO - (taps_n - 1) // 2
    factor = inv * gain[...]
    factor_out[...] = factor
    own = grad[EDGE : EDGE + rows]
    direct = taps_before[...] + factor * correlate(taps_n, own, shifted, first)
    own_live = live[EDGE : EDGE + rows]
    local = local_stats[0, 0:1, :] / jnp.maximum(jnp.sum(own_live), 1.0)
    with_scaled = inv * (crossed[...] + (local - mean) * alone[...])
    sums = jnp.concatenate(
        [
            jnp.sum(own, axis=0, keepdims=True),
            jnp.sum(own * scaled[EDGE : EDGE + rows], axis=0, keepdims=True),
        ],
        axis=0,
    )
    pay[step] = jnp.concatenate([*halves(direct), with_scaled, alone[...], *halves(sums)], axis=0)

    @pl.when(step == pl.num_programs(0) - 1)
    def _():
        turned = jnp.concatenate([jnp.transpose(pay[s]) for s in range(pay.shape[0])], axis=0)
        block = out.shape[1]
        for index in range(out.shape[0]):
            out[index] = turned[index * block : (index + 1) * block].astype(BF16)


def last(taps_n, peers, scal, counts, stats, conv, cot, gain, shift, glu, alone, crossed, local_stats, taps_before):
    span, half_width = conv.shape
    chunk = 128
    steps = half_width // chunk
    pay = 4 * taps_n + 4
    col = lambda n: pl.BlockSpec((n, chunk), lambda i: (0, i))
    smem = pl.BlockSpec(memory_space=pltpu.SMEM)
    return pl.pallas_call(
        functools.partial(last_kernel, taps_n),
        grid=(steps,),
        in_specs=[
            smem,
            smem,
            pl.BlockSpec((stats.shape[0], 2, chunk), lambda i: (0, 0, i)),
            col(span),
            col(span),
            col(1),
            col(1),
            col(glu.shape[0]),
            col(taps_n),
            col(taps_n),
            pl.BlockSpec((1, 2, chunk), lambda i: (0, 0, i)),
            col(taps_n),
        ],
        out_specs=[pl.BlockSpec((peers, half_width // peers, pay), lambda i: (0, 0, 0)), col(1)],
        out_shape=[
            jax.ShapeDtypeStruct((peers, half_width // peers, pay), BF16),
            jax.ShapeDtypeStruct((1, half_width), F32),
        ],
        scratch_shapes=[*shifted_scratch(glu.shape[0]), pltpu.VMEM((steps, pay, chunk), F32)],
        compiler_params=params(),
        cost_estimate=cost(100 * span * half_width, 10 * span * half_width),
        name="batch_norm_swish_taps",
    )(scal, counts, stats, conv, cot, gain, shift, glu, alone, crossed, local_stats, taps_before)


def finish_kernel(taps_n, scal, received, known, taps_out, norm_out):
    total = received[0].astype(F32)
    for index in range(1, received.shape[0]):
        total = total + received[index].astype(F32)
    total = jnp.transpose(total)
    n = taps_n
    sums = total[4 * n : 4 * n + 2] + total[4 * n + 2 : 4 * n + 4]
    shift_sum, gain_sum = sums[0:1], sums[1:2]
    factor = known[0:1] / scal[3].astype(F32)
    taps_out[...] = (total[:n] + total[n : 2 * n]) - factor * (
        gain_sum * total[2 * n : 3 * n] + shift_sum * total[3 * n : 4 * n]
    )
    norm_out[...] = jnp.concatenate([gain_sum + known[2:3], shift_sum + known[1:2]], axis=0)


def finish(taps_n, scal, received, known):
    width = received.shape[1]
    vmem = pl.BlockSpec(memory_space=pltpu.VMEM)
    return pl.pallas_call(
        functools.partial(finish_kernel, taps_n),
        in_specs=[pl.BlockSpec(memory_space=pltpu.SMEM), vmem, vmem],
        out_shape=[
            jax.ShapeDtypeStruct((taps_n, width), F32),
            jax.ShapeDtypeStruct((2, width), F32),
        ],
        compiler_params=params(),
        name="finish",
    )(scal, received, known)


def direction_kernel(scal, mine, other, features, noise, out, edge, squares):
    rows = mine.shape[0]
    first = scal[0] + scal[2] * rows
    block = 32
    total = jnp.zeros((1, 128), F32)
    for row in range(0, rows, block):
        at = slice(row, row + block)
        live = live_rows(first + row, block, scal[1])
        summed = features[at].astype(F32) + noise_scale * noise[at].astype(F32) * live
        normed, inverse = normalize(summed)
        grad = mine[at] + other[at]
        moved = (
            live
            * inverse
            * (
                grad
                - jnp.mean(grad, axis=-1, keepdims=True)
                - normed * jnp.mean(grad * normed, axis=-1, keepdims=True)
            )
        )
        out[0, at] = moved
        out[1, at] = summed
        total = total + jnp.sum(moved * moved)
    edge[...] = jnp.where(scal[2] == 0, out[:, :HALO], out[:, rows - HALO :])
    for peer in range(squares.shape[0]):
        squares[peer] = total


def direction(scal, mine, other, features, noise, peers):
    rows, width = mine.shape
    vmem = pl.BlockSpec(memory_space=pltpu.VMEM)
    return pl.pallas_call(
        direction_kernel,
        in_specs=[pl.BlockSpec(memory_space=pltpu.SMEM)] + [vmem] * 4,
        out_shape=[
            jax.ShapeDtypeStruct((2, rows, width), F32),
            jax.ShapeDtypeStruct((2, HALO, width), F32),
            jax.ShapeDtypeStruct((peers, 1, 128), F32),
        ],
        compiler_params=params(),
        cost_estimate=cost(30 * rows * width, 16 * rows * width),
        name="direction",
    )(scal, mine, other, features, noise)


def ascend_kernel(scal, squares, mine, partner, near, far, noise, perturbation, normed_out):
    start, end, core = scal[0], scal[1], scal[2]
    _, rows, width = mine.shape
    total = squares[0]
    for index in range(1, squares.shape[0]):
        total = total + squares[index]
    total = total[0:1, 0:1]
    length = jnp.full((1, 1), 1.0, F32) * end.astype(F32)
    rate = ascent_rate * jnp.sqrt(length * width) / (jnp.sqrt(total) + ascent_epsilon)
    block = 32
    is_first = core == 0

    def place_rows(row, one, two, at):
        moved = jnp.where(is_first, one[0, at], two[0, at])
        summed = jnp.where(is_first, one[1, at], two[1, at]) + moved * rate
        normed_out[row : row + block] = normalize(summed)[0].astype(BF16)

    place_rows(0, far, near, slice(0, HALO))
    for row in range(0, rows, block):
        at = slice(row, row + block)
        place_rows(HALO + row, mine, partner, at)
        place_rows(HALO + rows + row, partner, mine, at)
        live = live_rows(start + core * rows + row, block, end)
        perturbation[at] = noise_scale * noise[at].astype(F32) * live + mine[0, at] * rate
    place_rows(HALO + 2 * rows, near, far, slice(0, HALO))


def ascend(scal, squares, mine, partner, near, far, noise):
    _, rows, width = mine.shape
    vmem = pl.BlockSpec(memory_space=pltpu.VMEM)
    return pl.pallas_call(
        ascend_kernel,
        in_specs=[pl.BlockSpec(memory_space=pltpu.SMEM)] + [vmem] * 6,
        out_shape=[
            jax.ShapeDtypeStruct((rows, width), F32),
            jax.ShapeDtypeStruct((2 * (rows + HALO), width), BF16),
        ],
        compiler_params=params(),
        cost_estimate=cost(60 * rows * width, 30 * rows * width),
        name="ascend",
    )(scal, squares, mine, partner, near, far, noise)


def on_device(on_dp, features, start_noise, cotangent, in_weight, kernel, bn_gain, bn_shift, ends):
    rows, width = features.shape[1:]
    taps_n = kernel.shape[0]
    shards = lax.axis_size("tm")
    chips = shards // 2
    index = lax.axis_index("tm")
    group = lax.axis_index("dp")
    chip, core = index // 2, index % 2
    chip_rows = 2 * rows
    half_width = width // 2
    end = lax.dynamic_index_in_dim(ends, group, 0, keepdims=False)
    scal = jnp.stack([chip * chip_rows, end, core, jnp.sum(ends), chip % 4, chip // 4]).astype(jnp.int32)
    held = jnp.clip(
        ends[:, None] - chip_rows * jnp.arange(chips, dtype=jnp.int32)[None, :], 0, chip_rows
    ).reshape(-1).astype(F32)
    counts = jnp.stack([held, jnp.where(held > 0, 1.0 / jnp.maximum(held, 1.0), 0.0)])

    cores = [[2 * c + k for c in range(chips)] for k in range(2)]
    depth = chips // 4
    swap = [(i, i ^ 1) for i in range(shards)]
    swap_x = [(i, i ^ 2) for i in range(shards)]
    swap_y = [(i, i ^ 4) for i in range(shards)]
    near_pairs = [(2 * c, 2 * c - 2) for c in range(1, chips)] + [
        (2 * c + 1, 2 * c + 3) for c in range(chips - 1)
    ]
    far_pairs = [(2 * c, 2 * c - 1) for c in range(1, chips)] + [
        (2 * c + 1, 2 * c + 2) for c in range(chips - 1)
    ]
    first = core == 0

    def across(array, edge):
        return (
            lax.ppermute(array, "tm", swap),
            lax.ppermute(edge, "tm", near_pairs),
            lax.ppermute(edge, "tm", far_pairs),
        )

    def peers_of(array):
        array = lax.all_to_all(array, "tm", 0, 0, axis_index_groups=cores, tiled=True)
        if on_dp:
            array = lax.all_gather(array, "dp", axis=0, tiled=True)
        return array

    slice_width = width // shards
    pair = in_weight.reshape(2, slice_width, width)
    kept = lax.dynamic_index_in_dim(pair, core, 0, keepdims=False)
    given = lax.ppermute(lax.dynamic_index_in_dim(pair, 1 - core, 0, keepdims=False), "tm", swap)
    block = jnp.concatenate([jnp.where(first, kept, given), jnp.where(first, given, kept)], axis=0)
    shifts = [(0,)] + [(k, depth - k) if 2 * k < depth else (k,) for k in range(1, depth // 2 + 1)]
    forth = [(i, (i + 8) % shards) for i in range(shards)]
    back = [(i, (i - 8) % shards) for i in range(shards)]
    corner = [(i, i ^ (4 if i % 2 else 2)) for i in range(shards)]
    def mine_of(array):
        parts = array.reshape(array.shape[0], chips, 2, slice_width)
        return lax.dynamic_index_in_dim(parts, core, 2, keepdims=False).reshape(-1, half_width)

    def prepare_first(after):
        ours, noise, _ = lax.optimization_barrier((features[0], start_noise[0], after))
        own_ids = chip * chip_rows + core * rows + jnp.arange(rows, dtype=jnp.int32)
        own_live = (own_ids < end).astype(F32)[:, None]
        summed = ours.astype(F32) + noise_scale * noise.astype(F32) * own_live
        return [normalize(summed)[0].astype(BF16)]

    def prepare_second(after):
        own_taps, own_gain, own_shift, _ = lax.optimization_barrier((kernel, bn_gain, bn_shift, after))
        channel = mine_of(jnp.concatenate([own_taps, own_gain[None], own_shift[None]], axis=0))
        taps = jnp.broadcast_to(channel[:taps_n, None], (taps_n, 8, half_width))
        return [taps, channel[taps_n : taps_n + 1], channel[taps_n + 1 :], counts, scal]

    def assemble(own, partner, near, far):
        return jnp.concatenate(
            [
                jnp.where(first, far, near),
                jnp.where(first, own, partner),
                jnp.where(first, partner, own),
                jnp.where(first, near, far),
            ],
            axis=0,
        )

    along = {0: block, depth: block}
    kinds, pieces = [], []
    cot_own = cotangent[0]
    final = len(shifts) - 1
    for number, group in enumerate(shifts):
        blocks = jnp.concatenate([along[k] for k in group], axis=0)
        kinds.append((group, 0))
        pieces.append(blocks)
        sent = [lax.ppermute(blocks, "tm", swap_x), lax.ppermute(blocks, "tm", swap_y)]
        sent_kinds = [(group, 1), (group, 2)]
        if number:
            sent.append(lax.ppermute(relayed, "tm", corner))
            sent_kinds.append((shifts[number - 1], 3))
        onward = shifts[number + 1] if number < final else ()
        for k in onward:
            from_before = 2 * k <= depth
            sent.append(lax.ppermute(along[k - 1 if from_before else k + 1], "tm", forth if from_before else back))
        beside = []
        if number == 0:
            beside = prepare_first(sent[0])
        elif number == 1:
            both, *_ = lax.optimization_barrier((jnp.stack([normed_own, cot_own]), *sent[2:]))
            edge = jnp.concatenate(
                [
                    jnp.where(first, both[0, :HALO], both[0, rows - HALO :]),
                    jnp.where(first, both[1, :EDGE], both[1, rows - EDGE :]),
                ],
                axis=0,
            )
            beside = [*across(both, edge), *prepare_second(sent[-1])]
        if number == final:
            (partner, near, far), ready = (beside or crossing)[:3], beside[3:]
            beside = [
                assemble(normed_own, partner[0], near[:HALO], far[:HALO]),
                assemble(cot_own, partner[1], near[HALO:], far[HALO:]),
                place(scal, kinds, pieces, block.shape[0], chips),
                *ready,
            ]
        sent, beside = lax.optimization_barrier((sent, beside))
        relayed = jnp.where(first, sent[1], sent[0])
        if number == 0:
            (normed_own,) = beside
        elif number == 1:
            crossing, (taps, gain, shift, counts, scal) = beside[:3], beside[3:8]
        if number == final:
            normed_b, wide_cot, weight = beside[:3]
            late_kinds, late_pieces = sent_kinds, sent
        else:
            kinds += sent_kinds
            pieces += sent[: len(sent_kinds)]
            for k, arrived in zip(onward, sent[len(sent_kinds) :]):
                along[k] = arrived
    late_kinds.append((shifts[final], 3))
    late_pieces.append(lax.ppermute(relayed, "tm", corner))
    weight = place_late(scal, late_kinds, late_pieces, block.shape[0], weight)

    value, gate, glu, conv, stats = forward(
        scal, normed_b, weight, taps, chip_rows, chips, True
    )
    place_of = jnp.arange(half_width, dtype=jnp.int32)
    source = (2 * (place_of // slice_width) + core) * slice_width + place_of % slice_width
    chosen = (jnp.arange(width, dtype=jnp.int32)[:, None] == source[None, :]).astype(BF16)
    cot = jnp.dot(wide_cot, chosen, preferred_element_type=F32).astype(BF16)
    gathered = peers_of(stats)
    scaled, grad, inv, sums = batch(scal, counts, gathered, conv, cot, gain, shift, chips)
    mine, other, grad_conv, totals = backward(
        scal, peers_of(sums), scaled, grad, inv, gain, taps, value, gate, weight
    )
    other = lax.ppermute(other, "tm", swap)
    moved, edge, squares = direction(scal, mine, other, features[0], start_noise[0], shards)
    squares = lax.all_to_all(squares, "tm", 0, 0, tiled=True)
    partner, near, far = across(moved, edge)
    taps_before = tap_grad(taps_n, grad_conv, glu)
    squares, taps_before = lax.optimization_barrier((squares, taps_before))
    perturbation, normed_b = ascend(scal, squares, moved, partner, near, far, start_noise[0])

    glu, conv, stats = forward(scal, normed_b, weight, taps, chip_rows, chips, False)
    alone, crossed = raw_taps(taps_n, scal, conv, glu, stats)
    outgoing, factor = last(
        taps_n, chips, scal, counts, peers_of(stats), conv, cot, gain, shift, glu, alone, crossed, stats, taps_before
    )
    received = peers_of(outgoing)
    known = jnp.concatenate([factor, totals], axis=0)
    known = lax.dynamic_slice_in_dim(known, chip * slice_width, slice_width, 1)
    kernel_total, norm_total = finish(taps_n, scal, received, known)
    return (perturbation[None], kernel_total, norm_total)


def solution(mesh):
    return jax.shard_map(
        functools.partial(on_device, mesh.shape["dp"] > 1),
        mesh=mesh,
        in_specs=(
            P("dp", "tm", None),
            P("dp", "tm", None),
            P("dp", "tm", None),
            P("tm", None),
            P(),
            P(),
            P(),
            P(),
        ),
        out_specs=(P("dp", "tm", None), P(None, "tm"), P(None, "tm")),
        check_vma=False,
    )
```

```python
import functools

import jax
import jax.numpy as jnp
from jax import lax
from jax.experimental import pallas as pl
from jax.experimental.pallas import tpu as pltpu
from jax.sharding import PartitionSpec as P

ASCENT = 2

noise_scale = 0.5
ascent_rate = 0.5
layer_epsilon = 1e-05
batch_epsilon = 1e-05
ascent_epsilon = 1e-06

HALO = 32
EDGE = 16
F32 = jnp.float32
BF16 = jnp.bfloat16


def params(limit=56 * 1024 * 1024):
    return pltpu.CompilerParams(vmem_limit_bytes=limit)


def cost(flops, nbytes):
    return pl.CostEstimate(flops=int(flops), bytes_accessed=int(nbytes), transcendentals=0)


def normalize(summed):
    centre = summed - jnp.mean(summed, axis=-1, keepdims=True)
    inverse = lax.rsqrt(jnp.mean(centre * centre, axis=-1, keepdims=True) + layer_epsilon)
    return (centre * inverse, inverse)


def live_rows(first, rows, end):
    ids = first + lax.broadcasted_iota(jnp.int32, (rows, 1), 0)
    return jnp.where((ids >= 0) & (ids < end), 1.0, 0.0).astype(F32)


def spread(plain, shifted, array):
    plain[...] = array
    rows, tiles = shifted.shape[1] * 8, shifted.shape[1]
    for s in range(8):
        shifted[s] = plain[s : s + rows].reshape(tiles, 8, -1)


def tiles_at(shifted, row, tiles, lanes):
    first = (row - row % 8) // 8
    return shifted[row % 8, first : first + tiles, :, lanes]


def convolve(taps, shifted, offsets, rows, most):
    most = max(n for n in range(1, most + 1) if rows // 8 % n == 0)
    columns = []
    for lane in range(0, taps.shape[2], 128):
        lanes = slice(lane, lane + 128)
        parts = []
        for tile in range(0, rows // 8, most):
            total = jnp.zeros((most, 8, 128), F32)
            for tap, offset in enumerate(offsets):
                total = total + taps[tap, :, lanes][None] * tiles_at(
                    shifted, offset + 8 * tile, most, lanes
                )
            parts.append(total.reshape(most * 8, 128))
        columns.append(jnp.concatenate(parts, axis=0))
    return jnp.concatenate(columns, axis=1)


def correlate(taps_n, left, shifted, first):
    rows = left.shape[0]
    lanes = slice(0, 128)
    most = 32
    totals = [None] * taps_n
    for tile in range(0, rows // 8, most):
        part = left[8 * tile : 8 * (tile + most)].reshape(most, 8, 128)
        for tap in range(taps_n):
            product = jnp.sum(
                part * tiles_at(shifted, first + tap + 8 * tile, most, lanes), axis=0, keepdims=True
            )
            totals[tap] = product if totals[tap] is None else totals[tap] + product
    return jnp.sum(jnp.concatenate(totals, axis=0), axis=1)


def place_kernel(shifts, size, scal, *refs):
    pieces, out = refs[:-1], refs[-1]
    spot, layer = scal[4], scal[5]
    depth = out.shape[0] // (4 * size)

    for number, group in enumerate(shifts):
        for other, ref in enumerate(pieces[4 * number : 4 * number + 4]):
            for nth, shift in enumerate(group):
                chip = lax.rem(layer - shift + depth, depth) * 4 + (spot ^ other)
                row = pl.multiple_of(chip * size, 16)
                out[pl.ds(row, size), :] = ref[nth * size : (nth + 1) * size, :]


def place(scal, pieces, shifts, size):
    width = pieces[0].shape[1]
    chips = 4 * sum(len(group) for group in shifts)
    vmem = pl.BlockSpec(memory_space=pltpu.VMEM)
    return pl.pallas_call(
        functools.partial(place_kernel, shifts, size),
        in_specs=[pl.BlockSpec(memory_space=pltpu.SMEM)] + [vmem] * len(pieces),
        out_specs=vmem,
        out_shape=jax.ShapeDtypeStruct((chips * size, width), BF16),
        compiler_params=params(),
        cost_estimate=cost(0, 4 * chips * size * width),
        name="place_weights",
    )(scal, *pieces)


def forward_kernel(keep, scal, nb, value_w, gate_w, taps, *refs):
    kept, (glu, conv, stats, plain, shifted) = refs[: 2 * keep], refs[2 * keep :]
    start, end = scal[0], scal[1]
    span, taps_n = nb.shape[0], taps.shape[0]
    rows = conv.shape[0] - 2 * EDGE
    contract = (((1,), (1,)), ((), ()))
    v = lax.dot_general(nb[...], value_w[...], contract, preferred_element_type=F32)
    s = jax.nn.sigmoid(lax.dot_general(nb[...], gate_w[...], contract, preferred_element_type=F32))
    if keep:
        kept[0][...] = v[HALO : HALO + rows]
        kept[1][...] = s[HALO : HALO + rows]
    gated = (v * s * live_rows(start - HALO, span, end)).astype(BF16)
    glu[...] = gated
    spread(plain, shifted, gated.astype(F32))
    shift = HALO - EDGE - (taps_n - 1) // 2
    conv[...] = convolve(taps, shifted, [shift + tap for tap in range(taps_n)], conv.shape[0], 12)
    live = live_rows(start, rows, end)
    own = conv[EDGE : EDGE + rows, :]
    mass = jnp.sum(live * own, axis=0, keepdims=True)
    centre = live * (own - mass / jnp.maximum(jnp.sum(live), 1.0))
    both = jnp.concatenate([mass, jnp.sum(centre * centre, axis=0, keepdims=True)], axis=0)
    for peer in range(stats.shape[0]):
        stats[peer] = both


def forward(scal, nb, weight, taps, rows, peers, keep):
    span, width = nb.shape
    taps_n, _, half_width = taps.shape
    chunk = 256 if half_width % 256 == 0 else 128
    steps = half_width // chunk
    col = lambda n: pl.BlockSpec((n, chunk), lambda i: (0, i))
    return pl.pallas_call(
        functools.partial(forward_kernel, keep),
        grid=(steps,),
        in_specs=[
            pl.BlockSpec(memory_space=pltpu.SMEM),
            pl.BlockSpec((span, width), lambda i: (0, 0)),
            pl.BlockSpec((chunk, width), lambda i: (i, 0)),
            pl.BlockSpec((chunk, width), lambda i: (i + steps, 0)),
            pl.BlockSpec((taps_n, 8, chunk), lambda i: (0, 0, i)),
        ],
        out_specs=[
            *([col(rows)] * (2 * keep)),
            col(span),
            col(rows + 2 * EDGE),
            pl.BlockSpec((peers, 2, chunk), lambda i: (0, 0, i)),
        ],
        out_shape=[
            *([jax.ShapeDtypeStruct((rows, half_width), F32)] * (2 * keep)),
            jax.ShapeDtypeStruct((span, half_width), BF16),
            jax.ShapeDtypeStruct((rows + 2 * EDGE, half_width), F32),
            jax.ShapeDtypeStruct((peers, 2, half_width), F32),
        ],
        scratch_shapes=[
            pltpu.VMEM((span, chunk), F32),
            pltpu.VMEM((8, span // 8 - 1, 8, chunk), F32),
        ],
        compiler_params=params(),
        cost_estimate=cost(2 * span * width * 2 * half_width, 4 * half_width * width + 10 * span * half_width),
        name="project_glu_conv",
    )(scal, nb, weight, weight, taps)


def moments(counts, stats, live_count):
    mass = stats[0, 0:1, :]
    square = stats[0, 1:2, :]
    for peer in range(1, stats.shape[0]):
        mass = mass + stats[peer, 0:1, :]
        square = square + stats[peer, 1:2, :]
    mean = mass / live_count
    for peer in range(stats.shape[0]):
        off = stats[peer, 0:1, :] - counts[0, peer] * mean
        square = square + off * off * counts[1, peer]
    return mean, lax.rsqrt(square / live_count + batch_epsilon)


def swish_grads(scal, counts, stats, conv, cot, gain, shift):
    start, end = scal[0], scal[1]
    live_count = scal[3].astype(F32)
    mean, inv = moments(counts, stats, live_count)
    scaled = (conv[...] - mean) * inv
    pre = gain[...] * scaled + shift[...]
    sig = jax.nn.sigmoid(pre)
    live = live_rows(start - EDGE, conv.shape[0], end)
    upstream = live * cot[...].astype(F32) / ASCENT
    return scaled, upstream * sig * (1.0 + pre * (1.0 - sig)), live, mean, inv


def batch_kernel(scal, counts, stats, conv, cot, gain, shift, scaled_out, grad_out, inv_out, sums):
    scaled, grad, live, mean, inv = swish_grads(scal, counts, stats, conv, cot, gain, shift)
    scaled_out[...] = scaled
    grad_out[...] = grad
    inv_out[...] = inv
    rows = conv.shape[0] - 2 * EDGE
    own = grad[EDGE : EDGE + rows]
    both = jnp.concatenate(
        [
            jnp.sum(own, axis=0, keepdims=True),
            jnp.sum(own * scaled[EDGE : EDGE + rows], axis=0, keepdims=True),
        ],
        axis=0,
    )
    for peer in range(sums.shape[0]):
        sums[peer] = both


def batch(scal, counts, stats, conv, cot, gain, shift, peers):
    span, half_width = conv.shape
    chunk = 256 if half_width % 256 == 0 else 128
    col = lambda n: pl.BlockSpec((n, chunk), lambda i: (0, i))
    smem = pl.BlockSpec(memory_space=pltpu.SMEM)
    return pl.pallas_call(
        batch_kernel,
        grid=(half_width // chunk,),
        in_specs=[
            smem,
            smem,
            pl.BlockSpec((stats.shape[0], 2, chunk), lambda i: (0, 0, i)),
            col(span),
            col(span),
            col(1),
            col(1),
        ],
        out_specs=[col(span), col(span), col(1), pl.BlockSpec((peers, 2, chunk), lambda i: (0, 0, i))],
        out_shape=[
            jax.ShapeDtypeStruct((span, half_width), F32),
            jax.ShapeDtypeStruct((span, half_width), F32),
            jax.ShapeDtypeStruct((1, half_width), F32),
            jax.ShapeDtypeStruct((peers, 2, half_width), F32),
        ],
        compiler_params=params(),
        cost_estimate=cost(40 * span * half_width, 16 * span * half_width),
        name="batch_norm_swish",
    )(scal, counts, stats, conv, cot, gain, shift)


def backward_kernel(scal, sums, scaled, grad, inv, gain, taps, value, gate, value_w, gate_w, mine, other, grad_conv, totals, plain, shifted, part):
    start, end, core = scal[0], scal[1], scal[2]
    rows, taps_n = value.shape[0], taps.shape[0]
    half = (taps_n - 1) // 2
    live_count = scal[3].astype(F32)
    both = sums[0]
    for peer in range(1, sums.shape[0]):
        both = both + sums[peer]
    totals[...] = both
    shift_sum, gain_sum = both[0:1], both[1:2]
    live = live_rows(start - EDGE, scaled.shape[0], end)
    through = live * (inv[...] * gain[...]) * (
        grad[...] - (shift_sum + scaled[...] * gain_sum) / live_count
    )
    rounded = through.astype(BF16)
    grad_conv[...] = rounded[EDGE : EDGE + rows]
    spread(plain, shifted, rounded.astype(F32))
    grad_glu = convolve(taps, shifted, [EDGE + half - tap for tap in range(taps_n)], rows, 16)
    grad_glu = (grad_glu * live_rows(start, rows, end)).astype(BF16).astype(F32)
    sig = gate[...]
    to_value = (grad_glu * sig).astype(BF16)
    to_gate = (grad_glu * value[...] * sig * (1.0 - sig)).astype(BF16)
    product = jnp.dot(to_value, value_w[...], preferred_element_type=F32) + jnp.dot(
        to_gate, gate_w[...], preferred_element_type=F32
    )
    step, last_step = pl.program_id(0), pl.num_programs(0) - 1

    @pl.when(step == 0)
    def _():
        part[...] = product

    @pl.when(step > 0)
    def _():
        part[...] += product

    @pl.when(step == last_step)
    def _():
        count = mine.shape[0]
        mine[...] = part[pl.ds(pl.multiple_of(core * count, count), count), :]
        other[...] = part[pl.ds(pl.multiple_of((1 - core) * count, count), count), :]


def backward(scal, sums, scaled, grad, inv, gain, taps, value, gate, weight):
    span, half_width = scaled.shape
    rows, width = value.shape[0], weight.shape[1]
    chunk = 256 if half_width % 256 == 0 else 128
    steps = half_width // chunk
    taps_n = taps.shape[0]
    col = lambda n: pl.BlockSpec((n, chunk), lambda i: (0, i))
    own = pl.BlockSpec((rows // 2, width), lambda i: (0, 0))
    return pl.pallas_call(
        backward_kernel,
        grid=(steps,),
        in_specs=[
            pl.BlockSpec(memory_space=pltpu.SMEM),
            pl.BlockSpec((sums.shape[0], 2, chunk), lambda i: (0, 0, i)),
            col(span),
            col(span),
            col(1),
            col(1),
            pl.BlockSpec((taps_n, 8, chunk), lambda i: (0, 0, i)),
            col(rows),
            col(rows),
            pl.BlockSpec((chunk, width), lambda i: (i, 0)),
            pl.BlockSpec((chunk, width), lambda i: (i + steps, 0)),
        ],
        out_specs=[own, own, col(rows), col(2)],
        out_shape=[
            jax.ShapeDtypeStruct((rows // 2, width), F32),
            jax.ShapeDtypeStruct((rows // 2, width), F32),
            jax.ShapeDtypeStruct((rows, half_width), BF16),
            jax.ShapeDtypeStruct((2, half_width), F32),
        ],
        scratch_shapes=[
            pltpu.VMEM((span, chunk), F32),
            pltpu.VMEM((8, span // 8 - 1, 8, chunk), F32),
            pltpu.VMEM((rows, width), F32),
        ],
        compiler_params=params(),
        cost_estimate=cost(2 * rows * width * 2 * half_width, 4 * half_width * width + 20 * span * half_width),
        name="grad_conv_project_back",
    )(scal, sums, scaled, grad, inv, gain, taps, value, gate, weight, weight)


def shifted_scratch(span):
    return [pltpu.VMEM((span, 128), F32), pltpu.VMEM((8, span // 8 - 1, 8, 128), F32)]


def tap_grad_kernel(taps_n, grad_conv, glu, out, plain, shifted):
    spread(plain, shifted, glu[...].astype(F32))
    first = HALO - (taps_n - 1) // 2
    out[...] = correlate(taps_n, grad_conv[...].astype(F32), shifted, first)


def tap_grad(taps_n, grad_conv, glu):
    rows, half_width = grad_conv.shape
    span = glu.shape[0]
    col = lambda n: pl.BlockSpec((n, 128), lambda i: (0, i))
    return pl.pallas_call(
        functools.partial(tap_grad_kernel, taps_n),
        grid=(half_width // 128,),
        in_specs=[col(rows), col(span)],
        out_specs=col(taps_n),
        out_shape=jax.ShapeDtypeStruct((taps_n, half_width), F32),
        scratch_shapes=shifted_scratch(span),
        compiler_params=params(),
        cost_estimate=cost(2 * taps_n * rows * half_width, 4 * span * half_width),
        name="tap_grad",
    )(grad_conv, glu)


def raw_taps_kernel(taps_n, scal, conv, glu, stats, alone, crossed, plain, shifted):
    start, end = scal[0], scal[1]
    rows, span = conv.shape[0] - 2 * EDGE, glu.shape[0]
    spread(plain, shifted, glu[...].astype(F32))
    first = HALO - (taps_n - 1) // 2
    live = live_rows(start, rows, end)
    local = stats[0, 0:1, :] / jnp.maximum(jnp.sum(live), 1.0)
    crossed[...] = correlate(taps_n, live * (conv[EDGE : EDGE + rows, :] - local), shifted, first)
    tap = lax.broadcasted_iota(jnp.int32, (taps_n, span), 0)
    at = lax.broadcasted_iota(jnp.int32, (taps_n, span), 1) - first - tap
    inside = (at >= 0) & (at < jnp.clip(end - start, 0, rows))
    alone[...] = jnp.dot(
        jnp.where(inside, 1.0, 0.0).astype(BF16), glu[...], preferred_element_type=F32
    )


def raw_taps(taps_n, scal, conv, glu, stats):
    rows, half_width = conv.shape
    span = glu.shape[0]
    col = lambda n: pl.BlockSpec((n, 128), lambda i: (0, i))
    return pl.pallas_call(
        functools.partial(raw_taps_kernel, taps_n),
        grid=(half_width // 128,),
        in_specs=[
            pl.BlockSpec(memory_space=pltpu.SMEM),
            col(rows),
            col(span),
            pl.BlockSpec((1, 2, 128), lambda i: (0, 0, i)),
        ],
        out_specs=[col(taps_n), col(taps_n)],
        out_shape=[jax.ShapeDtypeStruct((taps_n, half_width), F32)] * 2,
        scratch_shapes=shifted_scratch(span),
        compiler_params=params(),
        cost_estimate=cost(2 * taps_n * rows * half_width, 8 * span * half_width),
        name="raw_taps",
    )(scal, conv, glu, stats)


def halves(array):
    high = array.astype(BF16).astype(F32)
    return high, array - high


def last_kernel(taps_n, scal, counts, stats, conv, cot, gain, shift, glu, alone, crossed, local_stats, taps_before, out, factor_out, plain, shifted, pay):
    step = pl.program_id(0)
    scaled, grad, live, mean, inv = swish_grads(scal, counts, stats, conv, cot, gain, shift)
    rows = conv.shape[0] - 2 * EDGE
    spread(plain, shifted, glu[...].astype(F32))
    first = HALO - (taps_n - 1) // 2
    factor = inv * gain[...]
    factor_out[...] = factor
    own = grad[EDGE : EDGE + rows]
    direct = taps_before[...] + factor * correlate(taps_n, own, shifted, first)
    own_live = live[EDGE : EDGE + rows]
    local = local_stats[0, 0:1, :] / jnp.maximum(jnp.sum(own_live), 1.0)
    with_scaled = inv * (crossed[...] + (local - mean) * alone[...])
    sums = jnp.concatenate(
        [
            jnp.sum(own, axis=0, keepdims=True),
            jnp.sum(own * scaled[EDGE : EDGE + rows], axis=0, keepdims=True),
        ],
        axis=0,
    )
    pay[step] = jnp.concatenate([*halves(direct), with_scaled, alone[...], *halves(sums)], axis=0)

    @pl.when(step == pl.num_programs(0) - 1)
    def _():
        turned = jnp.concatenate([jnp.transpose(pay[s]) for s in range(pay.shape[0])], axis=0)
        block = out.shape[1]
        for index in range(out.shape[0]):
            out[index] = turned[index * block : (index + 1) * block].astype(BF16)


def last(taps_n, peers, scal, counts, stats, conv, cot, gain, shift, glu, alone, crossed, local_stats, taps_before):
    span, half_width = conv.shape
    chunk = 128
    steps = half_width // chunk
    pay = 4 * taps_n + 4
    col = lambda n: pl.BlockSpec((n, chunk), lambda i: (0, i))
    smem = pl.BlockSpec(memory_space=pltpu.SMEM)
    return pl.pallas_call(
        functools.partial(last_kernel, taps_n),
        grid=(steps,),
        in_specs=[
            smem,
            smem,
            pl.BlockSpec((stats.shape[0], 2, chunk), lambda i: (0, 0, i)),
            col(span),
            col(span),
            col(1),
            col(1),
            col(glu.shape[0]),
            col(taps_n),
            col(taps_n),
            pl.BlockSpec((1, 2, chunk), lambda i: (0, 0, i)),
            col(taps_n),
        ],
        out_specs=[pl.BlockSpec((peers, half_width // peers, pay), lambda i: (0, 0, 0)), col(1)],
        out_shape=[
            jax.ShapeDtypeStruct((peers, half_width // peers, pay), BF16),
            jax.ShapeDtypeStruct((1, half_width), F32),
        ],
        scratch_shapes=[*shifted_scratch(glu.shape[0]), pltpu.VMEM((steps, pay, chunk), F32)],
        compiler_params=params(),
        cost_estimate=cost(100 * span * half_width, 10 * span * half_width),
        name="batch_norm_swish_taps",
    )(scal, counts, stats, conv, cot, gain, shift, glu, alone, crossed, local_stats, taps_before)


def finish_kernel(taps_n, scal, received, known, taps_out, norm_out):
    total = received[0].astype(F32)
    for index in range(1, received.shape[0]):
        total = total + received[index].astype(F32)
    total = jnp.transpose(total)
    n = taps_n
    sums = total[4 * n : 4 * n + 2] + total[4 * n + 2 : 4 * n + 4]
    shift_sum, gain_sum = sums[0:1], sums[1:2]
    factor = known[0:1] / scal[3].astype(F32)
    taps_out[...] = (total[:n] + total[n : 2 * n]) - factor * (
        gain_sum * total[2 * n : 3 * n] + shift_sum * total[3 * n : 4 * n]
    )
    norm_out[...] = jnp.concatenate([gain_sum + known[2:3], shift_sum + known[1:2]], axis=0)


def finish(taps_n, scal, received, known):
    width = received.shape[1]
    vmem = pl.BlockSpec(memory_space=pltpu.VMEM)
    return pl.pallas_call(
        functools.partial(finish_kernel, taps_n),
        in_specs=[pl.BlockSpec(memory_space=pltpu.SMEM), vmem, vmem],
        out_shape=[
            jax.ShapeDtypeStruct((taps_n, width), F32),
            jax.ShapeDtypeStruct((2, width), F32),
        ],
        compiler_params=params(),
        name="finish",
    )(scal, received, known)


def direction_kernel(scal, mine, other, features, noise, out, edge, squares):
    rows = mine.shape[0]
    first = scal[0] + scal[2] * rows
    block = 32
    total = jnp.zeros((1, 128), F32)
    for row in range(0, rows, block):
        at = slice(row, row + block)
        live = live_rows(first + row, block, scal[1])
        summed = features[at].astype(F32) + noise_scale * noise[at].astype(F32) * live
        normed, inverse = normalize(summed)
        grad = mine[at] + other[at]
        moved = (
            live
            * inverse
            * (
                grad
                - jnp.mean(grad, axis=-1, keepdims=True)
                - normed * jnp.mean(grad * normed, axis=-1, keepdims=True)
            )
        )
        out[at] = moved
        total = total + jnp.sum(moved * moved)
    edge[...] = jnp.where(scal[2] == 0, out[:HALO], out[rows - HALO :])
    for peer in range(squares.shape[0]):
        squares[peer] = total


def direction(scal, mine, other, features, noise, peers):
    rows, width = mine.shape
    vmem = pl.BlockSpec(memory_space=pltpu.VMEM)
    return pl.pallas_call(
        direction_kernel,
        in_specs=[pl.BlockSpec(memory_space=pltpu.SMEM)] + [vmem] * 4,
        out_shape=[
            jax.ShapeDtypeStruct((rows, width), F32),
            jax.ShapeDtypeStruct((HALO, width), F32),
            jax.ShapeDtypeStruct((peers, 1, 128), F32),
        ],
        compiler_params=params(),
        cost_estimate=cost(30 * rows * width, 16 * rows * width),
        name="direction",
    )(scal, mine, other, features, noise)


def ascend_kernel(scal, squares, features, noise, mine, partner, near, far, own_noise, perturbation, normed_out):
    start, end, core = scal[0], scal[1], scal[2]
    rows, width = mine.shape
    total = squares[0]
    for index in range(1, squares.shape[0]):
        total = total + squares[index]
    total = total[0:1, 0:1]
    length = jnp.full((1, 1), 1.0, F32) * end.astype(F32)
    rate = ascent_rate * jnp.sqrt(length * width) / (jnp.sqrt(total) + ascent_epsilon)
    block = 32
    is_first = core == 0

    def place(row, moved):
        at = slice(row, row + block)
        live = live_rows(start - HALO + row, block, end)
        summed = features[at].astype(F32) + (noise_scale * noise[at].astype(F32) * live + moved * rate)
        normed_out[at] = normalize(summed)[0].astype(BF16)

    place(0, jnp.where(is_first, far[...], near[...]))
    for row in range(0, rows, block):
        at = slice(row, row + block)
        place(HALO + row, jnp.where(is_first, mine[at], partner[at]))
        place(HALO + rows + row, jnp.where(is_first, partner[at], mine[at]))
        live = live_rows(start + core * rows + row, block, end)
        perturbation[at] = noise_scale * own_noise[at].astype(F32) * live + mine[at] * rate
    place(HALO + 2 * rows, jnp.where(is_first, near[...], far[...]))


def ascend(scal, squares, features, noise, mine, partner, near, far, own_noise):
    vmem = pl.BlockSpec(memory_space=pltpu.VMEM)
    return pl.pallas_call(
        ascend_kernel,
        in_specs=[pl.BlockSpec(memory_space=pltpu.SMEM)] + [vmem] * 8,
        out_shape=[
            jax.ShapeDtypeStruct(mine.shape, F32),
            jax.ShapeDtypeStruct(features.shape, BF16),
        ],
        compiler_params=params(),
        cost_estimate=cost(30 * features.size, 8 * features.size),
        name="ascend",
    )(scal, squares, features, noise, mine, partner, near, far, own_noise)


def on_device(on_dp, features, start_noise, cotangent, in_weight, kernel, bn_gain, bn_shift, ends):
    rows, width = features.shape[1:]
    taps_n = kernel.shape[0]
    shards = lax.axis_size("tm")
    chips = shards // 2
    index = lax.axis_index("tm")
    group = lax.axis_index("dp")
    chip, core = index // 2, index % 2
    chip_rows = 2 * rows
    half_width = width // 2
    end = lax.dynamic_index_in_dim(ends, group, 0, keepdims=False)
    scal = jnp.stack([chip * chip_rows, end, core, jnp.sum(ends), chip % 4, chip // 4]).astype(jnp.int32)
    held = jnp.clip(
        ends[:, None] - chip_rows * jnp.arange(chips, dtype=jnp.int32)[None, :], 0, chip_rows
    ).reshape(-1).astype(F32)
    counts = jnp.stack([held, jnp.where(held > 0, 1.0 / jnp.maximum(held, 1.0), 0.0)])

    cores = [[2 * c + k for c in range(chips)] for k in range(2)]
    depth = chips // 4
    swap = [(i, i ^ 1) for i in range(shards)]
    swap_x = [(i, i ^ 2) for i in range(shards)]
    swap_y = [(i, i ^ 4) for i in range(shards)]
    near_pairs = [(2 * c, 2 * c - 2) for c in range(1, chips)] + [
        (2 * c + 1, 2 * c + 3) for c in range(chips - 1)
    ]
    far_pairs = [(2 * c, 2 * c - 1) for c in range(1, chips)] + [
        (2 * c + 1, 2 * c + 2) for c in range(chips - 1)
    ]
    first = core == 0

    def across(array, edge):
        return (
            lax.ppermute(array, "tm", swap),
            lax.ppermute(edge, "tm", near_pairs),
            lax.ppermute(edge, "tm", far_pairs),
        )

    def peers_of(array):
        array = lax.all_to_all(array, "tm", 0, 0, axis_index_groups=cores, tiled=True)
        if on_dp:
            array = lax.all_gather(array, "dp", axis=0, tiled=True)
        return array

    slice_width = width // shards
    pair = in_weight.reshape(2, slice_width, width)
    kept = lax.dynamic_index_in_dim(pair, core, 0, keepdims=False)
    given = lax.ppermute(lax.dynamic_index_in_dim(pair, 1 - core, 0, keepdims=False), "tm", swap)
    block = jnp.concatenate([jnp.where(first, kept, given), jnp.where(first, given, kept)], axis=0)
    shifts = [(0,)] + [(k, depth - k) if 2 * k < depth else (k,) for k in range(1, depth // 2 + 1)]
    along = {0: block}
    for k in [k for group in shifts[1:] for k in group]:
        along[k] = lax.ppermute(block, "tm", [(i, (i + 8 * k) % shards) for i in range(shards)])
    corner = [(i, i ^ (4 if i % 2 else 2)) for i in range(shards)]
    pieces, relayed = [], None
    for number, group in enumerate(shifts):
        blocks = jnp.concatenate([along[k] for k in group], axis=0)
        if number == 1:
            blocks, relayed = lax.optimization_barrier((blocks, relayed))
        elif number > 1:
            blocks, _ = lax.optimization_barrier((blocks, pieces[4 * number - 5]))
        from_x = lax.ppermute(blocks, "tm", swap_x)
        from_y = lax.ppermute(blocks, "tm", swap_y)
        relayed = jnp.where(first, from_y, from_x)
        pieces += [blocks, from_x, from_y]
        if number + 1 < len(shifts):
            pieces.append(lax.ppermute(relayed, "tm", corner))
    features, start_noise, cotangent, kernel, bn_gain, bn_shift, _ = lax.optimization_barrier(
        (features, start_noise, cotangent, kernel, bn_gain, bn_shift, pieces[4])
    )
    packed = jnp.concatenate([features, start_noise, cotangent], axis=0)
    partner, near, far = across(
        packed, jnp.where(first, packed[:, :HALO], packed[:, rows - HALO :])
    )
    whole = jnp.concatenate(
        [
            jnp.where(first, far, near),
            jnp.where(first, packed, partner),
            jnp.where(first, partner, packed),
            jnp.where(first, near, far),
        ],
        axis=1,
    )
    wide_features, wide_noise, wide_cot = whole[0], whole[1], whole[2]

    place_of = jnp.arange(half_width, dtype=jnp.int32)
    source = (2 * (place_of // slice_width) + core) * slice_width + place_of % slice_width
    chosen = (jnp.arange(width, dtype=jnp.int32)[:, None] == source[None, :]).astype(BF16)
    cot = jnp.dot(wide_cot[HALO - EDGE : -(HALO - EDGE)], chosen, preferred_element_type=F32).astype(BF16)

    def mine_of(array):
        parts = array.reshape(array.shape[0], chips, 2, slice_width)
        return lax.dynamic_index_in_dim(parts, core, 2, keepdims=False).reshape(-1, half_width)

    channel = mine_of(jnp.concatenate([kernel, bn_gain[None], bn_shift[None]], axis=0))
    gain, shift = channel[taps_n : taps_n + 1], channel[taps_n + 1 :]
    taps = jnp.broadcast_to(channel[:taps_n, None], (taps_n, 8, half_width))

    frame_ids = chip * chip_rows - HALO + jnp.arange(whole.shape[1], dtype=jnp.int32)
    live = ((frame_ids >= 0) & (frame_ids < end)).astype(F32)
    summed = wide_features.astype(F32) + noise_scale * wide_noise.astype(F32) * live[:, None]
    normed_b = normalize(summed)[0].astype(BF16)

    relayed, normed_b, taps, gain, shift = lax.optimization_barrier(
        (relayed, normed_b, taps, gain, shift)
    )
    pieces.append(lax.ppermute(relayed, "tm", corner))
    weight = place(scal, pieces, shifts, block.shape[0])

    value, gate, glu, conv, stats = forward(
        scal, normed_b, weight, taps, chip_rows, chips, True
    )
    scaled, grad, inv, sums = batch(scal, counts, peers_of(stats), conv, cot, gain, shift, chips)
    mine, other, grad_conv, totals = backward(
        scal, peers_of(sums), scaled, grad, inv, gain, taps, value, gate, weight
    )
    other = lax.ppermute(other, "tm", swap)
    moved, edge, squares = direction(scal, mine, other, features[0], start_noise[0], shards)
    squares = lax.all_to_all(squares, "tm", 0, 0, tiled=True)
    partner, near, far = across(moved, edge)
    taps_before = tap_grad(taps_n, grad_conv, glu)
    squares, taps_before = lax.optimization_barrier((squares, taps_before))
    perturbation, normed_b = ascend(
        scal, squares, wide_features, wide_noise, moved, partner, near, far, start_noise[0]
    )

    glu, conv, stats = forward(scal, normed_b, weight, taps, chip_rows, chips, False)
    alone, crossed = raw_taps(taps_n, scal, conv, glu, stats)
    outgoing, factor = last(
        taps_n, chips, scal, counts, peers_of(stats), conv, cot, gain, shift, glu, alone, crossed, stats, taps_before
    )
    received = peers_of(outgoing)
    known = jnp.concatenate([factor, totals], axis=0)
    known = lax.dynamic_slice_in_dim(known, chip * slice_width, slice_width, 1)
    kernel_total, norm_total = finish(taps_n, scal, received, known)
    return (perturbation[None], kernel_total, norm_total)


def solution(mesh):
    return jax.shard_map(
        functools.partial(on_device, mesh.shape["dp"] > 1),
        mesh=mesh,
        in_specs=(
            P("dp", "tm", None),
            P("dp", "tm", None),
            P("dp", "tm", None),
            P("tm", None),
            P(),
            P(),
            P(),
            P(),
        ),
        out_specs=(P("dp", "tm", None), P(None, "tm"), P(None, "tm")),
        check_vma=False,
    )
```
